32 devices in a mesh: ctx: 8 (over y, x, core), tp: 4 (over z).
Axes of the slice: x: 2, y: 2, z: 4, core: 2. Of those that a mesh axis runs over, the one named last changes fastest.
Arguments:
- hyena_gate: bfloat16 [1024, 4096], P('ctx', 'tp'), may hold values from -6 to 6
- hyena_key: bfloat16 [1024, 4096], P('ctx', 'tp'), may hold values from -6 to 6
- hyena_value: bfloat16 [1024, 4096], P('ctx', 'tp'), may hold values from -6 to 6
- filter_taps: bfloat16 [1024, 4096], P(None, 'tp'), may hold values from -0.25 to 0.25
- skip_weight: float32 [4096], P('tp'), may hold values from -4 to 4
- queries: bfloat16 [1024, 4096], P('ctx', 'tp'), may hold values from -100 to 100
- attn_keys: bfloat16 [1024, 4096], P('ctx', 'tp'), may hold values from -4.5 to 4.5
- valid_length: int32 [1], replicated, may hold values from 513 to 1024
Outputs:
- hyena_out: bfloat16 [1024, 4096], P('ctx', 'tp')
- attn_out: bfloat16 [1024, 4096], P('ctx', 'tp')
The draws below stay inside these ranges and needn't reach their ends.
All inputs are finite; a program needn't handle non-finite values.
Results may differ from the reference program's by a relative error of at most 0.015.
Values may be sent and summed in bfloat16 or wider, within the bound.
A program may use at most 64 MiB of HBM per device.

```python
import math
import jax
import jax.numpy as jnp
from jax import lax

GROUP = 128
HEADS = 32
HD = 128
DW = 4096
SEQ = 1024


def key_rows(key):
    key_base = jnp.clip(jax.random.normal(jax.random.fold_in(key, 11), (SEQ, DW), jnp.float32), -4.5, 4.5)
    return key_base


def draw_attn_keys(key, part):
    key_base = key_rows(key)
    return key_base.astype(jnp.bfloat16)


def draw_queries(key, part):
    query_rows = jnp.clip(jax.random.normal(jax.random.fold_in(key, 12), (SEQ, DW), jnp.float32), -4.5, 4.5)
    return query_rows.astype(jnp.bfloat16)


def draw_filter_taps(key, part):
    channel = jnp.arange(DW, dtype=jnp.float32)
    spread = jnp.exp(jax.random.uniform(jax.random.fold_in(key, 21), (DW,), jnp.float32, math.log(0.25), math.log(2.5)))
    channel_ramp = jnp.sqrt(1.0 + 2.0 * channel / (DW - 1))
    taps_noise = jnp.clip(jax.random.normal(jax.random.fold_in(key, 22), (SEQ, DW), jnp.float32), -4.0, 4.0)
    filter_values = jnp.clip(taps_noise * (spread * channel_ramp)[None, :] / 64.0, -0.25, 0.25)
    return filter_values.astype(jnp.bfloat16)


def shard_levels(own_key, dims, pieces, low, largest):
    def one(dim, blocks):
        heights = jax.random.uniform(jax.random.fold_in(jax.random.fold_in(own_key, 6), dim), (blocks,), jnp.float32, low / len(pieces), largest / len(pieces))
        return jnp.repeat(jnp.exp(heights), dims[dim] // blocks).reshape((-1,) + (1,) * (len(dims) - dim - 1))

    gain = one(*pieces[0])
    for cut in pieces[1:]:
        gain = gain * one(*cut)
    return gain


def bell_draw(rng, dims, width, most, pieces=(), kind=jnp.bfloat16):
    values = jax.random.normal(rng, dims, jnp.float32) * width
    if len(pieces) > 0:
        values = shard_levels(rng, dims, pieces, -0.22, 0.18) * values
    return jnp.clip(values, min=-most, max=most).astype(kind)


def setup_inputs(seed: int = 0) -> dict:
    seeds = jax.random.split(jax.random.key(seed), 9)
    hyena_gate = bell_draw(seeds[0], (SEQ, DW), 1.0, 6.0, ((0, 8), (1, 4)))
    hyena_key = bell_draw(seeds[1], (SEQ, DW), 1.0, 6.0, ((0, 8), (1, 4)))
    hyena_value = bell_draw(seeds[2], (SEQ, DW), 1.0, 6.0, ((0, 8), (1, 4)))
    filter_taps = draw_filter_taps(jax.random.fold_in(seeds[8], 71), 0)
    skip_weight = bell_draw(seeds[4], (DW,), 1.0, 4.0, ((0, 4),), jnp.float32)
    queries = draw_queries(jax.random.fold_in(seeds[8], 71), 0)
    attn_keys = draw_attn_keys(jax.random.fold_in(seeds[8], 71), 0)
    valid_length = jax.random.randint(seeds[7], (1,), SEQ - 4 * GROUP + 1, SEQ + 1).astype(jnp.int32)
    return {"hyena_gate": hyena_gate, "hyena_key": hyena_key, "hyena_value": hyena_value, "filter_taps": filter_taps, "skip_weight": skip_weight, "queries": queries, "attn_keys": attn_keys, "valid_length": valid_length}


def reference(hyena_gate, hyena_key, hyena_value, filter_taps, skip_weight, queries, attn_keys, valid_length):
    mixed = (hyena_key.astype(jnp.float32) * hyena_value.astype(jnp.float32)).astype(jnp.bfloat16)
    mixed_float = mixed.astype(jnp.float32)
    doubled = 2 * SEQ
    spectrum = jnp.fft.rfft(mixed_float, n=doubled, axis=0) * jnp.fft.rfft(filter_taps.astype(jnp.float32), n=doubled, axis=0)
    convolved = jnp.fft.irfft(spectrum, n=doubled, axis=0)[:SEQ].astype(jnp.float32)
    positions = jnp.arange(SEQ, dtype=jnp.int32)
    valid_rows = positions < valid_length[0]
    gated = hyena_gate.astype(jnp.float32) * (convolved + skip_weight[None, :] * mixed_float)
    hyena_out = jnp.where(valid_rows[:, None], gated, 0.0).astype(jnp.bfloat16)
    allowed = (positions[None, :] <= positions[:, None]) & valid_rows[None, :]
    scale = 1.0 / math.sqrt(HD)

    def one_head(head):
        first = (head * HD).astype(jnp.int32)
        head_queries = lax.dynamic_slice_in_dim(queries, first, HD, 1)
        head_keys = lax.dynamic_slice_in_dim(attn_keys, first, HD, 1)
        head_values = lax.dynamic_slice_in_dim(hyena_out, first, HD, 1)
        score = jnp.dot(head_queries, head_keys.T, preferred_element_type=jnp.float32) * scale
        score = jnp.where(allowed, score, -1e+30)
        row_max = lax.optimization_barrier(jnp.max(score, axis=1, keepdims=True))
        raw = jnp.where(allowed, jnp.exp(score - row_max), 0.0)
        totals = lax.optimization_barrier(jnp.sum(raw, axis=1, keepdims=True))
        weights = raw.astype(jnp.bfloat16)
        return jnp.dot(weights, head_values, preferred_element_type=jnp.float32) / totals
    per_head = lax.map(one_head, jnp.arange(HEADS, dtype=jnp.int32))
    attended = jnp.transpose(per_head, (1, 0, 2)).reshape(SEQ, HEADS * HD)
    norm = jnp.sqrt(lax.optimization_barrier(jnp.mean(attended * attended, axis=1, keepdims=True)) + 1e-06)
    attn_out = jnp.where(valid_rows[:, None], attended / norm, 0.0).astype(jnp.bfloat16)
    return (hyena_out, attn_out)
```

```python
import functools
import math

import jax
import jax.numpy as jnp
import numpy as np
from jax import lax
from jax.experimental import pallas as pl
from jax.experimental.pallas import tpu as pltpu
from jax.sharding import PartitionSpec as P

HD = 128
DW = 4096


def tables(group_rows):
    doubled = 2 * group_rows
    freq = jnp.arange(doubled, dtype=jnp.int32)[:, None]
    place = jnp.arange(group_rows, dtype=jnp.int32)[None, :]
    phase = (freq * place % doubled).astype(jnp.float32) * (2.0 * math.pi / doubled)
    parity = (1 - 2 * (jnp.arange(doubled, dtype=jnp.int32) % 2)).astype(jnp.float32)[:, None]
    cosine = jnp.cos(phase)
    sine = jnp.sin(phase)
    cos_high = cosine.astype(jnp.bfloat16)
    cos_low = (cosine - cos_high.astype(jnp.float32)).astype(jnp.bfloat16)
    sin_high = sine.astype(jnp.bfloat16)
    sin_low = (sine - sin_high.astype(jnp.float32)).astype(jnp.bfloat16)
    return ((cos_high, cos_low, sin_high, sin_low, cosine, sine), parity)


def split_dot(high, low, block):
    return jnp.dot(high, block, preferred_element_type=jnp.float32) + jnp.dot(
        low, block, preferred_element_type=jnp.float32
    )


def forward(tabs, block):
    return (split_dot(tabs[0], tabs[1], block), -split_dot(tabs[2], tabs[3], block))


def inverse(tabs, real_part, imag_part):
    cosine, sine = (tabs[4], tabs[5])
    scale = 1.0 / cosine.shape[0]
    first = jnp.dot(
        cosine.T, real_part, precision=lax.Precision.HIGH, preferred_element_type=jnp.float32
    )
    second = jnp.dot(
        sine.T, imag_part, precision=lax.Precision.HIGH, preferred_element_type=jnp.float32
    )
    return (first - second) * scale


def complex_mul(left_real, left_imag, right_real, right_imag):
    return (
        left_real * right_real - left_imag * right_imag,
        left_real * right_imag + left_imag * right_real,
    )


def shards(
    hyena_gate, hyena_key, hyena_value, filter_taps, skip_weight, queries, attn_keys, valid_length
):
    group_rows = hyena_gate.shape[0]
    ranks = lax.axis_size("ctx")
    own_index = lax.axis_index("ctx")
    tabs, parity = tables(group_rows)
    mixed = (hyena_key.astype(jnp.float32) * hyena_value.astype(jnp.float32)).astype(jnp.bfloat16)
    mixed_float = mixed.astype(jnp.float32)
    input_real, input_imag = forward(tabs, mixed)
    own_block = lax.dynamic_slice_in_dim(filter_taps, own_index * group_rows, group_rows, 0)
    taps_real, taps_imag = forward(tabs, own_block)
    band = 2 * group_rows // ranks
    in_real = lax.all_to_all(
        input_real[None].astype(jnp.bfloat16), "ctx", split_axis=1, concat_axis=0, tiled=True
    ).astype(jnp.float32)
    in_imag = lax.all_to_all(
        input_imag[None].astype(jnp.bfloat16), "ctx", split_axis=1, concat_axis=0, tiled=True
    ).astype(jnp.float32)
    filt_real = lax.all_to_all(
        taps_real[None].astype(jnp.bfloat16), "ctx", split_axis=1, concat_axis=0, tiled=True
    ).astype(jnp.float32)
    filt_imag = lax.all_to_all(
        taps_imag[None].astype(jnp.bfloat16), "ctx", split_axis=1, concat_axis=0, tiled=True
    ).astype(jnp.float32)
    band_parity = lax.dynamic_slice_in_dim(parity, own_index * band, band, 0)[None]
    prior_real = jnp.concatenate([jnp.zeros_like(filt_real[:1]), filt_real[:-1]], 0)
    prior_imag = jnp.concatenate([jnp.zeros_like(filt_imag[:1]), filt_imag[:-1]], 0)
    lag_real = filt_real + band_parity * prior_real
    lag_imag = filt_imag + band_parity * prior_imag
    order = jnp.arange(ranks, dtype=jnp.int32)[:, None, None]

    def add_lag(lag, inner):
        later = order >= lag
        moved_real = jnp.where(later, jnp.roll(in_real, lag, 0), 0.0)
        moved_imag = jnp.where(later, jnp.roll(in_imag, lag, 0), 0.0)
        this_real = lax.dynamic_index_in_dim(lag_real, lag, 0, keepdims=True)
        this_imag = lax.dynamic_index_in_dim(lag_imag, lag, 0, keepdims=True)
        out_real, out_imag = complex_mul(this_real, this_imag, moved_real, moved_imag)
        return (inner[0] + out_real, inner[1] + out_imag)

    zeros = jnp.zeros_like(in_real)
    sum_real, sum_imag = lax.fori_loop(0, ranks, add_lag, (zeros, zeros))
    total_real = lax.all_to_all(
        sum_real.astype(jnp.bfloat16), "ctx", split_axis=0, concat_axis=1, tiled=True
    ).astype(sum_real.dtype)
    total_imag = lax.all_to_all(
        sum_imag.astype(jnp.bfloat16), "ctx", split_axis=0, concat_axis=1, tiled=True
    ).astype(sum_imag.dtype)
    convolved = inverse(tabs, total_real[0], total_imag[0])
    positions = own_index * group_rows + jnp.arange(group_rows, dtype=jnp.int32)
    valid_rows = (positions < valid_length[0])[:, None]
    gated = hyena_gate.astype(jnp.float32) * (convolved + skip_weight[None, :] * mixed_float)
    hyena_out = jnp.where(valid_rows, gated, 0.0).astype(jnp.bfloat16)
    heads_here = queries.shape[1] // HD
    scale = 1.0 / math.sqrt(HD)
    query_heads = queries.reshape(group_rows, heads_here, HD)
    start_max = jnp.full((heads_here, group_rows), -1e30, jnp.float32)
    key_piece = lax.all_gather(attn_keys, "ctx", axis=0, tiled=True)
    value_piece = lax.all_gather(hyena_out, "ctx", axis=0, tiled=True)
    width = key_piece.shape[0]
    key_heads = key_piece.reshape(width, heads_here, HD)
    value_heads = value_piece.reshape(width, heads_here, HD)
    scores = (
        jnp.einsum("qhd,khd->hqk", query_heads, key_heads, preferred_element_type=jnp.float32)
        * scale
    )
    key_places = jnp.arange(width, dtype=jnp.int32)
    allowed = (key_places[None, :] <= positions[:, None]) & (key_places < valid_length[0])[None, :]
    scores = jnp.where(allowed[None], scores, -1e30)
    new_max = jnp.maximum(start_max, jnp.max(scores, axis=2))
    weights = jnp.where(allowed[None], jnp.exp(scores - new_max[:, :, None]), 0.0)
    totals = jnp.sum(weights, axis=2)
    update = jnp.einsum(
        "hqk,khd->hqd",
        weights.astype(jnp.bfloat16),
        value_heads,
        preferred_element_type=jnp.float32,
    )
    attended = (update / totals[:, :, None]).transpose(1, 0, 2).reshape(group_rows, heads_here * HD)
    squares = jnp.sum(attended * attended, axis=1)
    total_squares = lax.psum(squares, "tp")
    scaled = attended / jnp.sqrt(total_squares / DW + 1e-06)[:, None]
    attn_out = jnp.where(valid_rows, scaled, 0.0).astype(jnp.bfloat16)
    return (hyena_out, attn_out)


MESH = pl.DeviceIdType.MESH
MIX, GATE, KEY, QUERY = range(4)


def half_shift_tables(block):
    freq = np.arange(block, dtype=np.float64)[:, None] + 0.5
    place = np.arange(2 * block, dtype=np.float64)[None, :] - block
    phase = freq * place * (math.pi / block)
    ahead = np.concatenate([np.cos(phase), -np.sin(phase)], 0)
    back = ahead[:, block:].T / block

    def split(table):
        high = table.astype(jnp.bfloat16)
        low = (table - high.astype(np.float64)).astype(jnp.bfloat16)
        return high, low

    return split(ahead) + split(back)


def head_kernel(
    ranks,
    depth,
    hk,
    hv,
    gate,
    taps,
    skip,
    queries,
    keys,
    valid,
    ahead_high,
    ahead_low,
    back_high,
    back_low,
    h_out,
    a_out,
    hk_v,
    hv_v,
    mix_v,
    taps_v,
    ah_v,
    al_v,
    bh_v,
    bl_v,
    got,
    lag_s,
    in_s,
    sum_high,
    sum_low,
    h_buf,
    a_buf,
    a_in,
    sq_mine,
    sq_in,
    local_sem,
    in_send,
    in_recv,
    h_send,
    h_recv,
    a_send,
    a_recv,
    sq_send,
    sq_recv,
):
    me = lax.axis_index("ctx")
    plane = lax.axis_index("tp")
    group = hk_v.shape[0]
    seq = ranks * group
    block = bh_v.shape[0]
    blocks = seq // block
    per_block = block // group

    def columns(index):
        return pl.ds(pl.multiple_of(index * HD, HD), HD)

    own = columns(me)
    local = [
        pltpu.make_async_copy(src, dst, local_sem.at[i])
        for i, (src, dst) in enumerate(
            (
                (hk, hk_v),
                (hv, hv_v),
                (taps.at[:, own], taps_v.at[pl.ds(block, seq)]),
                (ahead_high, ah_v),
                (ahead_low, al_v),
                (back_high, bh_v),
                (back_low, bl_v),
                (gate.at[:, own], got.at[GATE, me]),
                (keys.at[:, own], got.at[KEY, me]),
                (queries.at[:, own], got.at[QUERY, me]),
            )
        )
    ]
    for copy in local:
        copy.start()

    barrier = pltpu.get_barrier_semaphore()
    for step in range(1, ranks):
        pl.semaphore_signal(
            barrier, inc=1, device_id={"ctx": lax.rem(me + step, ranks)}, device_id_type=MESH
        )
    for step in range(1, depth):
        pl.semaphore_signal(
            barrier, inc=1, device_id={"tp": lax.rem(plane + step, depth)}, device_id_type=MESH
        )
    local[0].wait()
    local[1].wait()
    mix_v[...] = (hk_v[...].astype(jnp.float32) * hv_v[...].astype(jnp.float32)).astype(
        jnp.bfloat16
    )
    pl.semaphore_wait(barrier, ranks - 1 + depth - 1)

    sends = []
    for which, src in ((MIX, mix_v), (GATE, gate), (KEY, keys), (QUERY, queries)):
        for step in range(1, ranks):
            peer = lax.rem(me + step, ranks)
            copy = pltpu.make_async_remote_copy(
                src_ref=src.at[:, columns(peer)],
                dst_ref=got.at[which, me],
                send_sem=in_send.at[which, step],
                recv_sem=in_recv.at[which, me],
                device_id={"ctx": peer},
                device_id_type=MESH,
            )
            copy.start()
            sends.append(copy)

    def arrive(which):
        for step in range(1, ranks):
            peer = lax.rem(me + step, ranks)
            pltpu.make_async_remote_copy(
                src_ref=got.at[which, peer],
                dst_ref=got.at[which, peer],
                send_sem=in_send.at[which, step],
                recv_sem=in_recv.at[which, peer],
                device_id={"ctx": peer},
                device_id_type=MESH,
            ).wait_recv()

    got[MIX, me] = mix_v[:, own]
    taps_v[:block] = jnp.zeros((block, HD), jnp.bfloat16)
    for copy in local[2:7]:
        copy.wait()
    windows = jnp.concatenate(
        [taps_v[i * block : (i + 2) * block] for i in range(blocks)], axis=1
    )
    lag_s[...] = jnp.dot(ah_v[...], windows, preferred_element_type=jnp.float32) + jnp.dot(
        al_v[...], windows, preferred_element_type=jnp.float32
    )

    arrive(MIX)
    mixed = got[MIX].reshape(seq, HD)
    inputs = jnp.concatenate([mixed[i * block : (i + 1) * block] for i in range(blocks)], axis=1)
    in_s[...] = jnp.dot(
        ah_v[:, block:], inputs, preferred_element_type=jnp.float32
    ) + jnp.dot(al_v[:, block:], inputs, preferred_element_type=jnp.float32)

    rows_at_once = 16

    def multiply(step, carry):
        first = pl.multiple_of(step * rows_at_once, rows_at_once)
        real_rows = pl.ds(first, rows_at_once)
        imag_rows = pl.ds(block + first, rows_at_once)
        lanes = [slice(i * HD, (i + 1) * HD) for i in range(blocks)]
        in_real = [in_s[real_rows, s] for s in lanes]
        in_imag = [in_s[imag_rows, s] for s in lanes]
        lag_real = [lag_s[real_rows, s] for s in lanes]
        lag_imag = [lag_s[imag_rows, s] for s in lanes]
        for i in range(blocks):
            real = imag = None
            for j in range(i + 1):
                a, b, c, d = lag_real[i - j], lag_imag[i - j], in_real[j], in_imag[j]
                more_real = a * c - b * d
                more_imag = a * d + b * c
                real = more_real if real is None else real + more_real
                imag = more_imag if imag is None else imag + more_imag
            for rows, total in ((real_rows, real), (imag_rows, imag)):
                high = total.astype(jnp.bfloat16)
                sum_high[rows, lanes[i]] = high
                sum_low[rows, lanes[i]] = (total - high.astype(jnp.float32)).astype(jnp.bfloat16)
        return carry

    lax.fori_loop(0, block // rows_at_once, multiply, 0)
    convolved = (
        jnp.dot(bh_v[...], sum_high[...], preferred_element_type=jnp.float32)
        + jnp.dot(bl_v[...], sum_high[...], preferred_element_type=jnp.float32)
        + jnp.dot(bh_v[...], sum_low[...], preferred_element_type=jnp.float32)
    )

    length = valid[0]
    weight = skip[:, own]
    local[7].wait()
    arrive(GATE)
    row_ids = lax.broadcasted_iota(jnp.int32, (group, HD), 0)
    lane_ids = lax.broadcasted_iota(jnp.int32, (group, HD), 1)
    for g in range(ranks):
        part = convolved[
            g % per_block * group : (g % per_block + 1) * group,
            g // per_block * HD : (g // per_block + 1) * HD,
        ]
        gated = got[GATE, g].astype(jnp.float32) * (
            part + weight * got[MIX, g].astype(jnp.float32)
        )
        h_buf[g] = jnp.where(row_ids + g * group < length, gated, 0.0).astype(jnp.bfloat16)

    h_local = pltpu.make_async_copy(h_buf.at[me], h_out.at[:, own], local_sem.at[0])
    h_local.start()
    for step in range(1, ranks):
        peer = lax.rem(me + step, ranks)
        copy = pltpu.make_async_remote_copy(
            src_ref=h_buf.at[peer],
            dst_ref=h_out.at[:, own],
            send_sem=h_send.at[step],
            recv_sem=h_recv.at[me],
            device_id={"ctx": peer},
            device_id_type=MESH,
        )
        copy.start()
        sends.append(copy)

    local[8].wait()
    local[9].wait()
    arrive(KEY)
    arrive(QUERY)
    factor = math.log2(math.e) / math.sqrt(HD)
    order = [g for low in range(per_block - 1, -1, -1) for g in range(ranks - per_block + low, -1, -per_block)]

    def attended_copy(g, source):
        return pltpu.make_async_remote_copy(
            src_ref=a_buf.at[g],
            dst_ref=a_in.at[source],
            send_sem=a_send.at[g],
            recv_sem=a_recv.at[source],
            device_id={"ctx": g},
            device_id_type=MESH,
        )

    for g in order:
        width = (g + 1) * group
        score = lax.dot_general(
            got[QUERY, g],
            got[KEY, : g + 1].reshape(width, HD),
            (((1,), (1,)), ((), ())),
            preferred_element_type=jnp.float32,
        )
        last = jnp.where(lane_ids <= row_ids, score[:, g * group :], -1e30)
        score = last if g == 0 else jnp.concatenate([score[:, : g * group], last], axis=1)
        row_max = jnp.max(score, axis=1, keepdims=True)
        raw = jnp.exp2((score - row_max) * factor)
        totals = jnp.sum(raw, axis=1, keepdims=True)
        update = jnp.dot(
            raw.astype(jnp.bfloat16),
            h_buf[: g + 1].reshape(width, HD),
            preferred_element_type=jnp.float32,
        )
        a_buf[g] = (update / totals).astype(jnp.bfloat16)

        @pl.when(me != g)
        def _():
            attended_copy(g, me).start()

    a_in[me] = a_buf[me]
    for step in range(1, ranks):
        peer = lax.rem(me + step, ranks)
        attended_copy(peer, peer).wait_recv()

    squares = jnp.zeros((group, HD), jnp.float32)
    for s in range(ranks):
        piece = a_in[s].astype(jnp.float32)
        squares = squares + piece * piece
    row_squares = jnp.sum(squares.T, axis=0, keepdims=True)
    sq_mine[...] = jnp.broadcast_to(row_squares, sq_mine.shape)
    for step in range(1, depth):
        other = lax.rem(plane + step, depth)
        copy = pltpu.make_async_remote_copy(
            src_ref=sq_mine,
            dst_ref=sq_in.at[plane],
            send_sem=sq_send.at[step],
            recv_sem=sq_recv.at[plane],
            device_id={"tp": other},
            device_id_type=MESH,
        )
        copy.start()
        sends.append(copy)
    total_squares = sq_mine[:1]
    for step in range(1, depth):
        other = lax.rem(plane + step, depth)
        pltpu.make_async_remote_copy(
            src_ref=sq_in.at[other],
            dst_ref=sq_in.at[other],
            send_sem=sq_send.at[step],
            recv_sem=sq_recv.at[other],
            device_id={"tp": other},
            device_id_type=MESH,
        ).wait_recv()
        total_squares = total_squares + sq_in[other][:1]
    inverse_norm = lax.rsqrt(total_squares * (1.0 / (depth * ranks * HD)) + 1e-06)
    by_row = jnp.broadcast_to(inverse_norm, (group, HD)).T
    by_row = jnp.where(row_ids + me * group < length, by_row, 0.0)
    for s in range(ranks):
        a_out[:, s * HD : (s + 1) * HD] = (a_in[s].astype(jnp.float32) * by_row).astype(
            jnp.bfloat16
        )

    h_local.wait()
    for step in range(1, ranks):
        peer = lax.rem(me + step, ranks)
        pltpu.make_async_remote_copy(
            src_ref=h_buf.at[peer],
            dst_ref=h_out.at[:, columns(peer)],
            send_sem=h_send.at[step],
            recv_sem=h_recv.at[peer],
            device_id={"ctx": peer},
            device_id_type=MESH,
        ).wait_recv()
        attended_copy(peer, me).wait_send()
    for copy in sends:
        copy.wait_send()


def head_shards(ranks, depth, *arrays):
    hyena_gate, hyena_key, hyena_value, filter_taps, skip_weight, queries, attn_keys, valid = arrays
    group, channels = hyena_gate.shape
    seq = filter_taps.shape[0]
    block = 2 * group if ranks % 2 == 0 else group
    blocks = seq // block
    bf16, f32 = jnp.bfloat16, jnp.float32
    any_space = pl.BlockSpec(memory_space=pl.ANY)
    vmem = pl.BlockSpec(memory_space=pltpu.VMEM)
    smem = pl.BlockSpec(memory_space=pltpu.SMEM)
    return pl.pallas_call(
        functools.partial(head_kernel, ranks, depth),
        out_shape=(
            jax.ShapeDtypeStruct((group, channels), bf16),
            jax.ShapeDtypeStruct((group, channels), bf16),
        ),
        in_specs=[any_space] * 4 + [vmem] + [any_space] * 2 + [smem] + [any_space] * 4,
        out_specs=(any_space, vmem),
        scratch_shapes=[
            pltpu.VMEM((group, channels), bf16),
            pltpu.VMEM((group, channels), bf16),
            pltpu.VMEM((group, channels), bf16),
            pltpu.VMEM((block + seq, HD), bf16),
            pltpu.VMEM((2 * block, 2 * block), bf16),
            pltpu.VMEM((2 * block, 2 * block), bf16),
            pltpu.VMEM((block, 2 * block), bf16),
            pltpu.VMEM((block, 2 * block), bf16),
            pltpu.VMEM((4, ranks, group, HD), bf16),
            pltpu.VMEM((2 * block, blocks * HD), f32),
            pltpu.VMEM((2 * block, blocks * HD), f32),
            pltpu.VMEM((2 * block, blocks * HD), bf16),
            pltpu.VMEM((2 * block, blocks * HD), bf16),
            pltpu.VMEM((ranks, group, HD), bf16),
            pltpu.VMEM((ranks, group, HD), bf16),
            pltpu.VMEM((ranks, group, HD), bf16),
            pltpu.VMEM((8, group), f32),
            pltpu.VMEM((depth, 8, group), f32),
            pltpu.SemaphoreType.DMA((10,)),
            pltpu.SemaphoreType.DMA((4, ranks)),
            pltpu.SemaphoreType.DMA((4, ranks)),
            pltpu.SemaphoreType.DMA((ranks,)),
            pltpu.SemaphoreType.DMA((ranks,)),
            pltpu.SemaphoreType.DMA((ranks,)),
            pltpu.SemaphoreType.DMA((ranks,)),
            pltpu.SemaphoreType.DMA((depth,)),
            pltpu.SemaphoreType.DMA((depth,)),
        ],
        compiler_params=pltpu.CompilerParams(
            collective_id=0, has_side_effects=True, vmem_limit_bytes=40 * 1024 * 1024
        ),
    )(
        hyena_key,
        hyena_value,
        hyena_gate,
        filter_taps,
        skip_weight.reshape(1, channels),
        queries,
        attn_keys,
        valid,
        *(jnp.asarray(table) for table in half_shift_tables(block)),
    )


def solution(mesh):
    in_specs = (
        P("ctx", "tp"),
        P("ctx", "tp"),
        P("ctx", "tp"),
        P(None, "tp"),
        P("tp"),
        P("ctx", "tp"),
        P("ctx", "tp"),
        P(),
    )
    out_specs = (P("ctx", "tp"), P("ctx", "tp"))
    ranks, depth = mesh.shape["ctx"], mesh.shape["tp"]
    body = functools.partial(head_shards, ranks, depth) if DW // depth == ranks * HD else shards
    return jax.shard_map(
        body, mesh=mesh, in_specs=in_specs, out_specs=out_specs, check_vma=False
    )
```

```python
import functools
import math

import jax
import jax.numpy as jnp
import numpy as np
from jax import lax
from jax.experimental import pallas as pl
from jax.experimental.pallas import tpu as pltpu
from jax.sharding import PartitionSpec as P

HD = 128
DW = 4096


def tables(group_rows):
    doubled = 2 * group_rows
    freq = jnp.arange(doubled, dtype=jnp.int32)[:, None]
    place = jnp.arange(group_rows, dtype=jnp.int32)[None, :]
    phase = (freq * place % doubled).astype(jnp.float32) * (2.0 * math.pi / doubled)
    parity = (1 - 2 * (jnp.arange(doubled, dtype=jnp.int32) % 2)).astype(jnp.float32)[:, None]
    cosine = jnp.cos(phase)
    sine = jnp.sin(phase)
    cos_high = cosine.astype(jnp.bfloat16)
    cos_low = (cosine - cos_high.astype(jnp.float32)).astype(jnp.bfloat16)
    sin_high = sine.astype(jnp.bfloat16)
    sin_low = (sine - sin_high.astype(jnp.float32)).astype(jnp.bfloat16)
    return ((cos_high, cos_low, sin_high, sin_low, cosine, sine), parity)


def split_dot(high, low, block):
    return jnp.dot(high, block, preferred_element_type=jnp.float32) + jnp.dot(
        low, block, preferred_element_type=jnp.float32
    )


def forward(tabs, block):
    return (split_dot(tabs[0], tabs[1], block), -split_dot(tabs[2], tabs[3], block))


def inverse(tabs, real_part, imag_part):
    cosine, sine = (tabs[4], tabs[5])
    scale = 1.0 / cosine.shape[0]
    first = jnp.dot(
        cosine.T, real_part, precision=lax.Precision.HIGH, preferred_element_type=jnp.float32
    )
    second = jnp.dot(
        sine.T, imag_part, precision=lax.Precision.HIGH, preferred_element_type=jnp.float32
    )
    return (first - second) * scale


def complex_mul(left_real, left_imag, right_real, right_imag):
    return (
        left_real * right_real - left_imag * right_imag,
        left_real * right_imag + left_imag * right_real,
    )


def shards(
    hyena_gate, hyena_key, hyena_value, filter_taps, skip_weight, queries, attn_keys, valid_length
):
    group_rows = hyena_gate.shape[0]
    ranks = lax.axis_size("ctx")
    own_index = lax.axis_index("ctx")
    tabs, parity = tables(group_rows)
    mixed = (hyena_key.astype(jnp.float32) * hyena_value.astype(jnp.float32)).astype(jnp.bfloat16)
    mixed_float = mixed.astype(jnp.float32)
    input_real, input_imag = forward(tabs, mixed)
    own_block = lax.dynamic_slice_in_dim(filter_taps, own_index * group_rows, group_rows, 0)
    taps_real, taps_imag = forward(tabs, own_block)
    band = 2 * group_rows // ranks
    in_real = lax.all_to_all(
        input_real[None].astype(jnp.bfloat16), "ctx", split_axis=1, concat_axis=0, tiled=True
    ).astype(jnp.float32)
    in_imag = lax.all_to_all(
        input_imag[None].astype(jnp.bfloat16), "ctx", split_axis=1, concat_axis=0, tiled=True
    ).astype(jnp.float32)
    filt_real = lax.all_to_all(
        taps_real[None].astype(jnp.bfloat16), "ctx", split_axis=1, concat_axis=0, tiled=True
    ).astype(jnp.float32)
    filt_imag = lax.all_to_all(
        taps_imag[None].astype(jnp.bfloat16), "ctx", split_axis=1, concat_axis=0, tiled=True
    ).astype(jnp.float32)
    band_parity = lax.dynamic_slice_in_dim(parity, own_index * band, band, 0)[None]
    prior_real = jnp.concatenate([jnp.zeros_like(filt_real[:1]), filt_real[:-1]], 0)
    prior_imag = jnp.concatenate([jnp.zeros_like(filt_imag[:1]), filt_imag[:-1]], 0)
    lag_real = filt_real + band_parity * prior_real
    lag_imag = filt_imag + band_parity * prior_imag
    order = jnp.arange(ranks, dtype=jnp.int32)[:, None, None]

    def add_lag(lag, inner):
        later = order >= lag
        moved_real = jnp.where(later, jnp.roll(in_real, lag, 0), 0.0)
        moved_imag = jnp.where(later, jnp.roll(in_imag, lag, 0), 0.0)
        this_real = lax.dynamic_index_in_dim(lag_real, lag, 0, keepdims=True)
        this_imag = lax.dynamic_index_in_dim(lag_imag, lag, 0, keepdims=True)
        out_real, out_imag = complex_mul(this_real, this_imag, moved_real, moved_imag)
        return (inner[0] + out_real, inner[1] + out_imag)

    zeros = jnp.zeros_like(in_real)
    sum_real, sum_imag = lax.fori_loop(0, ranks, add_lag, (zeros, zeros))
    total_real = lax.all_to_all(
        sum_real.astype(jnp.bfloat16), "ctx", split_axis=0, concat_axis=1, tiled=True
    ).astype(sum_real.dtype)
    total_imag = lax.all_to_all(
        sum_imag.astype(jnp.bfloat16), "ctx", split_axis=0, concat_axis=1, tiled=True
    ).astype(sum_imag.dtype)
    convolved = inverse(tabs, total_real[0], total_imag[0])
    positions = own_index * group_rows + jnp.arange(group_rows, dtype=jnp.int32)
    valid_rows = (positions < valid_length[0])[:, None]
    gated = hyena_gate.astype(jnp.float32) * (convolved + skip_weight[None, :] * mixed_float)
    hyena_out = jnp.where(valid_rows, gated, 0.0).astype(jnp.bfloat16)
    heads_here = queries.shape[1] // HD
    scale = 1.0 / math.sqrt(HD)
    query_heads = queries.reshape(group_rows, heads_here, HD)
    start_max = jnp.full((heads_here, group_rows), -1e30, jnp.float32)
    key_piece = lax.all_gather(attn_keys, "ctx", axis=0, tiled=True)
    value_piece = lax.all_gather(hyena_out, "ctx", axis=0, tiled=True)
    width = key_piece.shape[0]
    key_heads = key_piece.reshape(width, heads_here, HD)
    value_heads = value_piece.reshape(width, heads_here, HD)
    scores = (
        jnp.einsum("qhd,khd->hqk", query_heads, key_heads, preferred_element_type=jnp.float32)
        * scale
    )
    key_places = jnp.arange(width, dtype=jnp.int32)
    allowed = (key_places[None, :] <= positions[:, None]) & (key_places < valid_length[0])[None, :]
    scores = jnp.where(allowed[None], scores, -1e30)
    new_max = jnp.maximum(start_max, jnp.max(scores, axis=2))
    weights = jnp.where(allowed[None], jnp.exp(scores - new_max[:, :, None]), 0.0)
    totals = jnp.sum(weights, axis=2)
    update = jnp.einsum(
        "hqk,khd->hqd",
        weights.astype(jnp.bfloat16),
        value_heads,
        preferred_element_type=jnp.float32,
    )
    attended = (update / totals[:, :, None]).transpose(1, 0, 2).reshape(group_rows, heads_here * HD)
    squares = jnp.sum(attended * attended, axis=1)
    total_squares = lax.psum(squares, "tp")
    scaled = attended / jnp.sqrt(total_squares / DW + 1e-06)[:, None]
    attn_out = jnp.where(valid_rows, scaled, 0.0).astype(jnp.bfloat16)
    return (hyena_out, attn_out)


MESH = pl.DeviceIdType.MESH
MIX, GATE, KEY, QUERY = range(4)


def half_shift_tables(block):
    freq = np.arange(block, dtype=np.float64)[:, None] + 0.5
    place = np.arange(2 * block, dtype=np.float64)[None, :] - block
    phase = freq * place * (math.pi / block)
    ahead = np.concatenate([np.cos(phase), -np.sin(phase)], 0)
    back = ahead[:, block:].T / block

    def split(table):
        high = table.astype(jnp.bfloat16)
        low = (table - high.astype(np.float64)).astype(jnp.bfloat16)
        return high, low

    return split(ahead) + split(back)


def head_kernel(
    ranks,
    depth,
    hk,
    hv,
    gate,
    taps,
    skip,
    queries,
    keys,
    valid,
    ahead_high,
    ahead_low,
    back_high,
    back_low,
    h_out,
    a_out,
    hk_v,
    hv_v,
    mix_v,
    taps_v,
    ah_v,
    al_v,
    bh_v,
    bl_v,
    got,
    lag_s,
    in_s,
    sum_high,
    sum_low,
    h_buf,
    a_buf,
    a_in,
    skip_v,
    length_s,
    sq_mine,
    sq_in,
    sq_sum,
    sq_got,
    local_sem,
    in_send,
    in_recv,
    h_send,
    h_recv,
    a_send,
    a_recv,
    sq_send,
    sq_recv,
    total_send,
    total_recv,
):
    me = lax.axis_index("ctx")
    plane = lax.axis_index("tp")
    group = hk_v.shape[0]
    seq = ranks * group
    block = bh_v.shape[0]
    blocks = seq // block
    per_block = block // group

    def columns(index):
        return pl.ds(pl.multiple_of(index * HD, HD), HD)

    own = columns(me)
    local = [
        pltpu.make_async_copy(src, dst, local_sem.at[i])
        for i, (src, dst) in enumerate(
            (
                (hk, hk_v),
                (hv, hv_v),
                (taps.at[:, own], taps_v.at[pl.ds(block, seq)]),
                (ahead_high, ah_v),
                (ahead_low, al_v),
                (back_high, bh_v),
                (back_low, bl_v),
                (gate.at[:, own], got.at[GATE, me]),
                (keys.at[:, own], got.at[KEY, me]),
                (queries.at[:, own], got.at[QUERY, me]),
                (skip.at[:, own], skip_v),
                (valid, length_s),
            )
        )
    ]
    for copy in local:
        copy.start()

    barrier = pltpu.get_barrier_semaphore()
    for step in range(1, ranks):
        pl.semaphore_signal(
            barrier, inc=1, device_id={"ctx": lax.rem(me + step, ranks)}, device_id_type=MESH
        )
    for step in range(1, depth):
        pl.semaphore_signal(
            barrier, inc=1, device_id={"tp": lax.rem(plane + step, depth)}, device_id_type=MESH
        )
    local[0].wait()
    local[1].wait()
    mix_v[...] = (hk_v[...].astype(jnp.float32) * hv_v[...].astype(jnp.float32)).astype(
        jnp.bfloat16
    )
    pl.semaphore_wait(barrier, ranks - 1 + depth - 1)

    sends = []
    for which, src in ((MIX, mix_v), (GATE, gate), (KEY, keys), (QUERY, queries)):
        for step in range(1, ranks):
            peer = lax.rem(me + step, ranks)
            copy = pltpu.make_async_remote_copy(
                src_ref=src.at[:, columns(peer)],
                dst_ref=got.at[which, me],
                send_sem=in_send.at[which, step],
                recv_sem=in_recv.at[which, me],
                device_id={"ctx": peer},
                device_id_type=MESH,
            )
            copy.start()
            sends.append(copy)

    def arrive(which):
        for step in range(1, ranks):
            peer = lax.rem(me + step, ranks)
            pltpu.make_async_remote_copy(
                src_ref=got.at[which, peer],
                dst_ref=got.at[which, peer],
                send_sem=in_send.at[which, step],
                recv_sem=in_recv.at[which, peer],
                device_id={"ctx": peer},
                device_id_type=MESH,
            ).wait_recv()

    got[MIX, me] = mix_v[:, own]
    taps_v[:block] = jnp.zeros((block, HD), jnp.bfloat16)
    for copy in local[2:7]:
        copy.wait()
    windows = jnp.concatenate(
        [taps_v[i * block : (i + 2) * block] for i in range(blocks)], axis=1
    )
    lag_s[...] = jnp.dot(ah_v[...], windows, preferred_element_type=jnp.float32) + jnp.dot(
        al_v[...], windows, preferred_element_type=jnp.float32
    )

    arrive(MIX)
    mixed = got[MIX].reshape(seq, HD)
    inputs = jnp.concatenate([mixed[i * block : (i + 1) * block] for i in range(blocks)], axis=1)
    in_s[...] = jnp.dot(
        ah_v[:, block:], inputs, preferred_element_type=jnp.float32
    ) + jnp.dot(al_v[:, block:], inputs, preferred_element_type=jnp.float32)

    rows_at_once = 16

    def multiply(step, carry):
        first = pl.multiple_of(step * rows_at_once, rows_at_once)
        real_rows = pl.ds(first, rows_at_once)
        imag_rows = pl.ds(block + first, rows_at_once)
        lanes = [slice(i * HD, (i + 1) * HD) for i in range(blocks)]
        in_real = [in_s[real_rows, s] for s in lanes]
        in_imag = [in_s[imag_rows, s] for s in lanes]
        lag_real = [lag_s[real_rows, s] for s in lanes]
        lag_imag = [lag_s[imag_rows, s] for s in lanes]
        for i in range(blocks):
            real = imag = None
            for j in range(i + 1):
                a, b, c, d = lag_real[i - j], lag_imag[i - j], in_real[j], in_imag[j]
                more_real = a * c - b * d
                more_imag = a * d + b * c
                real = more_real if real is None else real + more_real
                imag = more_imag if imag is None else imag + more_imag
            for rows, total in ((real_rows, real), (imag_rows, imag)):
                high = total.astype(jnp.bfloat16)
                sum_high[rows, lanes[i]] = high
                sum_low[rows, lanes[i]] = (total - high.astype(jnp.float32)).astype(jnp.bfloat16)
        return carry

    lax.fori_loop(0, block // rows_at_once, multiply, 0)
    convolved = (
        jnp.dot(bh_v[...], sum_high[...], preferred_element_type=jnp.float32)
        + jnp.dot(bl_v[...], sum_high[...], preferred_element_type=jnp.float32)
        + jnp.dot(bh_v[...], sum_low[...], preferred_element_type=jnp.float32)
    )

    local[7].wait()
    local[10].wait()
    local[11].wait()
    length = length_s[0]
    weight = skip_v[...]
    arrive(GATE)
    row_ids = lax.broadcasted_iota(jnp.int32, (group, HD), 0)
    lane_ids = lax.broadcasted_iota(jnp.int32, (group, HD), 1)
    for g in range(ranks):
        part = convolved[
            g % per_block * group : (g % per_block + 1) * group,
            g // per_block * HD : (g // per_block + 1) * HD,
        ]
        gated = got[GATE, g].astype(jnp.float32) * (
            part + weight * got[MIX, g].astype(jnp.float32)
        )
        h_buf[g] = jnp.where(row_ids + g * group < length, gated, 0.0).astype(jnp.bfloat16)

    h_local = pltpu.make_async_copy(h_buf.at[me], h_out.at[:, own], local_sem.at[0])
    h_local.start()
    for step in range(1, ranks):
        peer = lax.rem(me + step, ranks)
        copy = pltpu.make_async_remote_copy(
            src_ref=h_buf.at[peer],
            dst_ref=h_out.at[:, own],
            send_sem=h_send.at[step],
            recv_sem=h_recv.at[me],
            device_id={"ctx": peer},
            device_id_type=MESH,
        )
        copy.start()
        sends.append(copy)

    local[8].wait()
    local[9].wait()
    arrive(KEY)
    arrive(QUERY)
    factor = math.log2(math.e) / math.sqrt(HD)
    order = [g for low in range(per_block - 1, -1, -1) for g in range(ranks - per_block + low, -1, -per_block)]

    def attended_copy(g, source):
        return pltpu.make_async_remote_copy(
            src_ref=a_buf.at[g],
            dst_ref=a_in.at[source],
            send_sem=a_send.at[g],
            recv_sem=a_recv.at[source],
            device_id={"ctx": g},
            device_id_type=MESH,
        )

    for g in order:
        width = (g + 1) * group
        score = lax.dot_general(
            got[QUERY, g],
            got[KEY, : g + 1].reshape(width, HD),
            (((1,), (1,)), ((), ())),
            preferred_element_type=jnp.float32,
        )
        last = jnp.where(lane_ids <= row_ids, score[:, g * group :], -1e30)
        score = last if g == 0 else jnp.concatenate([score[:, : g * group], last], axis=1)
        row_max = jnp.max(score, axis=1, keepdims=True)
        raw = jnp.exp2((score - row_max) * factor)
        totals = jnp.sum(raw, axis=1, keepdims=True)
        update = jnp.dot(
            raw.astype(jnp.bfloat16),
            h_buf[: g + 1].reshape(width, HD),
            preferred_element_type=jnp.float32,
        )
        attended = update / totals
        a_buf[g] = attended.astype(jnp.bfloat16)
        sq_mine[g : g + 1] = jnp.sum((attended * attended).T, axis=0, keepdims=True)

        @pl.when(me != g)
        def _():
            attended_copy(g, me).start()

    for step in range(1, depth):
        other = lax.rem(plane + step, depth)
        copy = pltpu.make_async_remote_copy(
            src_ref=sq_mine,
            dst_ref=sq_in.at[plane],
            send_sem=sq_send.at[step],
            recv_sem=sq_recv.at[plane],
            device_id={"tp": other},
            device_id_type=MESH,
        )
        copy.start()
        sends.append(copy)
    a_in[me] = a_buf[me]
    slot_squares = sq_mine[...]
    for step in range(1, depth):
        other = lax.rem(plane + step, depth)
        pltpu.make_async_remote_copy(
            src_ref=sq_in.at[other],
            dst_ref=sq_in.at[other],
            send_sem=sq_send.at[step],
            recv_sem=sq_recv.at[other],
            device_id={"tp": other},
            device_id_type=MESH,
        ).wait_recv()
        slot_squares = slot_squares + sq_in[other]
    for g in range(ranks):
        sq_sum[g] = jnp.broadcast_to(slot_squares[g : g + 1], sq_sum.shape[1:])
    for step in range(1, ranks):
        peer = lax.rem(me + step, ranks)
        copy = pltpu.make_async_remote_copy(
            src_ref=sq_sum.at[peer],
            dst_ref=sq_got.at[me],
            send_sem=total_send.at[step],
            recv_sem=total_recv.at[me],
            device_id={"ctx": peer},
            device_id_type=MESH,
        )
        copy.start()
        sends.append(copy)
    total_squares = sq_sum[me]
    for step in range(1, ranks):
        peer = lax.rem(me + step, ranks)
        pltpu.make_async_remote_copy(
            src_ref=sq_sum.at[peer],
            dst_ref=sq_got.at[peer],
            send_sem=total_send.at[step],
            recv_sem=total_recv.at[peer],
            device_id={"ctx": peer},
            device_id_type=MESH,
        ).wait_recv()
        total_squares = total_squares + sq_got[peer]
    inverse_norm = lax.rsqrt(total_squares[:1] * (1.0 / (depth * ranks * HD)) + 1e-06)
    by_row = jnp.broadcast_to(inverse_norm, (group, HD)).T
    by_row = jnp.where(row_ids + me * group < length, by_row, 0.0)
    for step in range(1, ranks):
        peer = lax.rem(me + step, ranks)
        attended_copy(peer, peer).wait_recv()
    for s in range(ranks):
        a_out[:, s * HD : (s + 1) * HD] = (a_in[s].astype(jnp.float32) * by_row).astype(
            jnp.bfloat16
        )

    h_local.wait()
    for step in range(1, ranks):
        peer = lax.rem(me + step, ranks)
        pltpu.make_async_remote_copy(
            src_ref=h_buf.at[peer],
            dst_ref=h_out.at[:, columns(peer)],
            send_sem=h_send.at[step],
            recv_sem=h_recv.at[peer],
            device_id={"ctx": peer},
            device_id_type=MESH,
        ).wait_recv()
        attended_copy(peer, me).wait_send()
    for copy in sends:
        copy.wait_send()


def head_shards(ranks, depth, *arrays):
    hyena_gate, hyena_key, hyena_value, filter_taps, skip_weight, queries, attn_keys, valid = arrays
    group, channels = hyena_gate.shape
    seq = filter_taps.shape[0]
    block = 2 * group if ranks % 2 == 0 else group
    blocks = seq // block
    bf16, f32 = jnp.bfloat16, jnp.float32
    any_space = pl.BlockSpec(memory_space=pl.ANY)
    vmem = pl.BlockSpec(memory_space=pltpu.VMEM)
    hbm = pl.BlockSpec(memory_space=pltpu.HBM)
    return pl.pallas_call(
        functools.partial(head_kernel, ranks, depth),
        out_shape=(
            jax.ShapeDtypeStruct((group, channels), bf16),
            jax.ShapeDtypeStruct((group, channels), bf16),
        ),
        in_specs=[hbm] * 12,
        out_specs=(any_space, vmem),
        scratch_shapes=[
            pltpu.VMEM((group, channels), bf16),
            pltpu.VMEM((group, channels), bf16),
            pltpu.VMEM((group, channels), bf16),
            pltpu.VMEM((block + seq, HD), bf16),
            pltpu.VMEM((2 * block, 2 * block), bf16),
            pltpu.VMEM((2 * block, 2 * block), bf16),
            pltpu.VMEM((block, 2 * block), bf16),
            pltpu.VMEM((block, 2 * block), bf16),
            pltpu.VMEM((4, ranks, group, HD), bf16),
            pltpu.VMEM((2 * block, blocks * HD), f32),
            pltpu.VMEM((2 * block, blocks * HD), f32),
            pltpu.VMEM((2 * block, blocks * HD), bf16),
            pltpu.VMEM((2 * block, blocks * HD), bf16),
            pltpu.VMEM((ranks, group, HD), bf16),
            pltpu.VMEM((ranks, group, HD), bf16),
            pltpu.VMEM((ranks, group, HD), bf16),
            pltpu.VMEM((1, HD), f32),
            pltpu.SMEM((1,), jnp.int32),
            pltpu.VMEM((ranks, group), f32),
            pltpu.VMEM((depth, ranks, group), f32),
            pltpu.VMEM((ranks, 8, group), f32),
            pltpu.VMEM((ranks, 8, group), f32),
            pltpu.SemaphoreType.DMA((12,)),
            pltpu.SemaphoreType.DMA((4, ranks)),
            pltpu.SemaphoreType.DMA((4, ranks)),
            pltpu.SemaphoreType.DMA((ranks,)),
            pltpu.SemaphoreType.DMA((ranks,)),
            pltpu.SemaphoreType.DMA((ranks,)),
            pltpu.SemaphoreType.DMA((ranks,)),
            pltpu.SemaphoreType.DMA((depth,)),
            pltpu.SemaphoreType.DMA((depth,)),
            pltpu.SemaphoreType.DMA((ranks,)),
            pltpu.SemaphoreType.DMA((ranks,)),
        ],
        compiler_params=pltpu.CompilerParams(
            collective_id=0, has_side_effects=True, vmem_limit_bytes=62 * 1024 * 1024
        ),
    )(
        hyena_key,
        hyena_value,
        hyena_gate,
        filter_taps,
        skip_weight.reshape(1, channels),
        queries,
        attn_keys,
        valid,
        *(jnp.asarray(table) for table in half_shift_tables(block)),
    )


def solution(mesh):
    in_specs = (
        P("ctx", "tp"),
        P("ctx", "tp"),
        P("ctx", "tp"),
        P(None, "tp"),
        P("tp"),
        P("ctx", "tp"),
        P("ctx", "tp"),
        P(),
    )
    out_specs = (P("ctx", "tp"), P("ctx", "tp"))
    ranks, depth = mesh.shape["ctx"], mesh.shape["tp"]
    body = functools.partial(head_shards, ranks, depth) if DW // depth == ranks * HD else shards
    return jax.shard_map(
        body, mesh=mesh, in_specs=in_specs, out_specs=out_specs, check_vma=False
    )
```

```python
import functools
import math

import jax
import jax.numpy as jnp
import numpy as np
from jax import lax
from jax.experimental import pallas as pl
from jax.experimental.pallas import tpu as pltpu
from jax.sharding import PartitionSpec as P

HD = 128
DW = 4096


def tables(group_rows):
    doubled = 2 * group_rows
    freq = jnp.arange(doubled, dtype=jnp.int32)[:, None]
    place = jnp.arange(group_rows, dtype=jnp.int32)[None, :]
    phase = (freq * place % doubled).astype(jnp.float32) * (2.0 * math.pi / doubled)
    parity = (1 - 2 * (jnp.arange(doubled, dtype=jnp.int32) % 2)).astype(jnp.float32)[:, None]
    cosine = jnp.cos(phase)
    sine = jnp.sin(phase)
    cos_high = cosine.astype(jnp.bfloat16)
    cos_low = (cosine - cos_high.astype(jnp.float32)).astype(jnp.bfloat16)
    sin_high = sine.astype(jnp.bfloat16)
    sin_low = (sine - sin_high.astype(jnp.float32)).astype(jnp.bfloat16)
    return ((cos_high, cos_low, sin_high, sin_low, cosine, sine), parity)


def split_dot(high, low, block):
    return jnp.dot(high, block, preferred_element_type=jnp.float32) + jnp.dot(
        low, block, preferred_element_type=jnp.float32
    )


def forward(tabs, block):
    return (split_dot(tabs[0], tabs[1], block), -split_dot(tabs[2], tabs[3], block))


def inverse(tabs, real_part, imag_part):
    cosine, sine = (tabs[4], tabs[5])
    scale = 1.0 / cosine.shape[0]
    first = jnp.dot(
        cosine.T, real_part, precision=lax.Precision.HIGH, preferred_element_type=jnp.float32
    )
    second = jnp.dot(
        sine.T, imag_part, precision=lax.Precision.HIGH, preferred_element_type=jnp.float32
    )
    return (first - second) * scale


def complex_mul(left_real, left_imag, right_real, right_imag):
    return (
        left_real * right_real - left_imag * right_imag,
        left_real * right_imag + left_imag * right_real,
    )


def shards(
    hyena_gate, hyena_key, hyena_value, filter_taps, skip_weight, queries, attn_keys, valid_length
):
    group_rows = hyena_gate.shape[0]
    ranks = lax.axis_size("ctx")
    own_index = lax.axis_index("ctx")
    tabs, parity = tables(group_rows)
    mixed = (hyena_key.astype(jnp.float32) * hyena_value.astype(jnp.float32)).astype(jnp.bfloat16)
    mixed_float = mixed.astype(jnp.float32)
    input_real, input_imag = forward(tabs, mixed)
    own_block = lax.dynamic_slice_in_dim(filter_taps, own_index * group_rows, group_rows, 0)
    taps_real, taps_imag = forward(tabs, own_block)
    band = 2 * group_rows // ranks
    in_real = lax.all_to_all(
        input_real[None].astype(jnp.bfloat16), "ctx", split_axis=1, concat_axis=0, tiled=True
    ).astype(jnp.float32)
    in_imag = lax.all_to_all(
        input_imag[None].astype(jnp.bfloat16), "ctx", split_axis=1, concat_axis=0, tiled=True
    ).astype(jnp.float32)
    filt_real = lax.all_to_all(
        taps_real[None].astype(jnp.bfloat16), "ctx", split_axis=1, concat_axis=0, tiled=True
    ).astype(jnp.float32)
    filt_imag = lax.all_to_all(
        taps_imag[None].astype(jnp.bfloat16), "ctx", split_axis=1, concat_axis=0, tiled=True
    ).astype(jnp.float32)
    band_parity = lax.dynamic_slice_in_dim(parity, own_index * band, band, 0)[None]
    prior_real = jnp.concatenate([jnp.zeros_like(filt_real[:1]), filt_real[:-1]], 0)
    prior_imag = jnp.concatenate([jnp.zeros_like(filt_imag[:1]), filt_imag[:-1]], 0)
    lag_real = filt_real + band_parity * prior_real
    lag_imag = filt_imag + band_parity * prior_imag
    order = jnp.arange(ranks, dtype=jnp.int32)[:, None, None]

    def add_lag(lag, inner):
        later = order >= lag
        moved_real = jnp.where(later, jnp.roll(in_real, lag, 0), 0.0)
        moved_imag = jnp.where(later, jnp.roll(in_imag, lag, 0), 0.0)
        this_real = lax.dynamic_index_in_dim(lag_real, lag, 0, keepdims=True)
        this_imag = lax.dynamic_index_in_dim(lag_imag, lag, 0, keepdims=True)
        out_real, out_imag = complex_mul(this_real, this_imag, moved_real, moved_imag)
        return (inner[0] + out_real, inner[1] + out_imag)

    zeros = jnp.zeros_like(in_real)
    sum_real, sum_imag = lax.fori_loop(0, ranks, add_lag, (zeros, zeros))
    total_real = lax.all_to_all(
        sum_real.astype(jnp.bfloat16), "ctx", split_axis=0, concat_axis=1, tiled=True
    ).astype(sum_real.dtype)
    total_imag = lax.all_to_all(
        sum_imag.astype(jnp.bfloat16), "ctx", split_axis=0, concat_axis=1, tiled=True
    ).astype(sum_imag.dtype)
    convolved = inverse(tabs, total_real[0], total_imag[0])
    positions = own_index * group_rows + jnp.arange(group_rows, dtype=jnp.int32)
    valid_rows = (positions < valid_length[0])[:, None]
    gated = hyena_gate.astype(jnp.float32) * (convolved + skip_weight[None, :] * mixed_float)
    hyena_out = jnp.where(valid_rows, gated, 0.0).astype(jnp.bfloat16)
    heads_here = queries.shape[1] // HD
    scale = 1.0 / math.sqrt(HD)
    query_heads = queries.reshape(group_rows, heads_here, HD)
    start_max = jnp.full((heads_here, group_rows), -1e30, jnp.float32)
    key_piece = lax.all_gather(attn_keys, "ctx", axis=0, tiled=True)
    value_piece = lax.all_gather(hyena_out, "ctx", axis=0, tiled=True)
    width = key_piece.shape[0]
    key_heads = key_piece.reshape(width, heads_here, HD)
    value_heads = value_piece.reshape(width, heads_here, HD)
    scores = (
        jnp.einsum("qhd,khd->hqk", query_heads, key_heads, preferred_element_type=jnp.float32)
        * scale
    )
    key_places = jnp.arange(width, dtype=jnp.int32)
    allowed = (key_places[None, :] <= positions[:, None]) & (key_places < valid_length[0])[None, :]
    scores = jnp.where(allowed[None], scores, -1e30)
    new_max = jnp.maximum(start_max, jnp.max(scores, axis=2))
    weights = jnp.where(allowed[None], jnp.exp(scores - new_max[:, :, None]), 0.0)
    totals = jnp.sum(weights, axis=2)
    update = jnp.einsum(
        "hqk,khd->hqd",
        weights.astype(jnp.bfloat16),
        value_heads,
        preferred_element_type=jnp.float32,
    )
    attended = (update / totals[:, :, None]).transpose(1, 0, 2).reshape(group_rows, heads_here * HD)
    squares = jnp.sum(attended * attended, axis=1)
    total_squares = lax.psum(squares, "tp")
    scaled = attended / jnp.sqrt(total_squares / DW + 1e-06)[:, None]
    attn_out = jnp.where(valid_rows, scaled, 0.0).astype(jnp.bfloat16)
    return (hyena_out, attn_out)


MESH = pl.DeviceIdType.MESH
MIX, GATE, KEY, QUERY = range(4)


def half_shift_tables(block):
    freq = np.arange(block, dtype=np.float64)[:, None] + 0.5
    place = np.arange(2 * block, dtype=np.float64)[None, :] - block
    phase = freq * place * (math.pi / block)
    ahead = np.concatenate([np.cos(phase), -np.sin(phase)], 0)
    back = ahead[:, block:].T / block

    def split(table):
        high = table.astype(jnp.bfloat16)
        low = (table - high.astype(np.float64)).astype(jnp.bfloat16)
        return high, low

    return split(ahead) + split(back)


def head_kernel(
    ranks,
    depth,
    hk,
    hv,
    gate,
    taps,
    skip,
    queries,
    keys,
    valid,
    ahead_high,
    ahead_low,
    back_high,
    back_low,
    h_out,
    a_out,
    norm_out,
    hk_v,
    hv_v,
    mix_v,
    taps_v,
    ah_v,
    al_v,
    bh_v,
    bl_v,
    got,
    lag_s,
    in_s,
    sum_high,
    sum_low,
    h_buf,
    a_buf,
    skip_v,
    length_s,
    sq_mine,
    sq_in,
    sq_sum,
    sq_got,
    local_sem,
    in_send,
    in_recv,
    h_send,
    h_recv,
    a_send,
    a_recv,
    sq_send,
    sq_recv,
    total_send,
    total_recv,
):
    me = lax.axis_index("ctx")
    plane = lax.axis_index("tp")
    group = hk_v.shape[0]
    seq = ranks * group
    block = bh_v.shape[0]
    blocks = seq // block
    per_block = block // group

    def columns(index):
        return pl.ds(pl.multiple_of(index * HD, HD), HD)

    own = columns(me)
    local = [
        pltpu.make_async_copy(src, dst, local_sem.at[i])
        for i, (src, dst) in enumerate(
            (
                (hk, hk_v),
                (hv, hv_v),
                (taps.at[:, own], taps_v.at[pl.ds(block, seq)]),
                (ahead_high, ah_v),
                (ahead_low, al_v),
                (back_high, bh_v),
                (back_low, bl_v),
                (gate.at[:, own], got.at[GATE, me]),
                (keys.at[:, own], got.at[KEY, me]),
                (queries.at[:, own], got.at[QUERY, me]),
                (skip.at[:, own], skip_v),
                (valid, length_s),
            )
        )
    ]
    for copy in local:
        copy.start()

    barrier = pltpu.get_barrier_semaphore()
    for step in range(1, ranks):
        pl.semaphore_signal(
            barrier, inc=1, device_id={"ctx": lax.rem(me + step, ranks)}, device_id_type=MESH
        )
    for step in range(1, depth):
        pl.semaphore_signal(
            barrier, inc=1, device_id={"tp": lax.rem(plane + step, depth)}, device_id_type=MESH
        )
    local[0].wait()
    local[1].wait()
    mix_v[...] = (hk_v[...].astype(jnp.float32) * hv_v[...].astype(jnp.float32)).astype(
        jnp.bfloat16
    )
    pl.semaphore_wait(barrier, ranks - 1 + depth - 1)

    sends = []
    for which, src in ((MIX, mix_v), (GATE, gate), (KEY, keys), (QUERY, queries)):
        for step in range(1, ranks):
            peer = lax.rem(me + step, ranks)
            copy = pltpu.make_async_remote_copy(
                src_ref=src.at[:, columns(peer)],
                dst_ref=got.at[which, me],
                send_sem=in_send.at[which, step],
                recv_sem=in_recv.at[which, me],
                device_id={"ctx": peer},
                device_id_type=MESH,
            )
            copy.start()
            sends.append(copy)

    def arrive(which):
        for step in range(1, ranks):
            peer = lax.rem(me + step, ranks)
            pltpu.make_async_remote_copy(
                src_ref=got.at[which, peer],
                dst_ref=got.at[which, peer],
                send_sem=in_send.at[which, step],
                recv_sem=in_recv.at[which, peer],
                device_id={"ctx": peer},
                device_id_type=MESH,
            ).wait_recv()

    got[MIX, me] = mix_v[:, own]
    taps_v[:block] = jnp.zeros((block, HD), jnp.bfloat16)
    for copy in local[2:7]:
        copy.wait()
    windows = jnp.concatenate(
        [taps_v[i * block : (i + 2) * block] for i in range(blocks)], axis=1
    )
    lag_s[...] = jnp.dot(ah_v[...], windows, preferred_element_type=jnp.float32) + jnp.dot(
        al_v[...], windows, preferred_element_type=jnp.float32
    )

    arrive(MIX)
    mixed = got[MIX].reshape(seq, HD)
    inputs = jnp.concatenate([mixed[i * block : (i + 1) * block] for i in range(blocks)], axis=1)
    in_s[...] = jnp.dot(
        ah_v[:, block:], inputs, preferred_element_type=jnp.float32
    ) + jnp.dot(al_v[:, block:], inputs, preferred_element_type=jnp.float32)

    rows_at_once = 16

    def multiply(step, carry):
        first = pl.multiple_of(step * rows_at_once, rows_at_once)
        real_rows = pl.ds(first, rows_at_once)
        imag_rows = pl.ds(block + first, rows_at_once)
        lanes = [slice(i * HD, (i + 1) * HD) for i in range(blocks)]
        in_real = [in_s[real_rows, s] for s in lanes]
        in_imag = [in_s[imag_rows, s] for s in lanes]
        lag_real = [lag_s[real_rows, s] for s in lanes]
        lag_imag = [lag_s[imag_rows, s] for s in lanes]
        for i in range(blocks):
            real = imag = None
            for j in range(i + 1):
                a, b, c, d = lag_real[i - j], lag_imag[i - j], in_real[j], in_imag[j]
                more_real = a * c - b * d
                more_imag = a * d + b * c
                real = more_real if real is None else real + more_real
                imag = more_imag if imag is None else imag + more_imag
            for rows, total in ((real_rows, real), (imag_rows, imag)):
                high = total.astype(jnp.bfloat16)
                sum_high[rows, lanes[i]] = high
                sum_low[rows, lanes[i]] = (total - high.astype(jnp.float32)).astype(jnp.bfloat16)
        return carry

    lax.fori_loop(0, block // rows_at_once, multiply, 0)
    convolved = (
        jnp.dot(bh_v[...], sum_high[...], preferred_element_type=jnp.float32)
        + jnp.dot(bl_v[...], sum_high[...], preferred_element_type=jnp.float32)
        + jnp.dot(bh_v[...], sum_low[...], preferred_element_type=jnp.float32)
    )

    local[7].wait()
    local[10].wait()
    local[11].wait()
    length = length_s[0]
    weight = skip_v[...]
    arrive(GATE)
    row_ids = lax.broadcasted_iota(jnp.int32, (group, HD), 0)
    lane_ids = lax.broadcasted_iota(jnp.int32, (group, HD), 1)
    for g in range(ranks):
        part = convolved[
            g % per_block * group : (g % per_block + 1) * group,
            g // per_block * HD : (g // per_block + 1) * HD,
        ]
        gated = got[GATE, g].astype(jnp.float32) * (
            part + weight * got[MIX, g].astype(jnp.float32)
        )
        h_buf[g] = jnp.where(row_ids + g * group < length, gated, 0.0).astype(jnp.bfloat16)

    h_local = pltpu.make_async_copy(h_buf.at[me], h_out.at[:, own], local_sem.at[0])
    h_local.start()
    for step in range(1, ranks):
        peer = lax.rem(me + step, ranks)
        copy = pltpu.make_async_remote_copy(
            src_ref=h_buf.at[peer],
            dst_ref=h_out.at[:, own],
            send_sem=h_send.at[step],
            recv_sem=h_recv.at[me],
            device_id={"ctx": peer},
            device_id_type=MESH,
        )
        copy.start()
        sends.append(copy)

    local[8].wait()
    local[9].wait()
    arrive(KEY)
    factor = math.log2(math.e) / math.sqrt(HD)

    def attended_copy(g, source):
        return pltpu.make_async_remote_copy(
            src_ref=a_buf.at[g],
            dst_ref=a_out.at[:, columns(source)],
            send_sem=a_send.at[g],
            recv_sem=a_recv.at[source],
            device_id={"ctx": g},
            device_id_type=MESH,
        )

    def attend_group(g):
        width = (g + 1) * group
        score = lax.dot_general(
            got[QUERY, g],
            got[KEY, : g + 1].reshape(width, HD),
            (((1,), (1,)), ((), ())),
            preferred_element_type=jnp.float32,
        )
        last = jnp.where(lane_ids <= row_ids, score[:, g * group :], -1e30)
        score = last if g == 0 else jnp.concatenate([score[:, : g * group], last], axis=1)
        row_max = jnp.max(score, axis=1, keepdims=True)
        raw = jnp.exp2((score - row_max) * factor)
        totals = jnp.sum(raw, axis=1, keepdims=True)
        update = jnp.dot(
            raw.astype(jnp.bfloat16),
            h_buf[: g + 1].reshape(width, HD),
            preferred_element_type=jnp.float32,
        )
        attended = update / totals
        a_buf[g] = attended.astype(jnp.bfloat16)
        sq_mine[g : g + 1] = jnp.sum((attended * attended).T, axis=0, keepdims=True)

    def attend(step, carry):
        g = lax.rem(me + ranks - step, ranks)

        @pl.when(step > 0)
        def _():
            pltpu.make_async_remote_copy(
                src_ref=got.at[QUERY, g],
                dst_ref=got.at[QUERY, g],
                send_sem=in_send.at[QUERY, g],
                recv_sem=in_recv.at[QUERY, g],
                device_id={"ctx": g},
                device_id_type=MESH,
            ).wait_recv()

        for index in range(ranks):

            @pl.when(g == index)
            def _():
                attend_group(index)

        @pl.when(step > 0)
        def _():
            attended_copy(g, me).start()

        return carry

    lax.fori_loop(0, ranks, attend, 0)
    for step in range(1, depth):
        other = lax.rem(plane + step, depth)
        copy = pltpu.make_async_remote_copy(
            src_ref=sq_mine,
            dst_ref=sq_in.at[plane],
            send_sem=sq_send.at[step],
            recv_sem=sq_recv.at[plane],
            device_id={"tp": other},
            device_id_type=MESH,
        )
        copy.start()
        sends.append(copy)
    a_local = pltpu.make_async_copy(a_buf.at[me], a_out.at[:, own], local_sem.at[1])
    a_local.start()
    slot_squares = sq_mine[...]
    for step in range(1, depth):
        other = lax.rem(plane + step, depth)
        pltpu.make_async_remote_copy(
            src_ref=sq_in.at[other],
            dst_ref=sq_in.at[other],
            send_sem=sq_send.at[step],
            recv_sem=sq_recv.at[other],
            device_id={"tp": other},
            device_id_type=MESH,
        ).wait_recv()
        slot_squares = slot_squares + sq_in[other]
    for g in range(ranks):
        sq_sum[g] = jnp.broadcast_to(slot_squares[g : g + 1], sq_sum.shape[1:])
    for step in range(1, ranks):
        peer = lax.rem(me + step, ranks)
        copy = pltpu.make_async_remote_copy(
            src_ref=sq_sum.at[peer],
            dst_ref=sq_got.at[me],
            send_sem=total_send.at[step],
            recv_sem=total_recv.at[me],
            device_id={"ctx": peer},
            device_id_type=MESH,
        )
        copy.start()
        sends.append(copy)
    total_squares = sq_sum[me]
    for step in range(1, ranks):
        peer = lax.rem(me + step, ranks)
        pltpu.make_async_remote_copy(
            src_ref=sq_sum.at[peer],
            dst_ref=sq_got.at[peer],
            send_sem=total_send.at[step],
            recv_sem=total_recv.at[peer],
            device_id={"ctx": peer},
            device_id_type=MESH,
        ).wait_recv()
        total_squares = total_squares + sq_got[peer]
    inverse_norm = lax.rsqrt(total_squares[:1] * (1.0 / (depth * ranks * HD)) + 1e-06)
    by_row = jnp.broadcast_to(inverse_norm, (group, HD)).T
    norm_out[...] = jnp.where(row_ids + me * group < length, by_row, 0.0)
    for step in range(1, ranks):
        peer = lax.rem(me + step, ranks)
        attended_copy(peer, peer).wait_recv()
    a_local.wait()
    h_local.wait()
    for step in range(1, ranks):
        peer = lax.rem(me + step, ranks)
        pltpu.make_async_remote_copy(
            src_ref=h_buf.at[peer],
            dst_ref=h_out.at[:, columns(peer)],
            send_sem=h_send.at[step],
            recv_sem=h_recv.at[peer],
            device_id={"ctx": peer},
            device_id_type=MESH,
        ).wait_recv()
        attended_copy(peer, me).wait_send()
    for copy in sends:
        copy.wait_send()


def finish_kernel(h_rows, attended, norm, h_out, a_out):
    h_out[...] = h_rows[...]
    for first in range(0, attended.shape[1], HD):
        lanes = slice(first, first + HD)
        a_out[:, lanes] = (attended[:, lanes].astype(jnp.float32) * norm[...]).astype(jnp.bfloat16)


def head_shards(ranks, depth, *arrays):
    hyena_gate, hyena_key, hyena_value, filter_taps, skip_weight, queries, attn_keys, valid = arrays
    group, channels = hyena_gate.shape
    seq = filter_taps.shape[0]
    block = 2 * group if ranks % 2 == 0 else group
    blocks = seq // block
    bf16, f32 = jnp.bfloat16, jnp.float32
    any_space = pl.BlockSpec(memory_space=pl.ANY)
    vmem = pl.BlockSpec(memory_space=pltpu.VMEM)
    hbm = pl.BlockSpec(memory_space=pltpu.HBM)
    h_rows, attended, norm = pl.pallas_call(
        functools.partial(head_kernel, ranks, depth),
        out_shape=(
            jax.ShapeDtypeStruct((group, channels), bf16),
            jax.ShapeDtypeStruct((group, channels), bf16),
            jax.ShapeDtypeStruct((group, HD), f32),
        ),
        in_specs=[hbm] * 12,
        out_specs=(any_space, any_space, vmem),
        scratch_shapes=[
            pltpu.VMEM((group, channels), bf16),
            pltpu.VMEM((group, channels), bf16),
            pltpu.VMEM((group, channels), bf16),
            pltpu.VMEM((block + seq, HD), bf16),
            pltpu.VMEM((2 * block, 2 * block), bf16),
            pltpu.VMEM((2 * block, 2 * block), bf16),
            pltpu.VMEM((block, 2 * block), bf16),
            pltpu.VMEM((block, 2 * block), bf16),
            pltpu.VMEM((4, ranks, group, HD), bf16),
            pltpu.VMEM((2 * block, blocks * HD), f32),
            pltpu.VMEM((2 * block, blocks * HD), f32),
            pltpu.VMEM((2 * block, blocks * HD), bf16),
            pltpu.VMEM((2 * block, blocks * HD), bf16),
            pltpu.VMEM((ranks, group, HD), bf16),
            pltpu.VMEM((ranks, group, HD), bf16),
            pltpu.VMEM((1, HD), f32),
            pltpu.SMEM((1,), jnp.int32),
            pltpu.VMEM((ranks, group), f32),
            pltpu.VMEM((depth, ranks, group), f32),
            pltpu.VMEM((ranks, 8, group), f32),
            pltpu.VMEM((ranks, 8, group), f32),
            pltpu.SemaphoreType.DMA((12,)),
            pltpu.SemaphoreType.DMA((4, ranks)),
            pltpu.SemaphoreType.DMA((4, ranks)),
            pltpu.SemaphoreType.DMA((ranks,)),
            pltpu.SemaphoreType.DMA((ranks,)),
            pltpu.SemaphoreType.DMA((ranks,)),
            pltpu.SemaphoreType.DMA((ranks,)),
            pltpu.SemaphoreType.DMA((depth,)),
            pltpu.SemaphoreType.DMA((depth,)),
            pltpu.SemaphoreType.DMA((ranks,)),
            pltpu.SemaphoreType.DMA((ranks,)),
        ],
        compiler_params=pltpu.CompilerParams(
            collective_id=0, has_side_effects=True, vmem_limit_bytes=62 * 1024 * 1024
        ),
    )(
        hyena_key,
        hyena_value,
        hyena_gate,
        filter_taps,
        skip_weight.reshape(1, channels),
        queries,
        attn_keys,
        valid,
        *(jnp.asarray(table) for table in half_shift_tables(block)),
    )
    return pl.pallas_call(
        finish_kernel,
        out_shape=(
            jax.ShapeDtypeStruct((group, channels), bf16),
            jax.ShapeDtypeStruct((group, channels), bf16),
        ),
        in_specs=[vmem] * 3,
        out_specs=(vmem, vmem),
    )(h_rows, attended, norm)


def solution(mesh):
    in_specs = (
        P("ctx", "tp"),
        P("ctx", "tp"),
        P("ctx", "tp"),
        P(None, "tp"),
        P("tp"),
        P("ctx", "tp"),
        P("ctx", "tp"),
        P(),
    )
    out_specs = (P("ctx", "tp"), P("ctx", "tp"))
    ranks, depth = mesh.shape["ctx"], mesh.shape["tp"]
    body = functools.partial(head_shards, ranks, depth) if DW // depth == ranks * HD else shards
    return jax.shard_map(
        body, mesh=mesh, in_specs=in_specs, out_specs=out_specs, check_vma=False
    )
```

```python
import functools
import math

import jax
import jax.numpy as jnp
import numpy as np
from jax import lax
from jax.experimental import pallas as pl
from jax.experimental.pallas import tpu as pltpu
from jax.sharding import PartitionSpec as P

HD = 128
DW = 4096


def tables(group_rows):
    doubled = 2 * group_rows
    freq = jnp.arange(doubled, dtype=jnp.int32)[:, None]
    place = jnp.arange(group_rows, dtype=jnp.int32)[None, :]
    phase = (freq * place % doubled).astype(jnp.float32) * (2.0 * math.pi / doubled)
    parity = (1 - 2 * (jnp.arange(doubled, dtype=jnp.int32) % 2)).astype(jnp.float32)[:, None]
    cosine = jnp.cos(phase)
    sine = jnp.sin(phase)
    cos_high = cosine.astype(jnp.bfloat16)
    cos_low = (cosine - cos_high.astype(jnp.float32)).astype(jnp.bfloat16)
    sin_high = sine.astype(jnp.bfloat16)
    sin_low = (sine - sin_high.astype(jnp.float32)).astype(jnp.bfloat16)
    return ((cos_high, cos_low, sin_high, sin_low, cosine, sine), parity)


def split_dot(high, low, block):
    return jnp.dot(high, block, preferred_element_type=jnp.float32) + jnp.dot(
        low, block, preferred_element_type=jnp.float32
    )


def forward(tabs, block):
    return (split_dot(tabs[0], tabs[1], block), -split_dot(tabs[2], tabs[3], block))


def inverse(tabs, real_part, imag_part):
    cosine, sine = (tabs[4], tabs[5])
    scale = 1.0 / cosine.shape[0]
    first = jnp.dot(
        cosine.T, real_part, precision=lax.Precision.HIGH, preferred_element_type=jnp.float32
    )
    second = jnp.dot(
        sine.T, imag_part, precision=lax.Precision.HIGH, preferred_element_type=jnp.float32
    )
    return (first - second) * scale


def complex_mul(left_real, left_imag, right_real, right_imag):
    return (
        left_real * right_real - left_imag * right_imag,
        left_real * right_imag + left_imag * right_real,
    )


def shards(
    hyena_gate, hyena_key, hyena_value, filter_taps, skip_weight, queries, attn_keys, valid_length
):
    group_rows = hyena_gate.shape[0]
    ranks = lax.axis_size("ctx")
    own_index = lax.axis_index("ctx")
    tabs, parity = tables(group_rows)
    mixed = (hyena_key.astype(jnp.float32) * hyena_value.astype(jnp.float32)).astype(jnp.bfloat16)
    mixed_float = mixed.astype(jnp.float32)
    input_real, input_imag = forward(tabs, mixed)
    own_block = lax.dynamic_slice_in_dim(filter_taps, own_index * group_rows, group_rows, 0)
    taps_real, taps_imag = forward(tabs, own_block)
    band = 2 * group_rows // ranks
    in_real = lax.all_to_all(
        input_real[None].astype(jnp.bfloat16), "ctx", split_axis=1, concat_axis=0, tiled=True
    ).astype(jnp.float32)
    in_imag = lax.all_to_all(
        input_imag[None].astype(jnp.bfloat16), "ctx", split_axis=1, concat_axis=0, tiled=True
    ).astype(jnp.float32)
    filt_real = lax.all_to_all(
        taps_real[None].astype(jnp.bfloat16), "ctx", split_axis=1, concat_axis=0, tiled=True
    ).astype(jnp.float32)
    filt_imag = lax.all_to_all(
        taps_imag[None].astype(jnp.bfloat16), "ctx", split_axis=1, concat_axis=0, tiled=True
    ).astype(jnp.float32)
    band_parity = lax.dynamic_slice_in_dim(parity, own_index * band, band, 0)[None]
    prior_real = jnp.concatenate([jnp.zeros_like(filt_real[:1]), filt_real[:-1]], 0)
    prior_imag = jnp.concatenate([jnp.zeros_like(filt_imag[:1]), filt_imag[:-1]], 0)
    lag_real = filt_real + band_parity * prior_real
    lag_imag = filt_imag + band_parity * prior_imag
    order = jnp.arange(ranks, dtype=jnp.int32)[:, None, None]

    def add_lag(lag, inner):
        later = order >= lag
        moved_real = jnp.where(later, jnp.roll(in_real, lag, 0), 0.0)
        moved_imag = jnp.where(later, jnp.roll(in_imag, lag, 0), 0.0)
        this_real = lax.dynamic_index_in_dim(lag_real, lag, 0, keepdims=True)
        this_imag = lax.dynamic_index_in_dim(lag_imag, lag, 0, keepdims=True)
        out_real, out_imag = complex_mul(this_real, this_imag, moved_real, moved_imag)
        return (inner[0] + out_real, inner[1] + out_imag)

    zeros = jnp.zeros_like(in_real)
    sum_real, sum_imag = lax.fori_loop(0, ranks, add_lag, (zeros, zeros))
    total_real = lax.all_to_all(
        sum_real.astype(jnp.bfloat16), "ctx", split_axis=0, concat_axis=1, tiled=True
    ).astype(sum_real.dtype)
    total_imag = lax.all_to_all(
        sum_imag.astype(jnp.bfloat16), "ctx", split_axis=0, concat_axis=1, tiled=True
    ).astype(sum_imag.dtype)
    convolved = inverse(tabs, total_real[0], total_imag[0])
    positions = own_index * group_rows + jnp.arange(group_rows, dtype=jnp.int32)
    valid_rows = (positions < valid_length[0])[:, None]
    gated = hyena_gate.astype(jnp.float32) * (convolved + skip_weight[None, :] * mixed_float)
    hyena_out = jnp.where(valid_rows, gated, 0.0).astype(jnp.bfloat16)
    heads_here = queries.shape[1] // HD
    scale = 1.0 / math.sqrt(HD)
    query_heads = queries.reshape(group_rows, heads_here, HD)
    start_max = jnp.full((heads_here, group_rows), -1e30, jnp.float32)
    key_piece = lax.all_gather(attn_keys, "ctx", axis=0, tiled=True)
    value_piece = lax.all_gather(hyena_out, "ctx", axis=0, tiled=True)
    width = key_piece.shape[0]
    key_heads = key_piece.reshape(width, heads_here, HD)
    value_heads = value_piece.reshape(width, heads_here, HD)
    scores = (
        jnp.einsum("qhd,khd->hqk", query_heads, key_heads, preferred_element_type=jnp.float32)
        * scale
    )
    key_places = jnp.arange(width, dtype=jnp.int32)
    allowed = (key_places[None, :] <= positions[:, None]) & (key_places < valid_length[0])[None, :]
    scores = jnp.where(allowed[None], scores, -1e30)
    new_max = jnp.maximum(start_max, jnp.max(scores, axis=2))
    weights = jnp.where(allowed[None], jnp.exp(scores - new_max[:, :, None]), 0.0)
    totals = jnp.sum(weights, axis=2)
    update = jnp.einsum(
        "hqk,khd->hqd",
        weights.astype(jnp.bfloat16),
        value_heads,
        preferred_element_type=jnp.float32,
    )
    attended = (update / totals[:, :, None]).transpose(1, 0, 2).reshape(group_rows, heads_here * HD)
    squares = jnp.sum(attended * attended, axis=1)
    total_squares = lax.psum(squares, "tp")
    scaled = attended / jnp.sqrt(total_squares / DW + 1e-06)[:, None]
    attn_out = jnp.where(valid_rows, scaled, 0.0).astype(jnp.bfloat16)
    return (hyena_out, attn_out)


MESH = pl.DeviceIdType.MESH
MIX, GATE, KEY, QUERY = range(4)


def half_shift_tables(block):
    freq = np.arange(block, dtype=np.float64)[:, None] + 0.5
    place = np.arange(2 * block, dtype=np.float64)[None, :] - block
    phase = freq * place * (math.pi / block)
    ahead = np.concatenate([np.cos(phase), -np.sin(phase)], 0)
    back = ahead[:, block:].T / block

    def split(table):
        high = table.astype(jnp.bfloat16)
        low = (table - high.astype(np.float64)).astype(jnp.bfloat16)
        return high, low

    return split(ahead) + split(back)


def head_kernel(
    ranks,
    depth,
    hk,
    hv,
    gate,
    taps,
    skip,
    queries,
    keys,
    valid,
    ahead_high,
    ahead_low,
    back_high,
    back_low,
    h_out,
    a_out,
    norm_out,
    hk_v,
    hv_v,
    gate_v,
    key_v,
    query_v,
    stage,
    h_t,
    taps_v,
    ah_v,
    al_v,
    bh_v,
    bl_v,
    got,
    lag_s,
    in_s,
    sum_high,
    sum_low,
    h_buf,
    a_buf,
    skip_v,
    length_s,
    sq_mine,
    sq_in,
    sq_sum,
    sq_got,
    local_sem,
    in_send,
    in_recv,
    h_send,
    h_recv,
    a_send,
    a_recv,
    sq_send,
    sq_recv,
    total_send,
    total_recv,
):
    me = lax.axis_index("ctx")
    plane = lax.axis_index("tp")
    group = hk_v.shape[0]
    seq = ranks * group
    block = bh_v.shape[0]
    blocks = seq // block
    per_block = block // group

    def columns(index):
        return pl.ds(pl.multiple_of(index * HD, HD), HD)

    own = columns(me)
    local = [
        pltpu.make_async_copy(src, dst, local_sem.at[i])
        for i, (src, dst) in enumerate(
            (
                (hk, hk_v),
                (hv, hv_v),
                (taps.at[:, own], taps_v.at[pl.ds(block, seq)]),
                (ahead_high, ah_v),
                (ahead_low, al_v),
                (back_high, bh_v),
                (back_low, bl_v),
                (gate, gate_v),
                (keys, key_v),
                (queries, query_v),
                (skip.at[:, own], skip_v),
                (valid, length_s),
            )
        )
    ]
    for copy in local:
        copy.start()

    barrier = pltpu.get_barrier_semaphore()
    for step in range(1, ranks):
        pl.semaphore_signal(
            barrier, inc=1, device_id={"ctx": lax.rem(me + step, ranks)}, device_id_type=MESH
        )
    for step in range(1, depth):
        pl.semaphore_signal(
            barrier, inc=1, device_id={"tp": lax.rem(plane + step, depth)}, device_id_type=MESH
        )
    local[0].wait()
    local[1].wait()
    for p in range(ranks):
        lanes = slice(p * HD, (p + 1) * HD)
        stage[MIX, p] = (
            hk_v[:, lanes].astype(jnp.float32) * hv_v[:, lanes].astype(jnp.float32)
        ).astype(jnp.bfloat16)
    pl.semaphore_wait(barrier, ranks - 1 + depth - 1)

    sends = []
    for which, src in ((MIX, None), (GATE, gate_v), (KEY, key_v), (QUERY, query_v)):
        if src is not None:
            local[6 + which].wait()
            for p in range(ranks):
                stage[which, p] = src[:, p * HD : (p + 1) * HD]
        for step in range(1, ranks):
            peer = lax.rem(me + step, ranks)
            copy = pltpu.make_async_remote_copy(
                src_ref=stage.at[which, peer],
                dst_ref=got.at[which, me],
                send_sem=in_send.at[which, step],
                recv_sem=in_recv.at[which, me],
                device_id={"ctx": peer},
                device_id_type=MESH,
            )
            copy.start()
            sends.append(copy)

    def arrive(which):
        for step in range(1, ranks):
            peer = lax.rem(me + step, ranks)
            pltpu.make_async_remote_copy(
                src_ref=got.at[which, peer],
                dst_ref=got.at[which, peer],
                send_sem=in_send.at[which, step],
                recv_sem=in_recv.at[which, peer],
                device_id={"ctx": peer},
                device_id_type=MESH,
            ).wait_recv()

    for which in range(4):
        got[which, me] = stage[which, me]
    taps_v[:block] = jnp.zeros((block, HD), jnp.bfloat16)
    for copy in local[2:7]:
        copy.wait()
    windows = jnp.concatenate(
        [taps_v[i * block : (i + 2) * block] for i in range(blocks)], axis=1
    )
    lag_s[...] = jnp.dot(ah_v[...], windows, preferred_element_type=jnp.float32) + jnp.dot(
        al_v[...], windows, preferred_element_type=jnp.float32
    )

    arrive(MIX)
    mixed = got[MIX].reshape(seq, HD)
    inputs = jnp.concatenate([mixed[i * block : (i + 1) * block] for i in range(blocks)], axis=1)
    in_s[...] = jnp.dot(
        ah_v[:, block:], inputs, preferred_element_type=jnp.float32
    ) + jnp.dot(al_v[:, block:], inputs, preferred_element_type=jnp.float32)

    rows_at_once = 16

    def multiply(step, carry):
        first = pl.multiple_of(step * rows_at_once, rows_at_once)
        real_rows = pl.ds(first, rows_at_once)
        imag_rows = pl.ds(block + first, rows_at_once)
        lanes = [slice(i * HD, (i + 1) * HD) for i in range(blocks)]
        in_real = [in_s[real_rows, s] for s in lanes]
        in_imag = [in_s[imag_rows, s] for s in lanes]
        lag_real = [lag_s[real_rows, s] for s in lanes]
        lag_imag = [lag_s[imag_rows, s] for s in lanes]
        for i in range(blocks):
            real = imag = None
            for j in range(i + 1):
                a, b, c, d = lag_real[i - j], lag_imag[i - j], in_real[j], in_imag[j]
                more_real = a * c - b * d
                more_imag = a * d + b * c
                real = more_real if real is None else real + more_real
                imag = more_imag if imag is None else imag + more_imag
            for rows, total in ((real_rows, real), (imag_rows, imag)):
                high = total.astype(jnp.bfloat16)
                sum_high[rows, lanes[i]] = high
                sum_low[rows, lanes[i]] = (total - high.astype(jnp.float32)).astype(jnp.bfloat16)
        return carry

    lax.fori_loop(0, block // rows_at_once, multiply, 0)
    convolved = (
        jnp.dot(bh_v[...], sum_high[...], preferred_element_type=jnp.float32)
        + jnp.dot(bl_v[...], sum_high[...], preferred_element_type=jnp.float32)
        + jnp.dot(bh_v[...], sum_low[...], preferred_element_type=jnp.float32)
    )

    local[10].wait()
    local[11].wait()
    length = length_s[0]
    weight = skip_v[...]
    arrive(GATE)
    row_ids = lax.broadcasted_iota(jnp.int32, (group, HD), 0)
    lane_ids = lax.broadcasted_iota(jnp.int32, (group, HD), 1)
    for g in range(ranks):
        part = convolved[
            g % per_block * group : (g % per_block + 1) * group,
            g // per_block * HD : (g // per_block + 1) * HD,
        ]
        gated = got[GATE, g].astype(jnp.float32) * (
            part + weight * got[MIX, g].astype(jnp.float32)
        )
        h_buf[g] = jnp.where(row_ids + g * group < length, gated, 0.0).astype(jnp.bfloat16)

    h_local = pltpu.make_async_copy(h_buf.at[me], h_out.at[:, own], local_sem.at[0])
    h_local.start()
    for step in range(1, ranks):
        peer = lax.rem(me + step, ranks)
        copy = pltpu.make_async_remote_copy(
            src_ref=h_buf.at[peer],
            dst_ref=h_out.at[:, own],
            send_sem=h_send.at[step],
            recv_sem=h_recv.at[me],
            device_id={"ctx": peer},
            device_id_type=MESH,
        )
        copy.start()
        sends.append(copy)

    for g in range(ranks):
        h_t[:, g * group : (g + 1) * group] = (
            h_buf[g].astype(jnp.float32).T.astype(jnp.bfloat16)
        )
    arrive(KEY)
    factor = math.log2(math.e) / math.sqrt(HD)

    def attended_copy(g, source):
        return pltpu.make_async_remote_copy(
            src_ref=a_buf.at[g],
            dst_ref=a_out.at[:, columns(source)],
            send_sem=a_send.at[g],
            recv_sem=a_recv.at[source],
            device_id={"ctx": g},
            device_id_type=MESH,
        )

    def attend_group(g):
        width = (g + 1) * group
        score = lax.dot_general(
            got[KEY, : g + 1].reshape(width, HD),
            got[QUERY, g],
            (((1,), (1,)), ((), ())),
            preferred_element_type=jnp.float32,
        )
        last = jnp.where(row_ids <= lane_ids, score[g * group :], -1e30)
        score = last if g == 0 else jnp.concatenate([score[: g * group], last], axis=0)
        row_max = jnp.max(score, axis=0, keepdims=True)
        raw = jnp.exp2((score - row_max) * factor)
        totals = jnp.sum(raw, axis=0, keepdims=True)
        update = jnp.dot(
            h_t[:, :width], raw.astype(jnp.bfloat16), preferred_element_type=jnp.float32
        )
        attended = update / totals
        a_buf[g] = attended.T.astype(jnp.bfloat16)
        sq_mine[g : g + 1] = jnp.sum(attended * attended, axis=0, keepdims=True)

    def attend(step, carry):
        g = lax.rem(me + ranks - step, ranks)

        @pl.when(step > 0)
        def _():
            pltpu.make_async_remote_copy(
                src_ref=got.at[QUERY, g],
                dst_ref=got.at[QUERY, g],
                send_sem=in_send.at[QUERY, g],
                recv_sem=in_recv.at[QUERY, g],
                device_id={"ctx": g},
                device_id_type=MESH,
            ).wait_recv()

        for index in range(ranks):

            @pl.when(g == index)
            def _():
                attend_group(index)

        @pl.when(step > 0)
        def _():
            attended_copy(g, me).start()

        return carry

    lax.fori_loop(0, ranks, attend, 0)
    for step in range(1, depth):
        other = lax.rem(plane + step, depth)
        copy = pltpu.make_async_remote_copy(
            src_ref=sq_mine,
            dst_ref=sq_in.at[plane],
            send_sem=sq_send.at[step],
            recv_sem=sq_recv.at[plane],
            device_id={"tp": other},
            device_id_type=MESH,
        )
        copy.start()
        sends.append(copy)
    a_local = pltpu.make_async_copy(a_buf.at[me], a_out.at[:, own], local_sem.at[1])
    a_local.start()
    slot_squares = sq_mine[...]
    for step in range(1, depth):
        other = lax.rem(plane + step, depth)
        pltpu.make_async_remote_copy(
            src_ref=sq_in.at[other],
            dst_ref=sq_in.at[other],
            send_sem=sq_send.at[step],
            recv_sem=sq_recv.at[other],
            device_id={"tp": other},
            device_id_type=MESH,
        ).wait_recv()
        slot_squares = slot_squares + sq_in[other]
    for g in range(ranks):
        sq_sum[g] = jnp.broadcast_to(slot_squares[g : g + 1], sq_sum.shape[1:])
    for step in range(1, ranks):
        peer = lax.rem(me + step, ranks)
        copy = pltpu.make_async_remote_copy(
            src_ref=sq_sum.at[peer],
            dst_ref=sq_got.at[me],
            send_sem=total_send.at[step],
            recv_sem=total_recv.at[me],
            device_id={"ctx": peer},
            device_id_type=MESH,
        )
        copy.start()
        sends.append(copy)
    total_squares = sq_sum[me]
    for step in range(1, ranks):
        peer = lax.rem(me + step, ranks)
        pltpu.make_async_remote_copy(
            src_ref=sq_sum.at[peer],
            dst_ref=sq_got.at[peer],
            send_sem=total_send.at[step],
            recv_sem=total_recv.at[peer],
            device_id={"ctx": peer},
            device_id_type=MESH,
        ).wait_recv()
        total_squares = total_squares + sq_got[peer]
    inverse_norm = lax.rsqrt(total_squares[:1] * (1.0 / (depth * ranks * HD)) + 1e-06)
    by_row = jnp.broadcast_to(inverse_norm, (group, HD)).T
    norm_out[...] = jnp.where(row_ids + me * group < length, by_row, 0.0)
    for step in range(1, ranks):
        peer = lax.rem(me + step, ranks)
        attended_copy(peer, peer).wait_recv()
    a_local.wait()
    h_local.wait()
    for step in range(1, ranks):
        peer = lax.rem(me + step, ranks)
        pltpu.make_async_remote_copy(
            src_ref=h_buf.at[peer],
            dst_ref=h_out.at[:, columns(peer)],
            send_sem=h_send.at[step],
            recv_sem=h_recv.at[peer],
            device_id={"ctx": peer},
            device_id_type=MESH,
        ).wait_recv()
        attended_copy(peer, me).wait_send()
    for copy in sends:
        copy.wait_send()


def finish_kernel(h_rows, attended, norm, h_out, a_out):
    h_out[...] = h_rows[...]
    for first in range(0, attended.shape[1], HD):
        lanes = slice(first, first + HD)
        a_out[:, lanes] = (attended[:, lanes].astype(jnp.float32) * norm[...]).astype(jnp.bfloat16)


def head_shards(ranks, depth, *arrays):
    hyena_gate, hyena_key, hyena_value, filter_taps, skip_weight, queries, attn_keys, valid = arrays
    group, channels = hyena_gate.shape
    seq = filter_taps.shape[0]
    block = 2 * group if ranks % 2 == 0 else group
    blocks = seq // block
    bf16, f32 = jnp.bfloat16, jnp.float32
    any_space = pl.BlockSpec(memory_space=pl.ANY)
    vmem = pl.BlockSpec(memory_space=pltpu.VMEM)
    hbm = pl.BlockSpec(memory_space=pltpu.HBM)
    h_rows, attended, norm = pl.pallas_call(
        functools.partial(head_kernel, ranks, depth),
        out_shape=(
            jax.ShapeDtypeStruct((group, channels), bf16),
            jax.ShapeDtypeStruct((group, channels), bf16),
            jax.ShapeDtypeStruct((group, HD), f32),
        ),
        in_specs=[hbm] * 12,
        out_specs=(any_space, any_space, vmem),
        scratch_shapes=[
            pltpu.VMEM((group, channels), bf16),
            pltpu.VMEM((group, channels), bf16),
            pltpu.VMEM((group, channels), bf16),
            pltpu.VMEM((group, channels), bf16),
            pltpu.VMEM((group, channels), bf16),
            pltpu.VMEM((4, ranks, group, HD), bf16),
            pltpu.VMEM((HD, seq), bf16),
            pltpu.VMEM((block + seq, HD), bf16),
            pltpu.VMEM((2 * block, 2 * block), bf16),
            pltpu.VMEM((2 * block, 2 * block), bf16),
            pltpu.VMEM((block, 2 * block), bf16),
            pltpu.VMEM((block, 2 * block), bf16),
            pltpu.VMEM((4, ranks, group, HD), bf16),
            pltpu.VMEM((2 * block, blocks * HD), f32),
            pltpu.VMEM((2 * block, blocks * HD), f32),
            pltpu.VMEM((2 * block, blocks * HD), bf16),
            pltpu.VMEM((2 * block, blocks * HD), bf16),
            pltpu.VMEM((ranks, group, HD), bf16),
            pltpu.VMEM((ranks, group, HD), bf16),
            pltpu.VMEM((1, HD), f32),
            pltpu.SMEM((1,), jnp.int32),
            pltpu.VMEM((ranks, group), f32),
            pltpu.VMEM((depth, ranks, group), f32),
            pltpu.VMEM((ranks, 8, group), f32),
            pltpu.VMEM((ranks, 8, group), f32),
            pltpu.SemaphoreType.DMA((12,)),
            pltpu.SemaphoreType.DMA((4, ranks)),
            pltpu.SemaphoreType.DMA((4, ranks)),
            pltpu.SemaphoreType.DMA((ranks,)),
            pltpu.SemaphoreType.DMA((ranks,)),
            pltpu.SemaphoreType.DMA((ranks,)),
            pltpu.SemaphoreType.DMA((ranks,)),
            pltpu.SemaphoreType.DMA((depth,)),
            pltpu.SemaphoreType.DMA((depth,)),
            pltpu.SemaphoreType.DMA((ranks,)),
            pltpu.SemaphoreType.DMA((ranks,)),
        ],
        compiler_params=pltpu.CompilerParams(
            collective_id=0, has_side_effects=True, vmem_limit_bytes=62 * 1024 * 1024
        ),
    )(
        hyena_key,
        hyena_value,
        hyena_gate,
        filter_taps,
        skip_weight.reshape(1, channels),
        queries,
        attn_keys,
        valid,
        *(jnp.asarray(table) for table in half_shift_tables(block)),
    )
    return pl.pallas_call(
        finish_kernel,
        out_shape=(
            jax.ShapeDtypeStruct((group, channels), bf16),
            jax.ShapeDtypeStruct((group, channels), bf16),
        ),
        in_specs=[vmem] * 3,
        out_specs=(vmem, vmem),
    )(h_rows, attended, norm)


def solution(mesh):
    in_specs = (
        P("ctx", "tp"),
        P("ctx", "tp"),
        P("ctx", "tp"),
        P(None, "tp"),
        P("tp"),
        P("ctx", "tp"),
        P("ctx", "tp"),
        P(),
    )
    out_specs = (P("ctx", "tp"), P("ctx", "tp"))
    ranks, depth = mesh.shape["ctx"], mesh.shape["tp"]
    body = functools.partial(head_shards, ranks, depth) if DW // depth == ranks * HD else shards
    return jax.shard_map(
        body, mesh=mesh, in_specs=in_specs, out_specs=out_specs, check_vma=False
    )
```

```python
import functools
import math

import jax
import jax.numpy as jnp
import numpy as np
from jax import lax
from jax.experimental import pallas as pl
from jax.experimental.pallas import tpu as pltpu
from jax.sharding import PartitionSpec as P

HD = 128
DW = 4096


def tables(group_rows):
    doubled = 2 * group_rows
    freq = jnp.arange(doubled, dtype=jnp.int32)[:, None]
    place = jnp.arange(group_rows, dtype=jnp.int32)[None, :]
    phase = (freq * place % doubled).astype(jnp.float32) * (2.0 * math.pi / doubled)
    parity = (1 - 2 * (jnp.arange(doubled, dtype=jnp.int32) % 2)).astype(jnp.float32)[:, None]
    cosine = jnp.cos(phase)
    sine = jnp.sin(phase)
    cos_high = cosine.astype(jnp.bfloat16)
    cos_low = (cosine - cos_high.astype(jnp.float32)).astype(jnp.bfloat16)
    sin_high = sine.astype(jnp.bfloat16)
    sin_low = (sine - sin_high.astype(jnp.float32)).astype(jnp.bfloat16)
    return ((cos_high, cos_low, sin_high, sin_low, cosine, sine), parity)


def split_dot(high, low, block):
    return jnp.dot(high, block, preferred_element_type=jnp.float32) + jnp.dot(
        low, block, preferred_element_type=jnp.float32
    )


def forward(tabs, block):
    return (split_dot(tabs[0], tabs[1], block), -split_dot(tabs[2], tabs[3], block))


def inverse(tabs, real_part, imag_part):
    cosine, sine = (tabs[4], tabs[5])
    scale = 1.0 / cosine.shape[0]
    first = jnp.dot(
        cosine.T, real_part, precision=lax.Precision.HIGH, preferred_element_type=jnp.float32
    )
    second = jnp.dot(
        sine.T, imag_part, precision=lax.Precision.HIGH, preferred_element_type=jnp.float32
    )
    return (first - second) * scale


def complex_mul(left_real, left_imag, right_real, right_imag):
    return (
        left_real * right_real - left_imag * right_imag,
        left_real * right_imag + left_imag * right_real,
    )


def shards(
    hyena_gate, hyena_key, hyena_value, filter_taps, skip_weight, queries, attn_keys, valid_length
):
    group_rows = hyena_gate.shape[0]
    ranks = lax.axis_size("ctx")
    own_index = lax.axis_index("ctx")
    tabs, parity = tables(group_rows)
    mixed = (hyena_key.astype(jnp.float32) * hyena_value.astype(jnp.float32)).astype(jnp.bfloat16)
    mixed_float = mixed.astype(jnp.float32)
    input_real, input_imag = forward(tabs, mixed)
    own_block = lax.dynamic_slice_in_dim(filter_taps, own_index * group_rows, group_rows, 0)
    taps_real, taps_imag = forward(tabs, own_block)
    band = 2 * group_rows // ranks
    in_real = lax.all_to_all(
        input_real[None].astype(jnp.bfloat16), "ctx", split_axis=1, concat_axis=0, tiled=True
    ).astype(jnp.float32)
    in_imag = lax.all_to_all(
        input_imag[None].astype(jnp.bfloat16), "ctx", split_axis=1, concat_axis=0, tiled=True
    ).astype(jnp.float32)
    filt_real = lax.all_to_all(
        taps_real[None].astype(jnp.bfloat16), "ctx", split_axis=1, concat_axis=0, tiled=True
    ).astype(jnp.float32)
    filt_imag = lax.all_to_all(
        taps_imag[None].astype(jnp.bfloat16), "ctx", split_axis=1, concat_axis=0, tiled=True
    ).astype(jnp.float32)
    band_parity = lax.dynamic_slice_in_dim(parity, own_index * band, band, 0)[None]
    prior_real = jnp.concatenate([jnp.zeros_like(filt_real[:1]), filt_real[:-1]], 0)
    prior_imag = jnp.concatenate([jnp.zeros_like(filt_imag[:1]), filt_imag[:-1]], 0)
    lag_real = filt_real + band_parity * prior_real
    lag_imag = filt_imag + band_parity * prior_imag
    order = jnp.arange(ranks, dtype=jnp.int32)[:, None, None]

    def add_lag(lag, inner):
        later = order >= lag
        moved_real = jnp.where(later, jnp.roll(in_real, lag, 0), 0.0)
        moved_imag = jnp.where(later, jnp.roll(in_imag, lag, 0), 0.0)
        this_real = lax.dynamic_index_in_dim(lag_real, lag, 0, keepdims=True)
        this_imag = lax.dynamic_index_in_dim(lag_imag, lag, 0, keepdims=True)
        out_real, out_imag = complex_mul(this_real, this_imag, moved_real, moved_imag)
        return (inner[0] + out_real, inner[1] + out_imag)

    zeros = jnp.zeros_like(in_real)
    sum_real, sum_imag = lax.fori_loop(0, ranks, add_lag, (zeros, zeros))
    total_real = lax.all_to_all(
        sum_real.astype(jnp.bfloat16), "ctx", split_axis=0, concat_axis=1, tiled=True
    ).astype(sum_real.dtype)
    total_imag = lax.all_to_all(
        sum_imag.astype(jnp.bfloat16), "ctx", split_axis=0, concat_axis=1, tiled=True
    ).astype(sum_imag.dtype)
    convolved = inverse(tabs, total_real[0], total_imag[0])
    positions = own_index * group_rows + jnp.arange(group_rows, dtype=jnp.int32)
    valid_rows = (positions < valid_length[0])[:, None]
    gated = hyena_gate.astype(jnp.float32) * (convolved + skip_weight[None, :] * mixed_float)
    hyena_out = jnp.where(valid_rows, gated, 0.0).astype(jnp.bfloat16)
    heads_here = queries.shape[1] // HD
    scale = 1.0 / math.sqrt(HD)
    query_heads = queries.reshape(group_rows, heads_here, HD)
    start_max = jnp.full((heads_here, group_rows), -1e30, jnp.float32)
    key_piece = lax.all_gather(attn_keys, "ctx", axis=0, tiled=True)
    value_piece = lax.all_gather(hyena_out, "ctx", axis=0, tiled=True)
    width = key_piece.shape[0]
    key_heads = key_piece.reshape(width, heads_here, HD)
    value_heads = value_piece.reshape(width, heads_here, HD)
    scores = (
        jnp.einsum("qhd,khd->hqk", query_heads, key_heads, preferred_element_type=jnp.float32)
        * scale
    )
    key_places = jnp.arange(width, dtype=jnp.int32)
    allowed = (key_places[None, :] <= positions[:, None]) & (key_places < valid_length[0])[None, :]
    scores = jnp.where(allowed[None], scores, -1e30)
    new_max = jnp.maximum(start_max, jnp.max(scores, axis=2))
    weights = jnp.where(allowed[None], jnp.exp(scores - new_max[:, :, None]), 0.0)
    totals = jnp.sum(weights, axis=2)
    update = jnp.einsum(
        "hqk,khd->hqd",
        weights.astype(jnp.bfloat16),
        value_heads,
        preferred_element_type=jnp.float32,
    )
    attended = (update / totals[:, :, None]).transpose(1, 0, 2).reshape(group_rows, heads_here * HD)
    squares = jnp.sum(attended * attended, axis=1)
    total_squares = lax.psum(squares, "tp")
    scaled = attended / jnp.sqrt(total_squares / DW + 1e-06)[:, None]
    attn_out = jnp.where(valid_rows, scaled, 0.0).astype(jnp.bfloat16)
    return (hyena_out, attn_out)


MESH = pl.DeviceIdType.MESH
MIX, GATE, KEY, QUERY = range(4)


def half_shift_tables(block):
    freq = np.arange(block, dtype=np.float64)[:, None] + 0.5
    place = np.arange(2 * block, dtype=np.float64)[None, :] - block
    phase = freq * place * (math.pi / block)
    ahead = np.concatenate([np.cos(phase), -np.sin(phase)], 0)
    back = ahead[:, block:].T / block

    def split(table):
        high = table.astype(jnp.bfloat16)
        low = (table - high.astype(np.float64)).astype(jnp.bfloat16)
        return high, low

    return split(ahead) + split(back)


def head_kernel(
    ranks,
    depth,
    hk,
    hv,
    gate,
    taps,
    skip,
    queries,
    keys,
    valid,
    ahead_high,
    ahead_low,
    back_high,
    back_low,
    h_out,
    a_out,
    norm_out,
    hk_v,
    hv_v,
    gate_v,
    key_v,
    query_v,
    stage,
    h_t,
    taps_v,
    ah_v,
    al_v,
    bh_v,
    bl_v,
    got,
    lag_s,
    in_s,
    sum_high,
    sum_low,
    h_buf,
    a_buf,
    skip_v,
    length_s,
    sq_mine,
    sq_in,
    sq_sum,
    sq_got,
    local_sem,
    in_send,
    in_recv,
    h_send,
    h_recv,
    a_send,
    a_recv,
    sq_send,
    sq_recv,
    total_send,
    total_recv,
):
    me = lax.axis_index("ctx")
    plane = lax.axis_index("tp")
    group = hk_v.shape[0]
    seq = ranks * group
    block = bh_v.shape[0]
    blocks = seq // block
    per_block = block // group

    def columns(index):
        return pl.ds(pl.multiple_of(index * HD, HD), HD)

    own = columns(me)
    local = [
        pltpu.make_async_copy(src, dst, local_sem.at[i])
        for i, (src, dst) in enumerate(
            (
                (hk, hk_v),
                (hv, hv_v),
                (taps.at[:, own], taps_v.at[pl.ds(block, seq)]),
                (ahead_high, ah_v),
                (ahead_low, al_v),
                (back_high, bh_v),
                (back_low, bl_v),
                (gate, gate_v),
                (keys, key_v),
                (queries, query_v),
                (skip.at[:, own], skip_v),
                (valid, length_s),
            )
        )
    ]
    for copy in local:
        copy.start()

    barrier = pltpu.get_barrier_semaphore()
    for step in range(1, ranks):
        pl.semaphore_signal(
            barrier, inc=1, device_id={"ctx": lax.rem(me + step, ranks)}, device_id_type=MESH
        )
    for step in range(1, depth):
        pl.semaphore_signal(
            barrier, inc=1, device_id={"tp": lax.rem(plane + step, depth)}, device_id_type=MESH
        )
    local[0].wait()
    local[1].wait()
    for p in range(ranks):
        lanes = slice(p * HD, (p + 1) * HD)
        stage[MIX, p] = (
            hk_v[:, lanes].astype(jnp.float32) * hv_v[:, lanes].astype(jnp.float32)
        ).astype(jnp.bfloat16)
    pl.semaphore_wait(barrier, ranks - 1 + depth - 1)

    sends = []

    def send(which, src):
        if src is not None:
            local[6 + which].wait()
            for p in range(ranks):
                stage[which, p] = src[:, p * HD : (p + 1) * HD]
        for step in range(1, ranks):
            peer = lax.rem(me + step, ranks)
            copy = pltpu.make_async_remote_copy(
                src_ref=stage.at[which, peer],
                dst_ref=got.at[which, me],
                send_sem=in_send.at[which, step],
                recv_sem=in_recv.at[which, me],
                device_id={"ctx": peer},
                device_id_type=MESH,
            )
            copy.start()
            sends.append(copy)
        got[which, me] = stage[which, me]

    send(MIX, None)

    def arrive(which):
        for step in range(1, ranks):
            peer = lax.rem(me + step, ranks)
            pltpu.make_async_remote_copy(
                src_ref=got.at[which, peer],
                dst_ref=got.at[which, peer],
                send_sem=in_send.at[which, step],
                recv_sem=in_recv.at[which, peer],
                device_id={"ctx": peer},
                device_id_type=MESH,
            ).wait_recv()

    taps_v[:block] = jnp.zeros((block, HD), jnp.bfloat16)
    for copy in local[2:7]:
        copy.wait()
    windows = jnp.concatenate(
        [taps_v[i * block : (i + 2) * block] for i in range(blocks)], axis=1
    )
    lag_s[...] = jnp.dot(ah_v[...], windows, preferred_element_type=jnp.float32) + jnp.dot(
        al_v[...], windows, preferred_element_type=jnp.float32
    )

    send(GATE, gate_v)
    arrive(MIX)
    send(KEY, key_v)
    send(QUERY, query_v)
    mixed = got[MIX].reshape(seq, HD)
    inputs = jnp.concatenate([mixed[i * block : (i + 1) * block] for i in range(blocks)], axis=1)
    in_s[...] = jnp.dot(
        ah_v[:, block:], inputs, preferred_element_type=jnp.float32
    ) + jnp.dot(al_v[:, block:], inputs, preferred_element_type=jnp.float32)

    rows_at_once = 16

    def multiply(step, carry):
        first = pl.multiple_of(step * rows_at_once, rows_at_once)
        real_rows = pl.ds(first, rows_at_once)
        imag_rows = pl.ds(block + first, rows_at_once)
        lanes = [slice(i * HD, (i + 1) * HD) for i in range(blocks)]
        in_real = [in_s[real_rows, s] for s in lanes]
        in_imag = [in_s[imag_rows, s] for s in lanes]
        lag_real = [lag_s[real_rows, s] for s in lanes]
        lag_imag = [lag_s[imag_rows, s] for s in lanes]
        for i in range(blocks):
            real = imag = None
            for j in range(i + 1):
                a, b, c, d = lag_real[i - j], lag_imag[i - j], in_real[j], in_imag[j]
                more_real = a * c - b * d
                more_imag = a * d + b * c
                real = more_real if real is None else real + more_real
                imag = more_imag if imag is None else imag + more_imag
            for rows, total in ((real_rows, real), (imag_rows, imag)):
                high = total.astype(jnp.bfloat16)
                sum_high[rows, lanes[i]] = high
                sum_low[rows, lanes[i]] = (total - high.astype(jnp.float32)).astype(jnp.bfloat16)
        return carry

    lax.fori_loop(0, block // rows_at_once, multiply, 0, unroll=4)
    convolved = (
        jnp.dot(bh_v[...], sum_high[...], preferred_element_type=jnp.float32)
        + jnp.dot(bl_v[...], sum_high[...], preferred_element_type=jnp.float32)
        + jnp.dot(bh_v[...], sum_low[...], preferred_element_type=jnp.float32)
    )

    local[10].wait()
    local[11].wait()
    length = length_s[0]
    weight = skip_v[...]
    arrive(GATE)
    row_ids = lax.broadcasted_iota(jnp.int32, (group, HD), 0)
    lane_ids = lax.broadcasted_iota(jnp.int32, (group, HD), 1)
    for g in range(ranks):
        part = convolved[
            g % per_block * group : (g % per_block + 1) * group,
            g // per_block * HD : (g // per_block + 1) * HD,
        ]
        gated = got[GATE, g].astype(jnp.float32) * (
            part + weight * got[MIX, g].astype(jnp.float32)
        )
        h_buf[g] = jnp.where(row_ids + g * group < length, gated, 0.0).astype(jnp.bfloat16)

    h_local = pltpu.make_async_copy(h_buf.at[me], h_out.at[:, own], local_sem.at[0])
    h_local.start()
    for step in range(1, ranks):
        peer = lax.rem(me + step, ranks)
        copy = pltpu.make_async_remote_copy(
            src_ref=h_buf.at[peer],
            dst_ref=h_out.at[:, own],
            send_sem=h_send.at[step],
            recv_sem=h_recv.at[me],
            device_id={"ctx": peer},
            device_id_type=MESH,
        )
        copy.start()
        sends.append(copy)

    for g in range(ranks):
        h_t[:, g * group : (g + 1) * group] = (
            h_buf[g].astype(jnp.float32).T.astype(jnp.bfloat16)
        )
    arrive(KEY)
    factor = math.log2(math.e) / math.sqrt(HD)

    def attended_copy(g, source):
        return pltpu.make_async_remote_copy(
            src_ref=a_buf.at[g],
            dst_ref=a_out.at[:, columns(source)],
            send_sem=a_send.at[g],
            recv_sem=a_recv.at[source],
            device_id={"ctx": g},
            device_id_type=MESH,
        )

    def attend_group(g):
        width = (g + 1) * group
        score = lax.dot_general(
            got[KEY, : g + 1].reshape(width, HD),
            got[QUERY, g],
            (((1,), (1,)), ((), ())),
            preferred_element_type=jnp.float32,
        )
        last = jnp.where(row_ids <= lane_ids, score[g * group :], -1e30)
        score = last if g == 0 else jnp.concatenate([score[: g * group], last], axis=0)
        row_max = jnp.max(score, axis=0, keepdims=True)
        raw = jnp.exp2((score - row_max) * factor)
        totals = jnp.sum(raw, axis=0, keepdims=True)
        update = jnp.dot(
            h_t[:, :width], raw.astype(jnp.bfloat16), preferred_element_type=jnp.float32
        )
        attended = update / totals
        a_buf[g] = attended.T.astype(jnp.bfloat16)
        sq_mine[g : g + 1] = jnp.sum(attended * attended, axis=0, keepdims=True)

    def attend(step, carry):
        g = lax.rem(me + ranks - step, ranks)

        @pl.when(step > 0)
        def _():
            pltpu.make_async_remote_copy(
                src_ref=got.at[QUERY, g],
                dst_ref=got.at[QUERY, g],
                send_sem=in_send.at[QUERY, g],
                recv_sem=in_recv.at[QUERY, g],
                device_id={"ctx": g},
                device_id_type=MESH,
            ).wait_recv()

        for index in range(ranks):

            @pl.when(g == index)
            def _():
                attend_group(index)

        @pl.when(step > 0)
        def _():
            attended_copy(g, me).start()

        return carry

    lax.fori_loop(0, ranks, attend, 0)
    for step in range(1, depth):
        other = lax.rem(plane + step, depth)
        copy = pltpu.make_async_remote_copy(
            src_ref=sq_mine,
            dst_ref=sq_in.at[plane],
            send_sem=sq_send.at[step],
            recv_sem=sq_recv.at[plane],
            device_id={"tp": other},
            device_id_type=MESH,
        )
        copy.start()
        sends.append(copy)
    a_local = pltpu.make_async_copy(a_buf.at[me], a_out.at[:, own], local_sem.at[1])
    a_local.start()
    slot_squares = sq_mine[...]
    for step in range(1, depth):
        other = lax.rem(plane + step, depth)
        pltpu.make_async_remote_copy(
            src_ref=sq_in.at[other],
            dst_ref=sq_in.at[other],
            send_sem=sq_send.at[step],
            recv_sem=sq_recv.at[other],
            device_id={"tp": other},
            device_id_type=MESH,
        ).wait_recv()
        slot_squares = slot_squares + sq_in[other]
    for g in range(ranks):
        sq_sum[g] = jnp.broadcast_to(slot_squares[g : g + 1], sq_sum.shape[1:])
    for step in range(1, ranks):
        peer = lax.rem(me + step, ranks)
        copy = pltpu.make_async_remote_copy(
            src_ref=sq_sum.at[peer],
            dst_ref=sq_got.at[me],
            send_sem=total_send.at[step],
            recv_sem=total_recv.at[me],
            device_id={"ctx": peer},
            device_id_type=MESH,
        )
        copy.start()
        sends.append(copy)
    total_squares = sq_sum[me]
    for step in range(1, ranks):
        peer = lax.rem(me + step, ranks)
        pltpu.make_async_remote_copy(
            src_ref=sq_sum.at[peer],
            dst_ref=sq_got.at[peer],
            send_sem=total_send.at[step],
            recv_sem=total_recv.at[peer],
            device_id={"ctx": peer},
            device_id_type=MESH,
        ).wait_recv()
        total_squares = total_squares + sq_got[peer]
    inverse_norm = lax.rsqrt(total_squares[:1] * (1.0 / (depth * ranks * HD)) + 1e-06)
    by_row = jnp.broadcast_to(inverse_norm, (group, HD)).T
    norm_out[...] = jnp.where(row_ids + me * group < length, by_row, 0.0)
    for step in range(1, ranks):
        peer = lax.rem(me + step, ranks)
        attended_copy(peer, peer).wait_recv()
    a_local.wait()
    h_local.wait()
    for step in range(1, ranks):
        peer = lax.rem(me + step, ranks)
        pltpu.make_async_remote_copy(
            src_ref=h_buf.at[peer],
            dst_ref=h_out.at[:, columns(peer)],
            send_sem=h_send.at[step],
            recv_sem=h_recv.at[peer],
            device_id={"ctx": peer},
            device_id_type=MESH,
        ).wait_recv()
        attended_copy(peer, me).wait_send()
    for copy in sends:
        copy.wait_send()


def finish_kernel(h_rows, attended, norm, h_out, a_out):
    h_out[...] = h_rows[...]
    for first in range(0, attended.shape[1], HD):
        lanes = slice(first, first + HD)
        a_out[:, lanes] = (attended[:, lanes].astype(jnp.float32) * norm[...]).astype(jnp.bfloat16)


def head_shards(ranks, depth, *arrays):
    hyena_gate, hyena_key, hyena_value, filter_taps, skip_weight, queries, attn_keys, valid = arrays
    group, channels = hyena_gate.shape
    seq = filter_taps.shape[0]
    block = 2 * group if ranks % 2 == 0 else group
    blocks = seq // block
    bf16, f32 = jnp.bfloat16, jnp.float32
    any_space = pl.BlockSpec(memory_space=pl.ANY)
    vmem = pl.BlockSpec(memory_space=pltpu.VMEM)
    hbm = pl.BlockSpec(memory_space=pltpu.HBM)
    h_rows, attended, norm = pl.pallas_call(
        functools.partial(head_kernel, ranks, depth),
        out_shape=(
            jax.ShapeDtypeStruct((group, channels), bf16),
            jax.ShapeDtypeStruct((group, channels), bf16),
            jax.ShapeDtypeStruct((group, HD), f32),
        ),
        in_specs=[hbm] * 12,
        out_specs=(any_space, any_space, vmem),
        scratch_shapes=[
            pltpu.VMEM((group, channels), bf16),
            pltpu.VMEM((group, channels), bf16),
            pltpu.VMEM((group, channels), bf16),
            pltpu.VMEM((group, channels), bf16),
            pltpu.VMEM((group, channels), bf16),
            pltpu.VMEM((4, ranks, group, HD), bf16),
            pltpu.VMEM((HD, seq), bf16),
            pltpu.VMEM((block + seq, HD), bf16),
            pltpu.VMEM((2 * block, 2 * block), bf16),
            pltpu.VMEM((2 * block, 2 * block), bf16),
            pltpu.VMEM((block, 2 * block), bf16),
            pltpu.VMEM((block, 2 * block), bf16),
            pltpu.VMEM((4, ranks, group, HD), bf16),
            pltpu.VMEM((2 * block, blocks * HD), f32),
            pltpu.VMEM((2 * block, blocks * HD), f32),
            pltpu.VMEM((2 * block, blocks * HD), bf16),
            pltpu.VMEM((2 * block, blocks * HD), bf16),
            pltpu.VMEM((ranks, group, HD), bf16),
            pltpu.VMEM((ranks, group, HD), bf16),
            pltpu.VMEM((1, HD), f32),
            pltpu.SMEM((1,), jnp.int32),
            pltpu.VMEM((ranks, group), f32),
            pltpu.VMEM((depth, ranks, group), f32),
            pltpu.VMEM((ranks, 8, group), f32),
            pltpu.VMEM((ranks, 8, group), f32),
            pltpu.SemaphoreType.DMA((12,)),
            pltpu.SemaphoreType.DMA((4, ranks)),
            pltpu.SemaphoreType.DMA((4, ranks)),
            pltpu.SemaphoreType.DMA((ranks,)),
            pltpu.SemaphoreType.DMA((ranks,)),
            pltpu.SemaphoreType.DMA((ranks,)),
            pltpu.SemaphoreType.DMA((ranks,)),
            pltpu.SemaphoreType.DMA((depth,)),
            pltpu.SemaphoreType.DMA((depth,)),
            pltpu.SemaphoreType.DMA((ranks,)),
            pltpu.SemaphoreType.DMA((ranks,)),
        ],
        compiler_params=pltpu.CompilerParams(
            collective_id=0, has_side_effects=True, vmem_limit_bytes=62 * 1024 * 1024
        ),
    )(
        hyena_key,
        hyena_value,
        hyena_gate,
        filter_taps,
        skip_weight.reshape(1, channels),
        queries,
        attn_keys,
        valid,
        *(jnp.asarray(table) for table in half_shift_tables(block)),
    )
    return pl.pallas_call(
        finish_kernel,
        out_shape=(
            jax.ShapeDtypeStruct((group, channels), bf16),
            jax.ShapeDtypeStruct((group, channels), bf16),
        ),
        in_specs=[vmem] * 3,
        out_specs=(vmem, vmem),
    )(h_rows, attended, norm)


def solution(mesh):
    in_specs = (
        P("ctx", "tp"),
        P("ctx", "tp"),
        P("ctx", "tp"),
        P(None, "tp"),
        P("tp"),
        P("ctx", "tp"),
        P("ctx", "tp"),
        P(),
    )
    out_specs = (P("ctx", "tp"), P("ctx", "tp"))
    ranks, depth = mesh.shape["ctx"], mesh.shape["tp"]
    body = functools.partial(head_shards, ranks, depth) if DW // depth == ranks * HD else shards
    return jax.shard_map(
        body, mesh=mesh, in_specs=in_specs, out_specs=out_specs, check_vma=False
    )
```

```python
import functools
import math

import jax
import jax.numpy as jnp
import numpy as np
from jax import lax
from jax.experimental import pallas as pl
from jax.experimental.pallas import tpu as pltpu
from jax.sharding import PartitionSpec as P

HD = 128
DW = 4096


def tables(group_rows):
    doubled = 2 * group_rows
    freq = jnp.arange(doubled, dtype=jnp.int32)[:, None]
    place = jnp.arange(group_rows, dtype=jnp.int32)[None, :]
    phase = (freq * place % doubled).astype(jnp.float32) * (2.0 * math.pi / doubled)
    parity = (1 - 2 * (jnp.arange(doubled, dtype=jnp.int32) % 2)).astype(jnp.float32)[:, None]
    cosine = jnp.cos(phase)
    sine = jnp.sin(phase)
    cos_high = cosine.astype(jnp.bfloat16)
    cos_low = (cosine - cos_high.astype(jnp.float32)).astype(jnp.bfloat16)
    sin_high = sine.astype(jnp.bfloat16)
    sin_low = (sine - sin_high.astype(jnp.float32)).astype(jnp.bfloat16)
    return ((cos_high, cos_low, sin_high, sin_low, cosine, sine), parity)


def split_dot(high, low, block):
    return jnp.dot(high, block, preferred_element_type=jnp.float32) + jnp.dot(
        low, block, preferred_element_type=jnp.float32
    )


def forward(tabs, block):
    return (split_dot(tabs[0], tabs[1], block), -split_dot(tabs[2], tabs[3], block))


def inverse(tabs, real_part, imag_part):
    cosine, sine = (tabs[4], tabs[5])
    scale = 1.0 / cosine.shape[0]
    first = jnp.dot(
        cosine.T, real_part, precision=lax.Precision.HIGH, preferred_element_type=jnp.float32
    )
    second = jnp.dot(
        sine.T, imag_part, precision=lax.Precision.HIGH, preferred_element_type=jnp.float32
    )
    return (first - second) * scale


def complex_mul(left_real, left_imag, right_real, right_imag):
    return (
        left_real * right_real - left_imag * right_imag,
        left_real * right_imag + left_imag * right_real,
    )


def shards(
    hyena_gate, hyena_key, hyena_value, filter_taps, skip_weight, queries, attn_keys, valid_length
):
    group_rows = hyena_gate.shape[0]
    ranks = lax.axis_size("ctx")
    own_index = lax.axis_index("ctx")
    tabs, parity = tables(group_rows)
    mixed = (hyena_key.astype(jnp.float32) * hyena_value.astype(jnp.float32)).astype(jnp.bfloat16)
    mixed_float = mixed.astype(jnp.float32)
    input_real, input_imag = forward(tabs, mixed)
    own_block = lax.dynamic_slice_in_dim(filter_taps, own_index * group_rows, group_rows, 0)
    taps_real, taps_imag = forward(tabs, own_block)
    band = 2 * group_rows // ranks
    in_real = lax.all_to_all(
        input_real[None].astype(jnp.bfloat16), "ctx", split_axis=1, concat_axis=0, tiled=True
    ).astype(jnp.float32)
    in_imag = lax.all_to_all(
        input_imag[None].astype(jnp.bfloat16), "ctx", split_axis=1, concat_axis=0, tiled=True
    ).astype(jnp.float32)
    filt_real = lax.all_to_all(
        taps_real[None].astype(jnp.bfloat16), "ctx", split_axis=1, concat_axis=0, tiled=True
    ).astype(jnp.float32)
    filt_imag = lax.all_to_all(
        taps_imag[None].astype(jnp.bfloat16), "ctx", split_axis=1, concat_axis=0, tiled=True
    ).astype(jnp.float32)
    band_parity = lax.dynamic_slice_in_dim(parity, own_index * band, band, 0)[None]
    prior_real = jnp.concatenate([jnp.zeros_like(filt_real[:1]), filt_real[:-1]], 0)
    prior_imag = jnp.concatenate([jnp.zeros_like(filt_imag[:1]), filt_imag[:-1]], 0)
    lag_real = filt_real + band_parity * prior_real
    lag_imag = filt_imag + band_parity * prior_imag
    order = jnp.arange(ranks, dtype=jnp.int32)[:, None, None]

    def add_lag(lag, inner):
        later = order >= lag
        moved_real = jnp.where(later, jnp.roll(in_real, lag, 0), 0.0)
        moved_imag = jnp.where(later, jnp.roll(in_imag, lag, 0), 0.0)
        this_real = lax.dynamic_index_in_dim(lag_real, lag, 0, keepdims=True)
        this_imag = lax.dynamic_index_in_dim(lag_imag, lag, 0, keepdims=True)
        out_real, out_imag = complex_mul(this_real, this_imag, moved_real, moved_imag)
        return (inner[0] + out_real, inner[1] + out_imag)

    zeros = jnp.zeros_like(in_real)
    sum_real, sum_imag = lax.fori_loop(0, ranks, add_lag, (zeros, zeros))
    total_real = lax.all_to_all(
        sum_real.astype(jnp.bfloat16), "ctx", split_axis=0, concat_axis=1, tiled=True
    ).astype(sum_real.dtype)
    total_imag = lax.all_to_all(
        sum_imag.astype(jnp.bfloat16), "ctx", split_axis=0, concat_axis=1, tiled=True
    ).astype(sum_imag.dtype)
    convolved = inverse(tabs, total_real[0], total_imag[0])
    positions = own_index * group_rows + jnp.arange(group_rows, dtype=jnp.int32)
    valid_rows = (positions < valid_length[0])[:, None]
    gated = hyena_gate.astype(jnp.float32) * (convolved + skip_weight[None, :] * mixed_float)
    hyena_out = jnp.where(valid_rows, gated, 0.0).astype(jnp.bfloat16)
    heads_here = queries.shape[1] // HD
    scale = 1.0 / math.sqrt(HD)
    query_heads = queries.reshape(group_rows, heads_here, HD)
    start_max = jnp.full((heads_here, group_rows), -1e30, jnp.float32)
    key_piece = lax.all_gather(attn_keys, "ctx", axis=0, tiled=True)
    value_piece = lax.all_gather(hyena_out, "ctx", axis=0, tiled=True)
    width = key_piece.shape[0]
    key_heads = key_piece.reshape(width, heads_here, HD)
    value_heads = value_piece.reshape(width, heads_here, HD)
    scores = (
        jnp.einsum("qhd,khd->hqk", query_heads, key_heads, preferred_element_type=jnp.float32)
        * scale
    )
    key_places = jnp.arange(width, dtype=jnp.int32)
    allowed = (key_places[None, :] <= positions[:, None]) & (key_places < valid_length[0])[None, :]
    scores = jnp.where(allowed[None], scores, -1e30)
    new_max = jnp.maximum(start_max, jnp.max(scores, axis=2))
    weights = jnp.where(allowed[None], jnp.exp(scores - new_max[:, :, None]), 0.0)
    totals = jnp.sum(weights, axis=2)
    update = jnp.einsum(
        "hqk,khd->hqd",
        weights.astype(jnp.bfloat16),
        value_heads,
        preferred_element_type=jnp.float32,
    )
    attended = (update / totals[:, :, None]).transpose(1, 0, 2).reshape(group_rows, heads_here * HD)
    squares = jnp.sum(attended * attended, axis=1)
    total_squares = lax.psum(squares, "tp")
    scaled = attended / jnp.sqrt(total_squares / DW + 1e-06)[:, None]
    attn_out = jnp.where(valid_rows, scaled, 0.0).astype(jnp.bfloat16)
    return (hyena_out, attn_out)


MESH = pl.DeviceIdType.MESH
MIX, GATE, KEY, QUERY = range(4)


def half_shift_tables(block):
    freq = np.arange(block, dtype=np.float64)[:, None] + 0.5
    place = np.arange(2 * block, dtype=np.float64)[None, :] - block
    phase = freq * place * (math.pi / block)
    ahead = np.concatenate([np.cos(phase), -np.sin(phase)], 0)
    back = ahead[:, block:].T / block

    def split(table):
        high = table.astype(jnp.bfloat16)
        low = (table - high.astype(np.float64)).astype(jnp.bfloat16)
        return high, low

    return split(ahead) + split(back)


def head_kernel(
    ranks,
    depth,
    hk,
    hv,
    gate,
    taps,
    skip,
    queries,
    keys,
    valid,
    ahead_high,
    ahead_low,
    back_high,
    back_low,
    h_out,
    a_out,
    norm_out,
    hk_v,
    hv_v,
    gate_v,
    key_v,
    query_v,
    stage,
    h_t,
    taps_v,
    ah_v,
    al_v,
    bh_v,
    bl_v,
    got,
    lag_s,
    in_s,
    sum_high,
    sum_low,
    h_buf,
    a_buf,
    skip_v,
    length_s,
    sq_mine,
    sq_in,
    sq_sum,
    sq_got,
    local_sem,
    in_send,
    in_recv,
    h_send,
    h_recv,
    a_send,
    a_recv,
    sq_send,
    sq_recv,
    total_send,
    total_recv,
):
    me = lax.axis_index("ctx")
    plane = lax.axis_index("tp")
    group = hk_v.shape[0]
    seq = ranks * group
    block = bh_v.shape[0]
    blocks = seq // block
    per_block = block // group

    def columns(index):
        return pl.ds(pl.multiple_of(index * HD, HD), HD)

    core, across, along = lax.rem(me, 2), lax.rem(lax.div(me, 2), 2), lax.div(me, 4)

    def partner(step):
        if ranks != 8:
            return lax.rem(me + step, ranks)
        step = jnp.asarray(step, jnp.int32)
        kind = lax.rem(step, 4)
        low, high = lax.rem(kind, 2), lax.div(kind, 2)
        dx = low * (1 - core) + high * core
        dy = high * (1 - core) + low * core
        chip = lax.rem(along + dy, 2) * 2 + lax.rem(across + dx, 2)
        return chip * 2 + lax.rem(core + lax.div(step, 4), 2)

    own = columns(me)
    local = [
        pltpu.make_async_copy(src, dst, local_sem.at[i])
        for i, (src, dst) in enumerate(
            (
                (hk, hk_v),
                (hv, hv_v),
                (taps.at[:, own], taps_v.at[pl.ds(block, seq)]),
                (ahead_high, ah_v),
                (ahead_low, al_v),
                (back_high, bh_v),
                (back_low, bl_v),
                (gate, gate_v),
                (keys, key_v),
                (queries, query_v),
                (skip.at[:, own], skip_v),
                (valid, length_s),
            )
        )
    ]
    for copy in local:
        copy.start()

    barrier = pltpu.get_barrier_semaphore()
    for step in range(1, ranks):
        pl.semaphore_signal(
            barrier, inc=1, device_id={"ctx": partner(step)}, device_id_type=MESH
        )
    for step in range(1, depth):
        pl.semaphore_signal(
            barrier, inc=1, device_id={"tp": lax.rem(plane + step, depth)}, device_id_type=MESH
        )
    local[0].wait()
    local[1].wait()
    for p in range(ranks):
        lanes = slice(p * HD, (p + 1) * HD)
        stage[MIX, p] = (
            hk_v[:, lanes].astype(jnp.float32) * hv_v[:, lanes].astype(jnp.float32)
        ).astype(jnp.bfloat16)
    pl.semaphore_wait(barrier, ranks - 1 + depth - 1)

    sends = []

    def send(which, src):
        if src is not None:
            local[6 + which].wait()
            for p in range(ranks):
                stage[which, p] = src[:, p * HD : (p + 1) * HD]
        for step in range(1, ranks):
            peer = partner(step)
            copy = pltpu.make_async_remote_copy(
                src_ref=stage.at[which, peer],
                dst_ref=got.at[which, me],
                send_sem=in_send.at[which, step],
                recv_sem=in_recv.at[which, me],
                device_id={"ctx": peer},
                device_id_type=MESH,
            )
            copy.start()
            sends.append(copy)
        got[which, me] = stage[which, me]

    send(MIX, None)

    def arrive(which):
        for step in range(1, ranks):
            peer = partner(step)
            pltpu.make_async_remote_copy(
                src_ref=got.at[which, peer],
                dst_ref=got.at[which, peer],
                send_sem=in_send.at[which, step],
                recv_sem=in_recv.at[which, peer],
                device_id={"ctx": peer},
                device_id_type=MESH,
            ).wait_recv()

    taps_v[:block] = jnp.zeros((block, HD), jnp.bfloat16)
    for copy in local[2:7]:
        copy.wait()
    windows = jnp.concatenate(
        [taps_v[i * block : (i + 2) * block] for i in range(blocks)], axis=1
    )
    lag_s[...] = jnp.dot(ah_v[...], windows, preferred_element_type=jnp.float32) + jnp.dot(
        al_v[...], windows, preferred_element_type=jnp.float32
    )

    send(GATE, gate_v)
    arrive(MIX)
    send(KEY, key_v)
    send(QUERY, query_v)
    mixed = got[MIX].reshape(seq, HD)
    inputs = jnp.concatenate([mixed[i * block : (i + 1) * block] for i in range(blocks)], axis=1)
    in_s[...] = jnp.dot(
        ah_v[:, block:], inputs, preferred_element_type=jnp.float32
    ) + jnp.dot(al_v[:, block:], inputs, preferred_element_type=jnp.float32)

    rows_at_once = 16

    def multiply(step, carry):
        first = pl.multiple_of(step * rows_at_once, rows_at_once)
        real_rows = pl.ds(first, rows_at_once)
        imag_rows = pl.ds(block + first, rows_at_once)
        lanes = [slice(i * HD, (i + 1) * HD) for i in range(blocks)]
        in_real = [in_s[real_rows, s] for s in lanes]
        in_imag = [in_s[imag_rows, s] for s in lanes]
        lag_real = [lag_s[real_rows, s] for s in lanes]
        lag_imag = [lag_s[imag_rows, s] for s in lanes]
        for i in range(blocks):
            real = imag = None
            for j in range(i + 1):
                a, b, c, d = lag_real[i - j], lag_imag[i - j], in_real[j], in_imag[j]
                more_real = a * c - b * d
                more_imag = a * d + b * c
                real = more_real if real is None else real + more_real
                imag = more_imag if imag is None else imag + more_imag
            for rows, total in ((real_rows, real), (imag_rows, imag)):
                high = total.astype(jnp.bfloat16)
                sum_high[rows, lanes[i]] = high
                sum_low[rows, lanes[i]] = (total - high.astype(jnp.float32)).astype(jnp.bfloat16)
        return carry

    lax.fori_loop(0, block // rows_at_once, multiply, 0, unroll=4)
    convolved = (
        jnp.dot(bh_v[...], sum_high[...], preferred_element_type=jnp.float32)
        + jnp.dot(bl_v[...], sum_high[...], preferred_element_type=jnp.float32)
        + jnp.dot(bh_v[...], sum_low[...], preferred_element_type=jnp.float32)
    )

    local[10].wait()
    local[11].wait()
    length = length_s[0]
    weight = skip_v[...]
    arrive(GATE)
    row_ids = lax.broadcasted_iota(jnp.int32, (group, HD), 0)
    lane_ids = lax.broadcasted_iota(jnp.int32, (group, HD), 1)
    for g in range(ranks):
        part = convolved[
            g % per_block * group : (g % per_block + 1) * group,
            g // per_block * HD : (g // per_block + 1) * HD,
        ]
        gated = got[GATE, g].astype(jnp.float32) * (
            part + weight * got[MIX, g].astype(jnp.float32)
        )
        h_buf[g] = jnp.where(row_ids + g * group < length, gated, 0.0).astype(jnp.bfloat16)

    h_local = pltpu.make_async_copy(h_buf.at[me], h_out.at[:, own], local_sem.at[0])
    h_local.start()
    for step in range(1, ranks):
        peer = partner(step)
        copy = pltpu.make_async_remote_copy(
            src_ref=h_buf.at[peer],
            dst_ref=h_out.at[:, own],
            send_sem=h_send.at[step],
            recv_sem=h_recv.at[me],
            device_id={"ctx": peer},
            device_id_type=MESH,
        )
        copy.start()
        sends.append(copy)

    for g in range(ranks):
        h_t[:, g * group : (g + 1) * group] = (
            h_buf[g].astype(jnp.float32).T.astype(jnp.bfloat16)
        )
    arrive(KEY)
    factor = math.log2(math.e) / math.sqrt(HD)

    def attended_copy(g, source):
        return pltpu.make_async_remote_copy(
            src_ref=a_buf.at[g],
            dst_ref=a_out.at[:, columns(source)],
            send_sem=a_send.at[g],
            recv_sem=a_recv.at[source],
            device_id={"ctx": g},
            device_id_type=MESH,
        )

    def attend_group(g):
        width = (g + 1) * group
        score = lax.dot_general(
            got[KEY, : g + 1].reshape(width, HD),
            got[QUERY, g],
            (((1,), (1,)), ((), ())),
            preferred_element_type=jnp.float32,
        )
        last = jnp.where(row_ids <= lane_ids, score[g * group :], -1e30)
        score = last if g == 0 else jnp.concatenate([score[: g * group], last], axis=0)
        row_max = jnp.max(score, axis=0, keepdims=True)
        raw = jnp.exp2((score - row_max) * factor)
        totals = jnp.sum(raw, axis=0, keepdims=True)
        update = jnp.dot(
            h_t[:, :width], raw.astype(jnp.bfloat16), preferred_element_type=jnp.float32
        )
        attended = update / totals
        a_buf[g] = attended.T.astype(jnp.bfloat16)
        sq_mine[g : g + 1] = jnp.sum(attended * attended, axis=0, keepdims=True)

    def attend(step, carry):
        g = partner(step)

        @pl.when(step > 0)
        def _():
            pltpu.make_async_remote_copy(
                src_ref=got.at[QUERY, g],
                dst_ref=got.at[QUERY, g],
                send_sem=in_send.at[QUERY, g],
                recv_sem=in_recv.at[QUERY, g],
                device_id={"ctx": g},
                device_id_type=MESH,
            ).wait_recv()

        for index in range(ranks):

            @pl.when(g == index)
            def _():
                attend_group(index)

        @pl.when(step > 0)
        def _():
            attended_copy(g, me).start()

        return carry

    lax.fori_loop(0, ranks, attend, 0)
    for step in range(1, depth):
        other = lax.rem(plane + step, depth)
        copy = pltpu.make_async_remote_copy(
            src_ref=sq_mine,
            dst_ref=sq_in.at[plane],
            send_sem=sq_send.at[step],
            recv_sem=sq_recv.at[plane],
            device_id={"tp": other},
            device_id_type=MESH,
        )
        copy.start()
        sends.append(copy)
    a_local = pltpu.make_async_copy(a_buf.at[me], a_out.at[:, own], local_sem.at[1])
    a_local.start()
    slot_squares = sq_mine[...]
    for step in range(1, depth):
        other = lax.rem(plane + step, depth)
        pltpu.make_async_remote_copy(
            src_ref=sq_in.at[other],
            dst_ref=sq_in.at[other],
            send_sem=sq_send.at[step],
            recv_sem=sq_recv.at[other],
            device_id={"tp": other},
            device_id_type=MESH,
        ).wait_recv()
        slot_squares = slot_squares + sq_in[other]
    for g in range(ranks):
        sq_sum[g] = jnp.broadcast_to(slot_squares[g : g + 1], sq_sum.shape[1:])
    for step in range(1, ranks):
        peer = partner(step)
        copy = pltpu.make_async_remote_copy(
            src_ref=sq_sum.at[peer],
            dst_ref=sq_got.at[me],
            send_sem=total_send.at[step],
            recv_sem=total_recv.at[me],
            device_id={"ctx": peer},
            device_id_type=MESH,
        )
        copy.start()
        sends.append(copy)
    total_squares = sq_sum[me]
    for step in range(1, ranks):
        peer = partner(step)
        pltpu.make_async_remote_copy(
            src_ref=sq_sum.at[peer],
            dst_ref=sq_got.at[peer],
            send_sem=total_send.at[step],
            recv_sem=total_recv.at[peer],
            device_id={"ctx": peer},
            device_id_type=MESH,
        ).wait_recv()
        total_squares = total_squares + sq_got[peer]
    inverse_norm = lax.rsqrt(total_squares[:1] * (1.0 / (depth * ranks * HD)) + 1e-06)
    by_row = jnp.broadcast_to(inverse_norm, (group, HD)).T
    norm_out[...] = jnp.where(row_ids + me * group < length, by_row, 0.0)
    for step in range(1, ranks):
        peer = partner(step)
        attended_copy(peer, peer).wait_recv()
    a_local.wait()
    h_local.wait()
    for step in range(1, ranks):
        peer = partner(step)
        pltpu.make_async_remote_copy(
            src_ref=h_buf.at[peer],
            dst_ref=h_out.at[:, columns(peer)],
            send_sem=h_send.at[step],
            recv_sem=h_recv.at[peer],
            device_id={"ctx": peer},
            device_id_type=MESH,
        ).wait_recv()
        attended_copy(peer, me).wait_send()
    for copy in sends:
        copy.wait_send()


def finish_kernel(h_rows, attended, norm, h_out, a_out):
    h_out[...] = h_rows[...]
    for first in range(0, attended.shape[1], HD):
        lanes = slice(first, first + HD)
        a_out[:, lanes] = (attended[:, lanes].astype(jnp.float32) * norm[...]).astype(jnp.bfloat16)


def head_shards(ranks, depth, *arrays):
    hyena_gate, hyena_key, hyena_value, filter_taps, skip_weight, queries, attn_keys, valid = arrays
    group, channels = hyena_gate.shape
    seq = filter_taps.shape[0]
    block = 2 * group if ranks % 2 == 0 else group
    blocks = seq // block
    bf16, f32 = jnp.bfloat16, jnp.float32
    any_space = pl.BlockSpec(memory_space=pl.ANY)
    vmem = pl.BlockSpec(memory_space=pltpu.VMEM)
    hbm = pl.BlockSpec(memory_space=pltpu.HBM)
    h_rows, attended, norm = pl.pallas_call(
        functools.partial(head_kernel, ranks, depth),
        out_shape=(
            jax.ShapeDtypeStruct((group, channels), bf16),
            jax.ShapeDtypeStruct((group, channels), bf16),
            jax.ShapeDtypeStruct((group, HD), f32),
        ),
        in_specs=[hbm] * 12,
        out_specs=(any_space, any_space, vmem),
        scratch_shapes=[
            pltpu.VMEM((group, channels), bf16),
            pltpu.VMEM((group, channels), bf16),
            pltpu.VMEM((group, channels), bf16),
            pltpu.VMEM((group, channels), bf16),
            pltpu.VMEM((group, channels), bf16),
            pltpu.VMEM((4, ranks, group, HD), bf16),
            pltpu.VMEM((HD, seq), bf16),
            pltpu.VMEM((block + seq, HD), bf16),
            pltpu.VMEM((2 * block, 2 * block), bf16),
            pltpu.VMEM((2 * block, 2 * block), bf16),
            pltpu.VMEM((block, 2 * block), bf16),
            pltpu.VMEM((block, 2 * block), bf16),
            pltpu.VMEM((4, ranks, group, HD), bf16),
            pltpu.VMEM((2 * block, blocks * HD), f32),
            pltpu.VMEM((2 * block, blocks * HD), f32),
            pltpu.VMEM((2 * block, blocks * HD), bf16),
            pltpu.VMEM((2 * block, blocks * HD), bf16),
            pltpu.VMEM((ranks, group, HD), bf16),
            pltpu.VMEM((ranks, group, HD), bf16),
            pltpu.VMEM((1, HD), f32),
            pltpu.SMEM((1,), jnp.int32),
            pltpu.VMEM((ranks, group), f32),
            pltpu.VMEM((depth, ranks, group), f32),
            pltpu.VMEM((ranks, 8, group), f32),
            pltpu.VMEM((ranks, 8, group), f32),
            pltpu.SemaphoreType.DMA((12,)),
            pltpu.SemaphoreType.DMA((4, ranks)),
            pltpu.SemaphoreType.DMA((4, ranks)),
            pltpu.SemaphoreType.DMA((ranks,)),
            pltpu.SemaphoreType.DMA((ranks,)),
            pltpu.SemaphoreType.DMA((ranks,)),
            pltpu.SemaphoreType.DMA((ranks,)),
            pltpu.SemaphoreType.DMA((depth,)),
            pltpu.SemaphoreType.DMA((depth,)),
            pltpu.SemaphoreType.DMA((ranks,)),
            pltpu.SemaphoreType.DMA((ranks,)),
        ],
        compiler_params=pltpu.CompilerParams(
            collective_id=0, has_side_effects=True, vmem_limit_bytes=62 * 1024 * 1024
        ),
    )(
        hyena_key,
        hyena_value,
        hyena_gate,
        filter_taps,
        skip_weight.reshape(1, channels),
        queries,
        attn_keys,
        valid,
        *(jnp.asarray(table) for table in half_shift_tables(block)),
    )
    return pl.pallas_call(
        finish_kernel,
        out_shape=(
            jax.ShapeDtypeStruct((group, channels), bf16),
            jax.ShapeDtypeStruct((group, channels), bf16),
        ),
        in_specs=[vmem] * 3,
        out_specs=(vmem, vmem),
    )(h_rows, attended, norm)


def solution(mesh):
    in_specs = (
        P("ctx", "tp"),
        P("ctx", "tp"),
        P("ctx", "tp"),
        P(None, "tp"),
        P("tp"),
        P("ctx", "tp"),
        P("ctx", "tp"),
        P(),
    )
    out_specs = (P("ctx", "tp"), P("ctx", "tp"))
    ranks, depth = mesh.shape["ctx"], mesh.shape["tp"]
    body = functools.partial(head_shards, ranks, depth) if DW // depth == ranks * HD else shards
    return jax.shard_map(
        body, mesh=mesh, in_specs=in_specs, out_specs=out_specs, check_vma=False
    )
```

```python
import functools
import math

import jax
import jax.numpy as jnp
import numpy as np
from jax import lax
from jax.experimental import pallas as pl
from jax.experimental.pallas import tpu as pltpu
from jax.sharding import PartitionSpec as P

HD = 128
DW = 4096


def tables(group_rows):
    doubled = 2 * group_rows
    freq = jnp.arange(doubled, dtype=jnp.int32)[:, None]
    place = jnp.arange(group_rows, dtype=jnp.int32)[None, :]
    phase = (freq * place % doubled).astype(jnp.float32) * (2.0 * math.pi / doubled)
    parity = (1 - 2 * (jnp.arange(doubled, dtype=jnp.int32) % 2)).astype(jnp.float32)[:, None]
    cosine = jnp.cos(phase)
    sine = jnp.sin(phase)
    cos_high = cosine.astype(jnp.bfloat16)
    cos_low = (cosine - cos_high.astype(jnp.float32)).astype(jnp.bfloat16)
    sin_high = sine.astype(jnp.bfloat16)
    sin_low = (sine - sin_high.astype(jnp.float32)).astype(jnp.bfloat16)
    return ((cos_high, cos_low, sin_high, sin_low, cosine, sine), parity)


def split_dot(high, low, block):
    return jnp.dot(high, block, preferred_element_type=jnp.float32) + jnp.dot(
        low, block, preferred_element_type=jnp.float32
    )


def forward(tabs, block):
    return (split_dot(tabs[0], tabs[1], block), -split_dot(tabs[2], tabs[3], block))


def inverse(tabs, real_part, imag_part):
    cosine, sine = (tabs[4], tabs[5])
    scale = 1.0 / cosine.shape[0]
    first = jnp.dot(
        cosine.T, real_part, precision=lax.Precision.HIGH, preferred_element_type=jnp.float32
    )
    second = jnp.dot(
        sine.T, imag_part, precision=lax.Precision.HIGH, preferred_element_type=jnp.float32
    )
    return (first - second) * scale


def complex_mul(left_real, left_imag, right_real, right_imag):
    return (
        left_real * right_real - left_imag * right_imag,
        left_real * right_imag + left_imag * right_real,
    )


def shards(
    hyena_gate, hyena_key, hyena_value, filter_taps, skip_weight, queries, attn_keys, valid_length
):
    group_rows = hyena_gate.shape[0]
    ranks = lax.axis_size("ctx")
    own_index = lax.axis_index("ctx")
    tabs, parity = tables(group_rows)
    mixed = (hyena_key.astype(jnp.float32) * hyena_value.astype(jnp.float32)).astype(jnp.bfloat16)
    mixed_float = mixed.astype(jnp.float32)
    input_real, input_imag = forward(tabs, mixed)
    own_block = lax.dynamic_slice_in_dim(filter_taps, own_index * group_rows, group_rows, 0)
    taps_real, taps_imag = forward(tabs, own_block)
    band = 2 * group_rows // ranks
    in_real = lax.all_to_all(
        input_real[None].astype(jnp.bfloat16), "ctx", split_axis=1, concat_axis=0, tiled=True
    ).astype(jnp.float32)
    in_imag = lax.all_to_all(
        input_imag[None].astype(jnp.bfloat16), "ctx", split_axis=1, concat_axis=0, tiled=True
    ).astype(jnp.float32)
    filt_real = lax.all_to_all(
        taps_real[None].astype(jnp.bfloat16), "ctx", split_axis=1, concat_axis=0, tiled=True
    ).astype(jnp.float32)
    filt_imag = lax.all_to_all(
        taps_imag[None].astype(jnp.bfloat16), "ctx", split_axis=1, concat_axis=0, tiled=True
    ).astype(jnp.float32)
    band_parity = lax.dynamic_slice_in_dim(parity, own_index * band, band, 0)[None]
    prior_real = jnp.concatenate([jnp.zeros_like(filt_real[:1]), filt_real[:-1]], 0)
    prior_imag = jnp.concatenate([jnp.zeros_like(filt_imag[:1]), filt_imag[:-1]], 0)
    lag_real = filt_real + band_parity * prior_real
    lag_imag = filt_imag + band_parity * prior_imag
    order = jnp.arange(ranks, dtype=jnp.int32)[:, None, None]

    def add_lag(lag, inner):
        later = order >= lag
        moved_real = jnp.where(later, jnp.roll(in_real, lag, 0), 0.0)
        moved_imag = jnp.where(later, jnp.roll(in_imag, lag, 0), 0.0)
        this_real = lax.dynamic_index_in_dim(lag_real, lag, 0, keepdims=True)
        this_imag = lax.dynamic_index_in_dim(lag_imag, lag, 0, keepdims=True)
        out_real, out_imag = complex_mul(this_real, this_imag, moved_real, moved_imag)
        return (inner[0] + out_real, inner[1] + out_imag)

    zeros = jnp.zeros_like(in_real)
    sum_real, sum_imag = lax.fori_loop(0, ranks, add_lag, (zeros, zeros))
    total_real = lax.all_to_all(
        sum_real.astype(jnp.bfloat16), "ctx", split_axis=0, concat_axis=1, tiled=True
    ).astype(sum_real.dtype)
    total_imag = lax.all_to_all(
        sum_imag.astype(jnp.bfloat16), "ctx", split_axis=0, concat_axis=1, tiled=True
    ).astype(sum_imag.dtype)
    convolved = inverse(tabs, total_real[0], total_imag[0])
    positions = own_index * group_rows + jnp.arange(group_rows, dtype=jnp.int32)
    valid_rows = (positions < valid_length[0])[:, None]
    gated = hyena_gate.astype(jnp.float32) * (convolved + skip_weight[None, :] * mixed_float)
    hyena_out = jnp.where(valid_rows, gated, 0.0).astype(jnp.bfloat16)
    heads_here = queries.shape[1] // HD
    scale = 1.0 / math.sqrt(HD)
    query_heads = queries.reshape(group_rows, heads_here, HD)
    start_max = jnp.full((heads_here, group_rows), -1e30, jnp.float32)
    key_piece = lax.all_gather(attn_keys, "ctx", axis=0, tiled=True)
    value_piece = lax.all_gather(hyena_out, "ctx", axis=0, tiled=True)
    width = key_piece.shape[0]
    key_heads = key_piece.reshape(width, heads_here, HD)
    value_heads = value_piece.reshape(width, heads_here, HD)
    scores = (
        jnp.einsum("qhd,khd->hqk", query_heads, key_heads, preferred_element_type=jnp.float32)
        * scale
    )
    key_places = jnp.arange(width, dtype=jnp.int32)
    allowed = (key_places[None, :] <= positions[:, None]) & (key_places < valid_length[0])[None, :]
    scores = jnp.where(allowed[None], scores, -1e30)
    new_max = jnp.maximum(start_max, jnp.max(scores, axis=2))
    weights = jnp.where(allowed[None], jnp.exp(scores - new_max[:, :, None]), 0.0)
    totals = jnp.sum(weights, axis=2)
    update = jnp.einsum(
        "hqk,khd->hqd",
        weights.astype(jnp.bfloat16),
        value_heads,
        preferred_element_type=jnp.float32,
    )
    attended = (update / totals[:, :, None]).transpose(1, 0, 2).reshape(group_rows, heads_here * HD)
    squares = jnp.sum(attended * attended, axis=1)
    total_squares = lax.psum(squares, "tp")
    scaled = attended / jnp.sqrt(total_squares / DW + 1e-06)[:, None]
    attn_out = jnp.where(valid_rows, scaled, 0.0).astype(jnp.bfloat16)
    return (hyena_out, attn_out)


MESH = pl.DeviceIdType.MESH
EARLY, LATE = range(2)


def half_shift_tables(block):
    freq = np.arange(block, dtype=np.float64)[:, None] + 0.5
    place = np.arange(2 * block, dtype=np.float64)[None, :] - block
    phase = freq * place * (math.pi / block)
    ahead = np.concatenate([np.cos(phase), -np.sin(phase)], 0)
    back = ahead[:, block:].T / block

    def split(table):
        high = table.astype(jnp.bfloat16)
        low = (table - high.astype(np.float64)).astype(jnp.bfloat16)
        return high, low

    return split(ahead) + split(back)


def head_kernel(
    ranks,
    depth,
    hk,
    hv,
    gate,
    taps,
    skip,
    queries,
    keys,
    valid,
    ahead_high,
    ahead_low,
    back_high,
    back_low,
    h_out,
    a_out,
    norm_out,
    hk_v,
    hv_v,
    gate_v,
    key_v,
    query_v,
    stage,
    h_t,
    taps_v,
    ah_v,
    al_v,
    bh_v,
    bl_v,
    got,
    lag_s,
    in_s,
    sum_high,
    sum_low,
    h_buf,
    a_buf,
    skip_v,
    length_s,
    sq_mine,
    sq_in,
    sq_sum,
    sq_got,
    local_sem,
    in_send,
    in_recv,
    h_send,
    h_recv,
    a_send,
    a_recv,
    sq_send,
    sq_recv,
    total_send,
    total_recv,
):
    me = lax.axis_index("ctx")
    plane = lax.axis_index("tp")
    group = hk_v.shape[0]
    seq = ranks * group
    block = bh_v.shape[0]
    blocks = seq // block
    per_block = block // group

    def columns(index):
        return pl.ds(pl.multiple_of(index * HD, HD), HD)

    own = columns(me)
    local = [
        pltpu.make_async_copy(src, dst, local_sem.at[i])
        for i, (src, dst) in enumerate(
            (
                (hk, hk_v),
                (hv, hv_v),
                (taps.at[:, own], taps_v.at[pl.ds(block, seq)]),
                (ahead_high, ah_v),
                (ahead_low, al_v),
                (back_high, bh_v),
                (back_low, bl_v),
                (gate, gate_v),
                (keys, key_v),
                (queries, query_v),
                (skip.at[:, own], skip_v),
                (valid, length_s),
            )
        )
    ]
    for copy in local:
        copy.start()

    barrier = pltpu.get_barrier_semaphore()
    for step in range(1, ranks):
        pl.semaphore_signal(
            barrier, inc=1, device_id={"ctx": lax.rem(me + step, ranks)}, device_id_type=MESH
        )
    for step in range(1, depth):
        pl.semaphore_signal(
            barrier, inc=1, device_id={"tp": lax.rem(plane + step, depth)}, device_id_type=MESH
        )
    local[0].wait()
    local[1].wait()
    for p in range(ranks):
        lanes = slice(p * HD, (p + 1) * HD)
        stage[EARLY, p, 0] = (
            hk_v[:, lanes].astype(jnp.float32) * hv_v[:, lanes].astype(jnp.float32)
        ).astype(jnp.bfloat16)
    local[7].wait()
    for p in range(ranks):
        stage[EARLY, p, 1] = gate_v[:, p * HD : (p + 1) * HD]
    pl.semaphore_wait(barrier, ranks - 1 + depth - 1)

    sends = []

    def lay_out(bundle, which, src, ready):
        ready.wait()
        for p in range(ranks):
            stage[bundle, p, which] = src[:, p * HD : (p + 1) * HD]

    def send(bundle):
        for step in range(1, ranks):
            peer = lax.rem(me + step, ranks)
            pltpu.make_async_remote_copy(
                src_ref=stage.at[bundle, peer],
                dst_ref=got.at[bundle, me],
                send_sem=in_send.at[bundle],
                recv_sem=in_recv.at[bundle],
                device_id={"ctx": peer},
                device_id_type=MESH,
            ).start()

    def all_of(src, dst, send_sem, recv_sem):
        return pltpu.make_async_remote_copy(
            src_ref=src,
            dst_ref=dst,
            send_sem=send_sem,
            recv_sem=recv_sem,
            device_id={"ctx": lax.rem(me + 1, ranks)},
            device_id_type=MESH,
        )

    others = pl.ds(0, ranks - 1)

    def bundle_copies(bundle):
        return all_of(
            stage.at[bundle, others], got.at[bundle, others], in_send.at[bundle], in_recv.at[bundle]
        )

    send(EARLY)
    lay_out(LATE, 0, key_v, local[8])
    lay_out(LATE, 1, query_v, local[9])
    send(LATE)
    for bundle in (EARLY, LATE):
        got[bundle, me] = stage[bundle, me]
    taps_v[:block] = jnp.zeros((block, HD), jnp.bfloat16)
    for copy in local[2:7]:
        copy.wait()
    windows = jnp.concatenate(
        [taps_v[i * block : (i + 2) * block] for i in range(blocks)], axis=1
    )
    lag_s[...] = jnp.dot(ah_v[...], windows, preferred_element_type=jnp.float32) + jnp.dot(
        al_v[...], windows, preferred_element_type=jnp.float32
    )

    bundle_copies(EARLY).wait_recv()
    mixed = got[EARLY, :, 0].reshape(seq, HD)
    inputs = jnp.concatenate([mixed[i * block : (i + 1) * block] for i in range(blocks)], axis=1)
    in_s[...] = jnp.dot(
        ah_v[:, block:], inputs, preferred_element_type=jnp.float32
    ) + jnp.dot(al_v[:, block:], inputs, preferred_element_type=jnp.float32)

    rows_at_once = 16

    def multiply(step, carry):
        first = pl.multiple_of(step * rows_at_once, rows_at_once)
        real_rows = pl.ds(first, rows_at_once)
        imag_rows = pl.ds(block + first, rows_at_once)
        lanes = [slice(i * HD, (i + 1) * HD) for i in range(blocks)]
        in_real = [in_s[real_rows, s] for s in lanes]
        in_imag = [in_s[imag_rows, s] for s in lanes]
        lag_real = [lag_s[real_rows, s] for s in lanes]
        lag_imag = [lag_s[imag_rows, s] for s in lanes]
        for i in range(blocks):
            real = imag = None
            for j in range(i + 1):
                a, b, c, d = lag_real[i - j], lag_imag[i - j], in_real[j], in_imag[j]
                more_real = a * c - b * d
                more_imag = a * d + b * c
                real = more_real if real is None else real + more_real
                imag = more_imag if imag is None else imag + more_imag
            for rows, total in ((real_rows, real), (imag_rows, imag)):
                high = total.astype(jnp.bfloat16)
                sum_high[rows, lanes[i]] = high
                sum_low[rows, lanes[i]] = (total - high.astype(jnp.float32)).astype(jnp.bfloat16)
        return carry

    lax.fori_loop(0, block // rows_at_once, multiply, 0, unroll=4)
    convolved = (
        jnp.dot(bh_v[...], sum_high[...], preferred_element_type=jnp.float32)
        + jnp.dot(bl_v[...], sum_high[...], preferred_element_type=jnp.float32)
        + jnp.dot(bh_v[...], sum_low[...], preferred_element_type=jnp.float32)
    )

    local[10].wait()
    local[11].wait()
    length = length_s[0]
    weight = skip_v[...]
    row_ids = lax.broadcasted_iota(jnp.int32, (group, HD), 0)
    lane_ids = lax.broadcasted_iota(jnp.int32, (group, HD), 1)
    for g in range(ranks):
        part = convolved[
            g % per_block * group : (g % per_block + 1) * group,
            g // per_block * HD : (g // per_block + 1) * HD,
        ]
        gated = got[EARLY, g, 1].astype(jnp.float32) * (
            part + weight * got[EARLY, g, 0].astype(jnp.float32)
        )
        h_buf[g] = jnp.where(row_ids + g * group < length, gated, 0.0).astype(jnp.bfloat16)

    h_local = pltpu.make_async_copy(h_buf.at[me], h_out.at[:, own], local_sem.at[0])
    h_local.start()
    for step in range(1, ranks):
        peer = lax.rem(me + step, ranks)
        pltpu.make_async_remote_copy(
            src_ref=h_buf.at[peer],
            dst_ref=h_out.at[:, own],
            send_sem=h_send,
            recv_sem=h_recv,
            device_id={"ctx": peer},
            device_id_type=MESH,
        ).start()

    for g in range(ranks):
        h_t[:, g * group : (g + 1) * group] = (
            h_buf[g].astype(jnp.float32).T.astype(jnp.bfloat16)
        )
    bundle_copies(LATE).wait_recv()
    factor = math.log2(math.e) / math.sqrt(HD)

    def attended_copy(g, source):
        return pltpu.make_async_remote_copy(
            src_ref=a_buf.at[g],
            dst_ref=a_out.at[:, columns(source)],
            send_sem=a_send,
            recv_sem=a_recv,
            device_id={"ctx": g},
            device_id_type=MESH,
        )

    def attend_group(g):
        width = (g + 1) * group
        score = lax.dot_general(
            got[LATE, : g + 1, 0].reshape(width, HD),
            got[LATE, g, 1],
            (((1,), (1,)), ((), ())),
            preferred_element_type=jnp.float32,
        )
        last = jnp.where(row_ids <= lane_ids, score[g * group :], -1e30)
        score = last if g == 0 else jnp.concatenate([score[: g * group], last], axis=0)
        row_max = jnp.max(score, axis=0, keepdims=True)
        raw = jnp.exp2((score - row_max) * factor)
        totals = jnp.sum(raw, axis=0, keepdims=True)
        update = jnp.dot(
            h_t[:, :width], raw.astype(jnp.bfloat16), preferred_element_type=jnp.float32
        )
        attended = update / totals
        a_buf[g] = attended.T.astype(jnp.bfloat16)
        sq_mine[g : g + 1] = jnp.sum(attended * attended, axis=0, keepdims=True)

    def attend(step, carry):
        g = lax.rem(me + ranks - step, ranks)

        for index in range(ranks):

            @pl.when(g == index)
            def _():
                attend_group(index)

        @pl.when(step > 0)
        def _():
            attended_copy(g, me).start()

        return carry

    lax.fori_loop(0, ranks, attend, 0)
    for step in range(1, depth):
        other = lax.rem(plane + step, depth)
        copy = pltpu.make_async_remote_copy(
            src_ref=sq_mine,
            dst_ref=sq_in.at[plane],
            send_sem=sq_send.at[step],
            recv_sem=sq_recv.at[plane],
            device_id={"tp": other},
            device_id_type=MESH,
        )
        copy.start()
        sends.append(copy)
    a_local = pltpu.make_async_copy(a_buf.at[me], a_out.at[:, own], local_sem.at[1])
    a_local.start()
    slot_squares = sq_mine[...]
    for step in range(1, depth):
        other = lax.rem(plane + step, depth)
        pltpu.make_async_remote_copy(
            src_ref=sq_in.at[other],
            dst_ref=sq_in.at[other],
            send_sem=sq_send.at[step],
            recv_sem=sq_recv.at[other],
            device_id={"tp": other},
            device_id_type=MESH,
        ).wait_recv()
        slot_squares = slot_squares + sq_in[other]
    for g in range(ranks):
        sq_sum[g] = jnp.broadcast_to(slot_squares[g : g + 1], sq_sum.shape[1:])
    for step in range(1, ranks):
        peer = lax.rem(me + step, ranks)
        pltpu.make_async_remote_copy(
            src_ref=sq_sum.at[peer],
            dst_ref=sq_got.at[me],
            send_sem=total_send,
            recv_sem=total_recv,
            device_id={"ctx": peer},
            device_id_type=MESH,
        ).start()
    totals_copy = all_of(sq_sum.at[others], sq_got.at[others], total_send, total_recv)
    totals_copy.wait_recv()
    total_squares = sq_sum[me]
    for step in range(1, ranks):
        total_squares = total_squares + sq_got[lax.rem(me + step, ranks)]
    inverse_norm = lax.rsqrt(total_squares[:1] * (1.0 / (depth * ranks * HD)) + 1e-06)
    by_row = jnp.broadcast_to(inverse_norm, (group, HD)).T
    norm_out[...] = jnp.where(row_ids + me * group < length, by_row, 0.0)
    most = pl.ds(0, (ranks - 1) * HD)
    a_copies = all_of(a_buf.at[others], a_out.at[:, most], a_send, a_recv)
    a_copies.wait_recv()
    a_local.wait()
    h_local.wait()
    h_copies = all_of(h_buf.at[others], h_out.at[:, most], h_send, h_recv)
    h_copies.wait_recv()
    for copies in (bundle_copies(EARLY), bundle_copies(LATE), h_copies, a_copies, totals_copy):
        copies.wait_send()
    for copy in sends:
        copy.wait_send()


def finish_kernel(h_rows, attended, norm, h_out, a_out):
    h_out[...] = h_rows[...]
    for first in range(0, attended.shape[1], HD):
        lanes = slice(first, first + HD)
        a_out[:, lanes] = (attended[:, lanes].astype(jnp.float32) * norm[...]).astype(jnp.bfloat16)


def head_shards(ranks, depth, *arrays):
    hyena_gate, hyena_key, hyena_value, filter_taps, skip_weight, queries, attn_keys, valid = arrays
    group, channels = hyena_gate.shape
    seq = filter_taps.shape[0]
    block = 2 * group if ranks % 2 == 0 else group
    blocks = seq // block
    bf16, f32 = jnp.bfloat16, jnp.float32
    any_space = pl.BlockSpec(memory_space=pl.ANY)
    vmem = pl.BlockSpec(memory_space=pltpu.VMEM)
    hbm = pl.BlockSpec(memory_space=pltpu.HBM)
    h_rows, attended, norm = pl.pallas_call(
        functools.partial(head_kernel, ranks, depth),
        out_shape=(
            jax.ShapeDtypeStruct((group, channels), bf16),
            jax.ShapeDtypeStruct((group, channels), bf16),
            jax.ShapeDtypeStruct((group, HD), f32),
        ),
        in_specs=[hbm] * 12,
        out_specs=(any_space, any_space, vmem),
        scratch_shapes=[
            pltpu.VMEM((group, channels), bf16),
            pltpu.VMEM((group, channels), bf16),
            pltpu.VMEM((group, channels), bf16),
            pltpu.VMEM((group, channels), bf16),
            pltpu.VMEM((group, channels), bf16),
            pltpu.VMEM((2, ranks, 2, group, HD), bf16),
            pltpu.VMEM((HD, seq), bf16),
            pltpu.VMEM((block + seq, HD), bf16),
            pltpu.VMEM((2 * block, 2 * block), bf16),
            pltpu.VMEM((2 * block, 2 * block), bf16),
            pltpu.VMEM((block, 2 * block), bf16),
            pltpu.VMEM((block, 2 * block), bf16),
            pltpu.VMEM((2, ranks, 2, group, HD), bf16),
            pltpu.VMEM((2 * block, blocks * HD), f32),
            pltpu.VMEM((2 * block, blocks * HD), f32),
            pltpu.VMEM((2 * block, blocks * HD), bf16),
            pltpu.VMEM((2 * block, blocks * HD), bf16),
            pltpu.VMEM((ranks, group, HD), bf16),
            pltpu.VMEM((ranks, group, HD), bf16),
            pltpu.VMEM((1, HD), f32),
            pltpu.SMEM((1,), jnp.int32),
            pltpu.VMEM((ranks, group), f32),
            pltpu.VMEM((depth, ranks, group), f32),
            pltpu.VMEM((ranks, 8, group), f32),
            pltpu.VMEM((ranks, 8, group), f32),
            pltpu.SemaphoreType.DMA((12,)),
            pltpu.SemaphoreType.DMA((2,)),
            pltpu.SemaphoreType.DMA((2,)),
            pltpu.SemaphoreType.DMA,
            pltpu.SemaphoreType.DMA,
            pltpu.SemaphoreType.DMA,
            pltpu.SemaphoreType.DMA,
            pltpu.SemaphoreType.DMA((depth,)),
            pltpu.SemaphoreType.DMA((depth,)),
            pltpu.SemaphoreType.DMA,
            pltpu.SemaphoreType.DMA,
        ],
        compiler_params=pltpu.CompilerParams(
            collective_id=0, has_side_effects=True, vmem_limit_bytes=62 * 1024 * 1024
        ),
    )(
        hyena_key,
        hyena_value,
        hyena_gate,
        filter_taps,
        skip_weight.reshape(1, channels),
        queries,
        attn_keys,
        valid,
        *(jnp.asarray(table) for table in half_shift_tables(block)),
    )
    return pl.pallas_call(
        finish_kernel,
        out_shape=(
            jax.ShapeDtypeStruct((group, channels), bf16),
            jax.ShapeDtypeStruct((group, channels), bf16),
        ),
        in_specs=[vmem] * 3,
        out_specs=(vmem, vmem),
    )(h_rows, attended, norm)


def solution(mesh):
    in_specs = (
        P("ctx", "tp"),
        P("ctx", "tp"),
        P("ctx", "tp"),
        P(None, "tp"),
        P("tp"),
        P("ctx", "tp"),
        P("ctx", "tp"),
        P(),
    )
    out_specs = (P("ctx", "tp"), P("ctx", "tp"))
    ranks, depth = mesh.shape["ctx"], mesh.shape["tp"]
    body = functools.partial(head_shards, ranks, depth) if DW // depth == ranks * HD else shards
    return jax.shard_map(
        body, mesh=mesh, in_specs=in_specs, out_specs=out_specs, check_vma=False
    )
```

```python
import functools
import math

import jax
import jax.numpy as jnp
import numpy as np
from jax import lax
from jax.experimental import pallas as pl
from jax.experimental.pallas import tpu as pltpu
from jax.sharding import PartitionSpec as P

HD = 128
DW = 4096


def tables(group_rows):
    doubled = 2 * group_rows
    freq = jnp.arange(doubled, dtype=jnp.int32)[:, None]
    place = jnp.arange(group_rows, dtype=jnp.int32)[None, :]
    phase = (freq * place % doubled).astype(jnp.float32) * (2.0 * math.pi / doubled)
    parity = (1 - 2 * (jnp.arange(doubled, dtype=jnp.int32) % 2)).astype(jnp.float32)[:, None]
    cosine = jnp.cos(phase)
    sine = jnp.sin(phase)
    cos_high = cosine.astype(jnp.bfloat16)
    cos_low = (cosine - cos_high.astype(jnp.float32)).astype(jnp.bfloat16)
    sin_high = sine.astype(jnp.bfloat16)
    sin_low = (sine - sin_high.astype(jnp.float32)).astype(jnp.bfloat16)
    return ((cos_high, cos_low, sin_high, sin_low, cosine, sine), parity)


def split_dot(high, low, block):
    return jnp.dot(high, block, preferred_element_type=jnp.float32) + jnp.dot(
        low, block, preferred_element_type=jnp.float32
    )


def forward(tabs, block):
    return (split_dot(tabs[0], tabs[1], block), -split_dot(tabs[2], tabs[3], block))


def inverse(tabs, real_part, imag_part):
    cosine, sine = (tabs[4], tabs[5])
    scale = 1.0 / cosine.shape[0]
    first = jnp.dot(
        cosine.T, real_part, precision=lax.Precision.HIGH, preferred_element_type=jnp.float32
    )
    second = jnp.dot(
        sine.T, imag_part, precision=lax.Precision.HIGH, preferred_element_type=jnp.float32
    )
    return (first - second) * scale


def complex_mul(left_real, left_imag, right_real, right_imag):
    return (
        left_real * right_real - left_imag * right_imag,
        left_real * right_imag + left_imag * right_real,
    )


def shards(
    hyena_gate, hyena_key, hyena_value, filter_taps, skip_weight, queries, attn_keys, valid_length
):
    group_rows = hyena_gate.shape[0]
    ranks = lax.axis_size("ctx")
    own_index = lax.axis_index("ctx")
    tabs, parity = tables(group_rows)
    mixed = (hyena_key.astype(jnp.float32) * hyena_value.astype(jnp.float32)).astype(jnp.bfloat16)
    mixed_float = mixed.astype(jnp.float32)
    input_real, input_imag = forward(tabs, mixed)
    own_block = lax.dynamic_slice_in_dim(filter_taps, own_index * group_rows, group_rows, 0)
    taps_real, taps_imag = forward(tabs, own_block)
    band = 2 * group_rows // ranks
    in_real = lax.all_to_all(
        input_real[None].astype(jnp.bfloat16), "ctx", split_axis=1, concat_axis=0, tiled=True
    ).astype(jnp.float32)
    in_imag = lax.all_to_all(
        input_imag[None].astype(jnp.bfloat16), "ctx", split_axis=1, concat_axis=0, tiled=True
    ).astype(jnp.float32)
    filt_real = lax.all_to_all(
        taps_real[None].astype(jnp.bfloat16), "ctx", split_axis=1, concat_axis=0, tiled=True
    ).astype(jnp.float32)
    filt_imag = lax.all_to_all(
        taps_imag[None].astype(jnp.bfloat16), "ctx", split_axis=1, concat_axis=0, tiled=True
    ).astype(jnp.float32)
    band_parity = lax.dynamic_slice_in_dim(parity, own_index * band, band, 0)[None]
    prior_real = jnp.concatenate([jnp.zeros_like(filt_real[:1]), filt_real[:-1]], 0)
    prior_imag = jnp.concatenate([jnp.zeros_like(filt_imag[:1]), filt_imag[:-1]], 0)
    lag_real = filt_real + band_parity * prior_real
    lag_imag = filt_imag + band_parity * prior_imag
    order = jnp.arange(ranks, dtype=jnp.int32)[:, None, None]

    def add_lag(lag, inner):
        later = order >= lag
        moved_real = jnp.where(later, jnp.roll(in_real, lag, 0), 0.0)
        moved_imag = jnp.where(later, jnp.roll(in_imag, lag, 0), 0.0)
        this_real = lax.dynamic_index_in_dim(lag_real, lag, 0, keepdims=True)
        this_imag = lax.dynamic_index_in_dim(lag_imag, lag, 0, keepdims=True)
        out_real, out_imag = complex_mul(this_real, this_imag, moved_real, moved_imag)
        return (inner[0] + out_real, inner[1] + out_imag)

    zeros = jnp.zeros_like(in_real)
    sum_real, sum_imag = lax.fori_loop(0, ranks, add_lag, (zeros, zeros))
    total_real = lax.all_to_all(
        sum_real.astype(jnp.bfloat16), "ctx", split_axis=0, concat_axis=1, tiled=True
    ).astype(sum_real.dtype)
    total_imag = lax.all_to_all(
        sum_imag.astype(jnp.bfloat16), "ctx", split_axis=0, concat_axis=1, tiled=True
    ).astype(sum_imag.dtype)
    convolved = inverse(tabs, total_real[0], total_imag[0])
    positions = own_index * group_rows + jnp.arange(group_rows, dtype=jnp.int32)
    valid_rows = (positions < valid_length[0])[:, None]
    gated = hyena_gate.astype(jnp.float32) * (convolved + skip_weight[None, :] * mixed_float)
    hyena_out = jnp.where(valid_rows, gated, 0.0).astype(jnp.bfloat16)
    heads_here = queries.shape[1] // HD
    scale = 1.0 / math.sqrt(HD)
    query_heads = queries.reshape(group_rows, heads_here, HD)
    start_max = jnp.full((heads_here, group_rows), -1e30, jnp.float32)
    key_piece = lax.all_gather(attn_keys, "ctx", axis=0, tiled=True)
    value_piece = lax.all_gather(hyena_out, "ctx", axis=0, tiled=True)
    width = key_piece.shape[0]
    key_heads = key_piece.reshape(width, heads_here, HD)
    value_heads = value_piece.reshape(width, heads_here, HD)
    scores = (
        jnp.einsum("qhd,khd->hqk", query_heads, key_heads, preferred_element_type=jnp.float32)
        * scale
    )
    key_places = jnp.arange(width, dtype=jnp.int32)
    allowed = (key_places[None, :] <= positions[:, None]) & (key_places < valid_length[0])[None, :]
    scores = jnp.where(allowed[None], scores, -1e30)
    new_max = jnp.maximum(start_max, jnp.max(scores, axis=2))
    weights = jnp.where(allowed[None], jnp.exp(scores - new_max[:, :, None]), 0.0)
    totals = jnp.sum(weights, axis=2)
    update = jnp.einsum(
        "hqk,khd->hqd",
        weights.astype(jnp.bfloat16),
        value_heads,
        preferred_element_type=jnp.float32,
    )
    attended = (update / totals[:, :, None]).transpose(1, 0, 2).reshape(group_rows, heads_here * HD)
    squares = jnp.sum(attended * attended, axis=1)
    total_squares = lax.psum(squares, "tp")
    scaled = attended / jnp.sqrt(total_squares / DW + 1e-06)[:, None]
    attn_out = jnp.where(valid_rows, scaled, 0.0).astype(jnp.bfloat16)
    return (hyena_out, attn_out)


MESH = pl.DeviceIdType.MESH
MIX, GATE, KEY, QUERY = range(4)


def half_shift_tables(block):
    freq = np.arange(block, dtype=np.float64)[:, None] + 0.5
    place = np.arange(2 * block, dtype=np.float64)[None, :] - block
    phase = freq * place * (math.pi / block)
    ahead = np.concatenate([np.cos(phase), -np.sin(phase)], 0)
    back = ahead[:, block:].T / block

    def split(table):
        high = table.astype(jnp.bfloat16)
        low = (table - high.astype(np.float64)).astype(jnp.bfloat16)
        return high, low

    return split(ahead) + split(back)


def head_kernel(
    ranks,
    depth,
    hk,
    hv,
    gate,
    taps,
    skip,
    queries,
    keys,
    valid,
    ahead_high,
    ahead_low,
    back_high,
    back_low,
    h_out,
    a_out,
    norm_out,
    hk_v,
    hv_v,
    gate_v,
    key_v,
    query_v,
    stage,
    h_t,
    taps_v,
    ah_v,
    al_v,
    bh_v,
    bl_v,
    got,
    lag_s,
    in_s,
    sums,
    h_buf,
    a_buf,
    skip_v,
    length_s,
    sq_mine,
    sq_in,
    sq_sum,
    sq_got,
    local_sem,
    in_send,
    in_recv,
    h_send,
    h_recv,
    a_send,
    a_recv,
    sq_send,
    sq_recv,
    total_send,
    total_recv,
):
    me = lax.axis_index("ctx")
    plane = lax.axis_index("tp")
    group = hk_v.shape[0]
    seq = ranks * group
    block = bh_v.shape[0]
    blocks = seq // block
    per_block = block // group

    def columns(index):
        return pl.ds(pl.multiple_of(index * HD, HD), HD)

    own = columns(me)
    local = [
        pltpu.make_async_copy(src, dst, local_sem.at[i])
        for i, (src, dst) in enumerate(
            (
                (hk, hk_v),
                (hv, hv_v),
                (taps.at[:, own], taps_v.at[pl.ds(block, seq)]),
                (ahead_high, ah_v),
                (ahead_low, al_v),
                (back_high, bh_v),
                (back_low, bl_v),
                (gate, gate_v),
                (keys, key_v),
                (queries, query_v),
                (skip.at[:, own], skip_v),
                (valid, length_s),
            )
        )
    ]
    for copy in local:
        copy.start()

    barrier = pltpu.get_barrier_semaphore()
    for step in range(1, ranks):
        pl.semaphore_signal(
            barrier, inc=1, device_id={"ctx": lax.rem(me + step, ranks)}, device_id_type=MESH
        )
    for step in range(1, depth):
        pl.semaphore_signal(
            barrier, inc=1, device_id={"tp": lax.rem(plane + step, depth)}, device_id_type=MESH
        )
    local[0].wait()
    local[1].wait()
    for p in range(ranks):
        lanes = slice(p * HD, (p + 1) * HD)
        stage[MIX, p] = (
            hk_v[:, lanes].astype(jnp.float32) * hv_v[:, lanes].astype(jnp.float32)
        ).astype(jnp.bfloat16)
    pl.semaphore_wait(barrier, ranks - 1 + depth - 1)

    sends = []

    def send(which, src):
        if src is not None:
            local[6 + which].wait()
            for p in range(ranks):
                stage[which, p] = src[:, p * HD : (p + 1) * HD]
        for step in range(1, ranks):
            peer = lax.rem(me + step, ranks)
            copy = pltpu.make_async_remote_copy(
                src_ref=stage.at[which, peer],
                dst_ref=got.at[which, me],
                send_sem=in_send.at[which, step],
                recv_sem=in_recv.at[which, me],
                device_id={"ctx": peer},
                device_id_type=MESH,
            )
            copy.start()
            sends.append(copy)
        got[which, me] = stage[which, me]

    send(MIX, None)

    def arrive(which):
        for step in range(1, ranks):
            peer = lax.rem(me + step, ranks)
            pltpu.make_async_remote_copy(
                src_ref=got.at[which, peer],
                dst_ref=got.at[which, peer],
                send_sem=in_send.at[which, step],
                recv_sem=in_recv.at[which, peer],
                device_id={"ctx": peer},
                device_id_type=MESH,
            ).wait_recv()

    taps_v[:block] = jnp.zeros((block, HD), jnp.bfloat16)
    for copy in local[2:7]:
        copy.wait()
    windows = jnp.concatenate(
        [taps_v[i * block : (i + 2) * block] for i in range(blocks)], axis=1
    )
    lag_s[...] = jnp.dot(ah_v[...], windows, preferred_element_type=jnp.float32) + jnp.dot(
        al_v[...], windows, preferred_element_type=jnp.float32
    )

    send(GATE, gate_v)
    arrive(MIX)
    send(KEY, key_v)
    send(QUERY, query_v)
    mixed = got[MIX].reshape(seq, HD)
    inputs = jnp.concatenate([mixed[i * block : (i + 1) * block] for i in range(blocks)], axis=1)
    in_s[...] = jnp.dot(
        ah_v[:, block:], inputs, preferred_element_type=jnp.float32
    ) + jnp.dot(al_v[:, block:], inputs, preferred_element_type=jnp.float32)

    rows_at_once = 16

    def multiply(step, carry):
        first = pl.multiple_of(step * rows_at_once, rows_at_once)
        real_rows = pl.ds(first, rows_at_once)
        imag_rows = pl.ds(block + first, rows_at_once)
        lanes = [slice(i * HD, (i + 1) * HD) for i in range(blocks)]
        in_real = [in_s[real_rows, s] for s in lanes]
        in_imag = [in_s[imag_rows, s] for s in lanes]
        lag_real = [lag_s[real_rows, s] for s in lanes]
        lag_imag = [lag_s[imag_rows, s] for s in lanes]
        for i in range(blocks):
            real = imag = None
            for j in range(i + 1):
                a, b, c, d = lag_real[i - j], lag_imag[i - j], in_real[j], in_imag[j]
                more_real = a * c - b * d
                more_imag = a * d + b * c
                real = more_real if real is None else real + more_real
                imag = more_imag if imag is None else imag + more_imag
            for rows, total in ((real_rows, real), (imag_rows, imag)):
                sums[rows, lanes[i]] = total.astype(jnp.bfloat16)
        return carry

    lax.fori_loop(0, block // rows_at_once, multiply, 0, unroll=4)
    convolved = jnp.dot(bh_v[...], sums[...], preferred_element_type=jnp.float32) + jnp.dot(
        bl_v[...], sums[...], preferred_element_type=jnp.float32
    )

    local[10].wait()
    local[11].wait()
    length = length_s[0]
    weight = skip_v[...]
    arrive(GATE)
    row_ids = lax.broadcasted_iota(jnp.int32, (group, HD), 0)
    lane_ids = lax.broadcasted_iota(jnp.int32, (group, HD), 1)
    for g in range(ranks):
        part = convolved[
            g % per_block * group : (g % per_block + 1) * group,
            g // per_block * HD : (g // per_block + 1) * HD,
        ]
        gated = got[GATE, g].astype(jnp.float32) * (
            part + weight * got[MIX, g].astype(jnp.float32)
        )
        h_buf[g] = jnp.where(row_ids + g * group < length, gated, 0.0).astype(jnp.bfloat16)

    h_local = pltpu.make_async_copy(h_buf.at[me], h_out.at[:, own], local_sem.at[0])
    h_local.start()
    for step in range(1, ranks):
        peer = lax.rem(me + step, ranks)
        copy = pltpu.make_async_remote_copy(
            src_ref=h_buf.at[peer],
            dst_ref=h_out.at[:, own],
            send_sem=h_send.at[step],
            recv_sem=h_recv.at[me],
            device_id={"ctx": peer},
            device_id_type=MESH,
        )
        copy.start()
        sends.append(copy)

    for g in range(ranks):
        h_t[:, g * group : (g + 1) * group] = (
            h_buf[g].astype(jnp.float32).T.astype(jnp.bfloat16)
        )
    arrive(KEY)
    factor = math.log2(math.e) / math.sqrt(HD)

    def attended_copy(g, source):
        return pltpu.make_async_remote_copy(
            src_ref=a_buf.at[g],
            dst_ref=a_out.at[:, columns(source)],
            send_sem=a_send.at[g],
            recv_sem=a_recv.at[source],
            device_id={"ctx": g},
            device_id_type=MESH,
        )

    def attend_group(g):
        width = (g + 1) * group
        score = lax.dot_general(
            got[KEY, : g + 1].reshape(width, HD),
            got[QUERY, g],
            (((1,), (1,)), ((), ())),
            preferred_element_type=jnp.float32,
        )
        last = jnp.where(row_ids <= lane_ids, score[g * group :], -1e30)
        score = last if g == 0 else jnp.concatenate([score[: g * group], last], axis=0)
        row_max = jnp.max(score, axis=0, keepdims=True)
        raw = jnp.exp2((score - row_max) * factor)
        totals = jnp.sum(raw, axis=0, keepdims=True)
        update = jnp.dot(
            h_t[:, :width], raw.astype(jnp.bfloat16), preferred_element_type=jnp.float32
        )
        attended = update / totals
        a_buf[g] = attended.T.astype(jnp.bfloat16)
        sq_mine[g : g + 1] = jnp.sum(attended * attended, axis=0, keepdims=True)

    def attend(step, carry):
        g = lax.rem(me + ranks - step, ranks)

        @pl.when(step > 0)
        def _():
            pltpu.make_async_remote_copy(
                src_ref=got.at[QUERY, g],
                dst_ref=got.at[QUERY, g],
                send_sem=in_send.at[QUERY, g],
                recv_sem=in_recv.at[QUERY, g],
                device_id={"ctx": g},
                device_id_type=MESH,
            ).wait_recv()

        for index in range(ranks):

            @pl.when(g == index)
            def _():
                attend_group(index)

        @pl.when(step > 0)
        def _():
            attended_copy(g, me).start()

        return carry

    lax.fori_loop(0, ranks, attend, 0)
    for step in range(1, depth):
        other = lax.rem(plane + step, depth)
        copy = pltpu.make_async_remote_copy(
            src_ref=sq_mine,
            dst_ref=sq_in.at[plane],
            send_sem=sq_send.at[step],
            recv_sem=sq_recv.at[plane],
            device_id={"tp": other},
            device_id_type=MESH,
        )
        copy.start()
        sends.append(copy)
    a_local = pltpu.make_async_copy(a_buf.at[me], a_out.at[:, own], local_sem.at[1])
    a_local.start()
    slot_squares = sq_mine[...]
    for step in range(1, depth):
        other = lax.rem(plane + step, depth)
        pltpu.make_async_remote_copy(
            src_ref=sq_in.at[other],
            dst_ref=sq_in.at[other],
            send_sem=sq_send.at[step],
            recv_sem=sq_recv.at[other],
            device_id={"tp": other},
            device_id_type=MESH,
        ).wait_recv()
        slot_squares = slot_squares + sq_in[other]
    for g in range(ranks):
        sq_sum[g] = jnp.broadcast_to(slot_squares[g : g + 1], sq_sum.shape[1:])
    for step in range(1, ranks):
        peer = lax.rem(me + step, ranks)
        copy = pltpu.make_async_remote_copy(
            src_ref=sq_sum.at[peer],
            dst_ref=sq_got.at[me],
            send_sem=total_send.at[step],
            recv_sem=total_recv.at[me],
            device_id={"ctx": peer},
            device_id_type=MESH,
        )
        copy.start()
        sends.append(copy)
    total_squares = sq_sum[me]
    for step in range(1, ranks):
        peer = lax.rem(me + step, ranks)
        pltpu.make_async_remote_copy(
            src_ref=sq_sum.at[peer],
            dst_ref=sq_got.at[peer],
            send_sem=total_send.at[step],
            recv_sem=total_recv.at[peer],
            device_id={"ctx": peer},
            device_id_type=MESH,
        ).wait_recv()
        total_squares = total_squares + sq_got[peer]
    inverse_norm = lax.rsqrt(total_squares[:1] * (1.0 / (depth * ranks * HD)) + 1e-06)
    by_row = jnp.broadcast_to(inverse_norm, (group, HD)).T
    norm_out[...] = jnp.where(row_ids + me * group < length, by_row, 0.0)
    for step in range(1, ranks):
        peer = lax.rem(me + step, ranks)
        attended_copy(peer, peer).wait_recv()
    a_local.wait()
    h_local.wait()
    for step in range(1, ranks):
        peer = lax.rem(me + step, ranks)
        pltpu.make_async_remote_copy(
            src_ref=h_buf.at[peer],
            dst_ref=h_out.at[:, columns(peer)],
            send_sem=h_send.at[step],
            recv_sem=h_recv.at[peer],
            device_id={"ctx": peer},
            device_id_type=MESH,
        ).wait_recv()
        attended_copy(peer, me).wait_send()
    for copy in sends:
        copy.wait_send()


def finish_kernel(h_rows, attended, norm, h_out, a_out):
    h_out[...] = h_rows[...]
    for first in range(0, attended.shape[1], HD):
        lanes = slice(first, first + HD)
        a_out[:, lanes] = (attended[:, lanes].astype(jnp.float32) * norm[...]).astype(jnp.bfloat16)


def head_shards(ranks, depth, *arrays):
    hyena_gate, hyena_key, hyena_value, filter_taps, skip_weight, queries, attn_keys, valid = arrays
    group, channels = hyena_gate.shape
    seq = filter_taps.shape[0]
    block = 2 * group if ranks % 2 == 0 else group
    blocks = seq // block
    bf16, f32 = jnp.bfloat16, jnp.float32
    any_space = pl.BlockSpec(memory_space=pl.ANY)
    vmem = pl.BlockSpec(memory_space=pltpu.VMEM)
    hbm = pl.BlockSpec(memory_space=pltpu.HBM)
    h_rows, attended, norm = pl.pallas_call(
        functools.partial(head_kernel, ranks, depth),
        out_shape=(
            jax.ShapeDtypeStruct((group, channels), bf16),
            jax.ShapeDtypeStruct((group, channels), bf16),
            jax.ShapeDtypeStruct((group, HD), f32),
        ),
        in_specs=[hbm] * 12,
        out_specs=(any_space, any_space, vmem),
        scratch_shapes=[
            pltpu.VMEM((group, channels), bf16),
            pltpu.VMEM((group, channels), bf16),
            pltpu.VMEM((group, channels), bf16),
            pltpu.VMEM((group, channels), bf16),
            pltpu.VMEM((group, channels), bf16),
            pltpu.VMEM((4, ranks, group, HD), bf16),
            pltpu.VMEM((HD, seq), bf16),
            pltpu.VMEM((block + seq, HD), bf16),
            pltpu.VMEM((2 * block, 2 * block), bf16),
            pltpu.VMEM((2 * block, 2 * block), bf16),
            pltpu.VMEM((block, 2 * block), bf16),
            pltpu.VMEM((block, 2 * block), bf16),
            pltpu.VMEM((4, ranks, group, HD), bf16),
            pltpu.VMEM((2 * block, blocks * HD), f32),
            pltpu.VMEM((2 * block, blocks * HD), f32),
            pltpu.VMEM((2 * block, blocks * HD), bf16),
            pltpu.VMEM((ranks, group, HD), bf16),
            pltpu.VMEM((ranks, group, HD), bf16),
            pltpu.VMEM((1, HD), f32),
            pltpu.SMEM((1,), jnp.int32),
            pltpu.VMEM((ranks, group), f32),
            pltpu.VMEM((depth, ranks, group), f32),
            pltpu.VMEM((ranks, 8, group), f32),
            pltpu.VMEM((ranks, 8, group), f32),
            pltpu.SemaphoreType.DMA((12,)),
            pltpu.SemaphoreType.DMA((4, ranks)),
            pltpu.SemaphoreType.DMA((4, ranks)),
            pltpu.SemaphoreType.DMA((ranks,)),
            pltpu.SemaphoreType.DMA((ranks,)),
            pltpu.SemaphoreType.DMA((ranks,)),
            pltpu.SemaphoreType.DMA((ranks,)),
            pltpu.SemaphoreType.DMA((depth,)),
            pltpu.SemaphoreType.DMA((depth,)),
            pltpu.SemaphoreType.DMA((ranks,)),
            pltpu.SemaphoreType.DMA((ranks,)),
        ],
        compiler_params=pltpu.CompilerParams(
            collective_id=0, has_side_effects=True, vmem_limit_bytes=62 * 1024 * 1024
        ),
    )(
        hyena_key,
        hyena_value,
        hyena_gate,
        filter_taps,
        skip_weight.reshape(1, channels),
        queries,
        attn_keys,
        valid,
        *(jnp.asarray(table) for table in half_shift_tables(block)),
    )
    return pl.pallas_call(
        finish_kernel,
        out_shape=(
            jax.ShapeDtypeStruct((group, channels), bf16),
            jax.ShapeDtypeStruct((group, channels), bf16),
        ),
        in_specs=[vmem] * 3,
        out_specs=(vmem, vmem),
    )(h_rows, attended, norm)


def solution(mesh):
    in_specs = (
        P("ctx", "tp"),
        P("ctx", "tp"),
        P("ctx", "tp"),
        P(None, "tp"),
        P("tp"),
        P("ctx", "tp"),
        P("ctx", "tp"),
        P(),
    )
    out_specs = (P("ctx", "tp"), P("ctx", "tp"))
    ranks, depth = mesh.shape["ctx"], mesh.shape["tp"]
    body = functools.partial(head_shards, ranks, depth) if DW // depth == ranks * HD else shards
    return jax.shard_map(
        body, mesh=mesh, in_specs=in_specs, out_specs=out_specs, check_vma=False
    )
```
